32 devices in a mesh: clip: 8 (over z, x), tensor: 4 (over y, core).
Axes of the slice: x: 2, y: 2, z: 4, core: 2. Of those that a mesh axis runs over, the one named last changes fastest.
Arguments:
- tokens_in: float32 [2, 8, 2048, 384], P(None, 'clip'), may hold values from -6 to 6
- gain_one: float32 [384], replicated, may hold values from 0.1 to 1.9
- heads_in_one: bfloat16 [384, 3, 384], P(None, None, 'tensor'), may hold values from -0.3125 to 0.3125
- heads_out_one: bfloat16 [384, 384], P('tensor'), may hold values from -6 to 6
- gain_two: float32 [384], replicated, may hold values from 0.1 to 1.9
- hidden_in_one: bfloat16 [384, 1536], P(None, 'tensor'), may hold values from -0.3125 to 0.3125
- hidden_out_one: bfloat16 [1536, 384], P('tensor'), may hold values from -0.15625 to 0.15625
- gain_three: float32 [384], replicated, may hold values from 0.1 to 1.9
- heads_in_two: bfloat16 [384, 3, 768], P(None, None, 'tensor'), may hold values from -0.3125 to 0.3125
- skip_weight: bfloat16 [384, 768], P('tensor'), may hold values from -0.625 to 0.625
- heads_out_two: bfloat16 [768, 768], P('tensor'), may hold values from -4 to 4
- gain_four: float32 [768], replicated, may hold values from 0.1 to 1.9
- hidden_in_two: bfloat16 [768, 3072], P(None, 'tensor'), may hold values from -0.21875 to 0.21875
- hidden_out_two: bfloat16 [3072, 768], P('tensor'), may hold values from -0.109375 to 0.109375
- resolution: int32 [2, 8], replicated, may hold values from 0 to 1
- continues: int32 [2, 8], replicated, may hold values from 0 to 1, as said below
- cotangent: float32 [2, 8, 512, 768], P(None, 'clip'), may hold values from -6 to 6
Outputs:
- output: float32 [2, 8, 512, 768], P(None, 'clip')
- grad_input: float32 [2, 8, 2048, 384], P(None, 'clip', 'tensor')
- grad_gain_one: float32 [384], replicated
- grad_heads_in_one: float32 [384, 3, 384], P(None, None, 'tensor')
- grad_heads_out_one: float32 [384, 384], P('tensor')
- grad_gain_two: float32 [384], replicated
- grad_hidden_in_one: float32 [384, 1536], P(None, 'tensor')
- grad_hidden_out_one: float32 [1536, 384], P('tensor')
- grad_gain_three: float32 [384], replicated
- grad_heads_in_two: float32 [384, 3, 768], P(None, None, 'tensor')
- grad_skip_weight: float32 [384, 768], P('tensor')
- grad_heads_out_two: float32 [768, 768], P('tensor')
- grad_gain_four: float32 [768], replicated
- grad_hidden_in_two: float32 [768, 3072], P(None, 'tensor')
- grad_hidden_out_two: float32 [3072, 768], P('tensor')
The draws below stay inside these ranges and needn't reach their ends.
Inputs may be any that keep to these rules, and one draw needn't show every extreme that they name: `resolution`: 1 marks a clip whose first 2048 token slots are valid, 0 one whose first 1052 are; the rest are padding. 1 where a clip continues the video of the clip before it in its micro-batch; in one micro-batch, drawn from the seed, every clip does; the entry of the first clip is not read.
All inputs are finite; a program needn't handle non-finite values.
Results may differ from the reference program's by a relative error of at most 0.025.
Values may be sent and summed in bfloat16 or wider, within the bound.
No kernel may reach another device: no remote copies, remote signals or barrier semaphores. Data moves between devices by JAX's collectives and lax.ppermute only.
A program may use at most 320 MiB of HBM per device.

```python
from functools import partial
import jax
import jax.numpy as jnp
from jax import lax

D1 = 384
HD = 96
F1 = 1536
D2 = 768
F2 = 3072
TOK = 2048
MICRO = 2
TOK_LOW = 1052
CLIPS = 8


def draw_continues(key, part):
    key = jax.random.fold_in(key, 7)
    first_key, second_key = jax.random.split(key)
    picks = jax.random.randint(first_key, (MICRO, CLIPS), 0, 4)
    flags = (picks > 0).astype(jnp.int32)
    chosen = jax.random.randint(second_key, (), 0, MICRO)
    whole_row = jnp.arange(MICRO)[:, None] == chosen
    return jnp.where(whole_row, 1, flags).astype(jnp.int32)


def set_ends(values, own_key, smallest, largest):
    longest = values.shape.index(max(values.shape))
    spots = []
    for shift in (0, 1):
        where = [jax.random.randint(jax.random.fold_in(own_key, axis), (), 0, length) for axis, length in enumerate(values.shape)]
        where[longest] = (where[longest] + shift) % values.shape[longest]
        spots.append(tuple(where))
    return values.at[spots[0]].set(smallest).at[spots[1]].set(largest)


def block_scale(key, shape, shards, smallest, top_value):
    def one(position, parts):
        draws = jax.random.uniform(jax.random.fold_in(jax.random.fold_in(key, 6), position), (parts,), jnp.float32, smallest / len(shards), top_value / len(shards))
        return jnp.repeat(jnp.exp(draws), shape[position] // parts).reshape((-1,) + (1,) * (len(shape) - position - 1))

    factor_of = one(*shards[0])
    for cut in shards[1:]:
        factor_of = factor_of * one(*cut)
    return factor_of


def centred(own_key, dims, spread, reach, cuts=(), held_as=jnp.bfloat16):
    values = jax.random.normal(own_key, dims, jnp.float32) * spread
    if len(cuts) > 0:
        values = block_scale(own_key, dims, cuts, -0.22, 0.18) * values
    return jnp.clip(values, min=-reach, max=reach).astype(held_as)


def setup_inputs(seed: int = 0) -> dict:
    key_list = jax.random.split(jax.random.key(seed), 18)
    tokens_in = centred(key_list[0], (MICRO, CLIPS, TOK, D1), 1.0, 6.0, ((1, 8),), jnp.float32)
    gain_one = jnp.clip(1.0 + 0.18 * jax.random.normal(key_list[1], (D1,), jnp.float32), 0.1, 1.9)
    heads_in_one = centred(key_list[2], (D1, 3, D1), D1 ** -0.5, 0.3125, ((2, 4),))
    heads_out_one = centred(key_list[3], (D1, D1), 1 ** -0.5, 6.0, ((0, 4),))
    gain_two = jnp.clip(1.0 + 0.18 * jax.random.normal(key_list[4], (D1,), jnp.float32), 0.1, 1.9)
    hidden_in_one = centred(key_list[5], (D1, F1), D1 ** -0.5, 0.3125, ((1, 4),))
    hidden_out_one = centred(key_list[6], (F1, D1), F1 ** -0.5, 0.15625, ((0, 4),))
    gain_three = jnp.clip(1.0 + 0.18 * jax.random.normal(key_list[7], (D1,), jnp.float32), 0.1, 1.9)
    heads_in_two = centred(key_list[8], (D1, 3, D2), D1 ** -0.5, 0.3125, ((2, 4),))
    skip_weight = centred(key_list[9], (D1, D2), (D1 // 4) ** -0.5, 0.625, ((0, 4),))
    heads_out_two = centred(key_list[10], (D2, D2), 2 ** -0.5, 4.0, ((0, 4),))
    gain_four = jnp.clip(1.0 + 0.18 * jax.random.normal(key_list[11], (D2,), jnp.float32), 0.1, 1.9)
    hidden_in_two = centred(key_list[12], (D2, F2), D2 ** -0.5, 0.21875, ((1, 4),))
    hidden_out_two = centred(key_list[13], (F2, D2), F2 ** -0.5, 0.109375, ((0, 4),))
    resolution = set_ends(jax.random.randint(key_list[14], (MICRO, CLIPS), 0, 2), jax.random.fold_in(key_list[14], 1), 0, 1).astype(jnp.int32)
    continues = draw_continues(jax.random.fold_in(key_list[17], 71), 0)
    cotangent = centred(key_list[16], (MICRO, CLIPS, TOK // 4, D2), 1.0, 6.0, ((1, 8),), jnp.float32)
    return dict(tokens_in=tokens_in, gain_one=gain_one, heads_in_one=heads_in_one, heads_out_one=heads_out_one, gain_two=gain_two, hidden_in_one=hidden_in_one, hidden_out_one=hidden_out_one, gain_three=gain_three, heads_in_two=heads_in_two, skip_weight=skip_weight, heads_out_two=heads_out_two, gain_four=gain_four, hidden_in_two=hidden_in_two, hidden_out_two=hidden_out_two, resolution=resolution, continues=continues, cotangent=cotangent)


EPSILON = 1e-06
MASKED_SCORE = -1e+30
HIGHEST_PRECISION = lax.Precision.HIGHEST

@jax.custom_vjp
def low(v):
    return lax.optimization_barrier(v.astype(jnp.bfloat16)).astype(jnp.float32)

@jax.custom_vjp
def low_back(v):
    return v

def low_keep(v):
    return (low(v), None)

def low_pass(kept, grad):
    return (grad,)

def back_keep(v):
    return (v, None)

def back_low(kept, grad):
    return (low(grad),)
low.defvjp(low_keep, low_pass)
low_back.defvjp(back_keep, back_low)

def rms_norm(values, norm_gain):
    return values * lax.rsqrt(lax.optimization_barrier(jnp.mean(values * values, -1, keepdims=True)) + EPSILON) * norm_gain

def gelu_tanh(values):
    return jax.nn.gelu(values, approximate=True)

def pool_rows(values):
    extent = values.shape
    return lax.optimization_barrier(jnp.mean(values.reshape(extent[:2] + (extent[2] // 4, 4) + extent[3:]), axis=3))

def with_memory(paired):
    memory = low_back(low(pool_rows(paired)))
    shifted = jnp.concatenate([jnp.zeros_like(memory[:, :1]), memory[:, :-1]], 1)
    return jnp.concatenate([paired, shifted], 2)

def one_clip(inputs):
    queries, paired, usable = inputs
    scaling = queries.shape[-1] ** (-0.5)
    scores = jnp.einsum('qhe,khe->hqk', queries, paired[:, 0], precision=HIGHEST_PRECISION) * scaling
    scores = jnp.where(usable[None, None, :], low_back(scores), MASKED_SCORE)
    weights = low(jax.nn.softmax(scores, axis=-1))
    return jnp.einsum('hqk,khe->qhe', weights, paired[:, 1], precision=HIGHEST_PRECISION)

def attention(queries, paired, usable):
    extent = queries.shape
    heads = extent[-1] // HD
    flat_query = queries.reshape((-1, extent[2], heads, HD))
    flat_pair = paired.reshape((-1, paired.shape[2], 2, heads, HD))
    flat_usable = usable.reshape((-1, usable.shape[-1]))
    result = lax.map(jax.checkpoint(one_clip), (flat_query, flat_pair, flat_usable))
    return result.reshape(extent)

def product(left, right, form):
    return jnp.einsum(form, left, right, precision=HIGHEST_PRECISION)

def layer_pair(usable, residual, gain_one, heads_in_one, heads_out_one, gain_two, hidden_in_one, hidden_out_one, gain_three, heads_in_two, skip_weight, heads_out_two, gain_four, hidden_in_two, hidden_out_two):
    normed = low(rms_norm(residual, gain_one))
    mixed = product(normed, heads_in_one, 'mctd,dje->mctje')
    queries = low_back(low(mixed[:, :, :, 0]))
    paired = with_memory(low_back(low(mixed[:, :, :, 1:])))
    heads = low_back(low(attention(queries, paired, usable)))
    residual = residual + low_back(product(heads, heads_out_one, 'mcte,ed->mctd'))
    normed = low(rms_norm(residual, gain_two))
    hidden = low(gelu_tanh(low_back(product(normed, hidden_in_one, 'mctd,df->mctf'))))
    residual = residual + low_back(product(hidden, hidden_out_one, 'mctf,fd->mctd'))
    normed = low(rms_norm(residual, gain_three))
    mixed = product(normed, heads_in_two, 'mctd,dje->mctje')
    queries = low_back(low(pool_rows(mixed[:, :, :, 0])))
    paired = with_memory(low_back(low(mixed[:, :, :, 1:])))
    heads = low_back(low(attention(queries, paired, usable)))
    pooled = low(pool_rows(normed))
    residual = low_back(product(pooled, skip_weight, 'mctd,de->mcte') + product(heads, heads_out_two, 'mcte,ed->mctd'))
    normed = low(rms_norm(residual, gain_four))
    hidden = low(gelu_tanh(low_back(product(normed, hidden_in_two, 'mctd,df->mctf'))))
    return residual + low_back(product(hidden, hidden_out_two, 'mctf,fd->mctd'))

def reference(tokens_in, gain_one, heads_in_one, heads_out_one, gain_two, hidden_in_one, hidden_out_one, gain_three, heads_in_two, skip_weight, heads_out_two, gain_four, hidden_in_two, hidden_out_two, resolution, continues, cotangent):
    own_len = jnp.where(resolution == 1, TOK, TOK_LOW).astype(jnp.int32)
    prev_len = jnp.concatenate([jnp.zeros((MICRO, 1), jnp.int32), own_len[:, :-1]], 1)
    memory_ok = (continues == 1) & (jnp.arange(CLIPS)[None, :] > 0)
    places = jnp.arange(TOK)
    own_valid = places[None, None, :] < own_len[..., None]
    memory_valid = ((places[:TOK // 4] * 4)[None, None, :] < prev_len[..., None]) & memory_ok[..., None]
    usable = jnp.concatenate([own_valid, memory_valid], 2)
    weights = (tokens_in, gain_one, heads_in_one, heads_out_one, gain_two, hidden_in_one, hidden_out_one, gain_three, heads_in_two, skip_weight, heads_out_two, gain_four, hidden_in_two, hidden_out_two)
    weights = tuple((item.astype(jnp.float32) for item in weights))
    output, pullback = jax.vjp(partial(layer_pair, usable), *weights)
    grads = pullback(cotangent.astype(jnp.float32))
    return (output, grads[0], grads[1], grads[2], grads[3], grads[4], grads[5], grads[6], grads[7], grads[8], grads[9], grads[10], grads[11], grads[12], grads[13])
```

```python
import functools

import jax
import jax.numpy as jnp
from jax import lax
from jax.experimental import pallas as pl
from jax.experimental.pallas import tpu as pltpu
from jax.sharding import PartitionSpec as P

HD = 96
PAD = 128
TOK_LOW = 1052
EPSILON = 1e-06
MASKED_SCORE = -1e30
LOG2E = 1.4426950408889634
LN2 = 0.6931471805599453
SCALING = HD ** (-0.5)
BF = jnp.bfloat16
F32 = jnp.float32
MIB = 2**20

NN = (((1,), (0,)), ((), ()))
NT = (((1,), (1,)), ((), ()))
TN = (((0,), (0,)), ((), ()))


def dot(left, right, form=NN):
    return lax.dot_general(left, right, form, preferred_element_type=F32)


def rms_factor(values):
    return lax.rsqrt(jnp.mean(values * values, -1, keepdims=True) + EPSILON)


def norm_grads(values, gain, grad):
    factor = rms_factor(values)
    scaled = values * factor
    term = grad * gain
    inner = jnp.mean(scaled * term, -1, keepdims=True)
    return factor * (term - scaled * inner), grad * scaled


def gelu_parts(values):
    root = 0.7978845608028654
    square = values * values
    tanh = jnp.tanh(values * (root + (root * 0.044715) * square))
    half = 0.5 + 0.5 * tanh
    slope = half + (0.5 * values) * (1.0 - tanh * tanh) * (root + (3 * root * 0.044715) * square)
    return values * half, slope


def gelu_only(values):
    root = 0.7978845608028654
    tanh = jnp.tanh(values * (root + (root * 0.044715) * (values * values)))
    return values * (0.5 + 0.5 * tanh)


def split_three(row):
    high = row.astype(BF).astype(F32)
    rest = row - high
    middle = rest.astype(BF).astype(F32)
    return high, middle, rest - middle


def call(body, name, grid, in_specs, out_specs, out_shape, scratch=(), prefetch=0, flops=0, vmem=44):
    return pl.pallas_call(
        body,
        name=name,
        grid_spec=pltpu.PrefetchScalarGridSpec(
            num_scalar_prefetch=prefetch,
            grid=grid,
            in_specs=in_specs,
            out_specs=out_specs,
            scratch_shapes=list(scratch),
        ),
        out_shape=out_shape,
        compiler_params=pltpu.CompilerParams(vmem_limit_bytes=vmem * MIB),
        cost_estimate=pl.CostEstimate(flops=flops, bytes_accessed=4 * MIB, transcendentals=0),
    )


def whole(shape):
    return pl.BlockSpec(shape, lambda *_: (0,) * len(shape))


def shape_of(shape, dtype):
    return jax.ShapeDtypeStruct(shape, dtype)


def lane_scratch(rows, width):
    return pltpu.VMEM((width // PAD, rows, PAD), F32)


def slabs_of(block, lanes):
    parts = lanes.shape[0]
    rows = block.shape[0] // 4
    for part in range(parts):
        lanes[part] = block[:, part * PAD : (part + 1) * PAD]
    return [
        jnp.concatenate([lanes[part, pl.ds(s, rows, stride=4), :] for part in range(parts)], 1)
        for s in range(4)
    ]


def entry_body(_, x_ref, gain_ref, normed_ref, pooled_ref, lanes):
    total = None
    slabs = slabs_of(x_ref[0, 0], lanes)
    for slab in range(4):
        values = slabs[slab]
        normed = (values * rms_factor(values) * gain_ref[...]).astype(BF)
        normed_ref[slab] = normed
        part = normed.astype(F32)
        total = part if total is None else total + part
    pooled_ref[...] = (total * 0.25).astype(BF)


def entry_norm(micro, tokens, gain):
    length, width = tokens.shape[2:]
    rows = length // 4
    block = rows // 4
    return call(
        entry_body,
        "entry_norm",
        (4,),
        [
            pl.BlockSpec((1, 1, 4 * block, width), lambda i, m: (m[0], 0, i, 0)),
            whole((1, width)),
        ],
        [
            pl.BlockSpec((4, block, width), lambda i, m: (0, i, 0)),
            pl.BlockSpec((block, width), lambda i, m: (i, 0)),
        ],
        [shape_of((4, rows, width), BF), shape_of((rows, width), BF)],
        scratch=[lane_scratch(4 * block, width)],
        prefetch=1,
        flops=length * width * 8,
    )(micro, tokens, gain.reshape(1, -1))


def make_pairs(limits, head, normed, memory, weights, keys_ref, values_ref, keys_t_ref, values_t):
    rows = memory.shape[0]
    place = lax.broadcasted_iota(jnp.int32, (rows, 1), 0) * 4
    lane = lax.broadcasted_iota(jnp.int32, (rows, PAD), 1)
    for chunk in range(5):
        source = normed[chunk] if chunk < 4 else memory[...]
        if chunk < 4:
            usable = place + chunk < limits[0]
        else:
            usable = place < limits[1]
        bias = jnp.where(usable, 0.0, MASKED_SCORE)
        both = dot(source, weights[PAD:], NT)
        keys = jnp.where(lane < HD, both[:, :PAD], jnp.where(lane == HD, bias, 1.0))
        keys_ref[head, chunk] = keys.astype(BF)
        values_ref[head, chunk] = jnp.where(lane < HD, both[:, PAD:], 1.0).astype(BF)
        turned = dot(weights[PAD:], source, NT)
        keys_t_ref[head, chunk] = turned[:HD].astype(BF)
        tail = jnp.ones((PAD - HD, rows), F32)
        values_t[chunk] = jnp.concatenate([turned[PAD : PAD + HD], tail], 0).astype(BF)


def query_tail(rows, parts):
    index = lax.broadcasted_iota(jnp.int32, (PAD - HD, rows), 0)
    tail = jnp.where(index == 0, 1.0, 0.0)
    for step, part in enumerate(parts):
        tail = jnp.where(index == step + 1, -part, tail)
    return tail.astype(BF)


def attend_rows(source, weights, keys, values_t):
    rows = source.shape[0]
    query = (dot(weights[:HD], source, NT) * (SCALING * LOG2E)).astype(BF)
    asked = jnp.concatenate([query, query_tail(rows, ())], 0)
    half = rows // 256
    scores = []
    for chunk in range(5):
        for part in range(half):
            scores.append(dot(keys[chunk, part * 256 : (part + 1) * 256], asked))
    top = functools.reduce(jnp.maximum, [jnp.max(item, 0, keepdims=True) for item in scores])
    result = None
    for chunk in range(5):
        for part in range(half):
            raised = jnp.exp2(scores[chunk * half + part] - top).astype(BF)
            term = dot(values_t[chunk, :, part * 256 : (part + 1) * 256], raised)
            result = term if result is None else result + term
    summed = result[HD : HD + 1]
    heads = (result[:HD] / summed).astype(BF)
    logsum = top + jnp.log2(summed)
    return heads, jnp.concatenate([query, query_tail(rows, split_three(logsum))], 0)


def attend_one_body(
    limits, normed, memory, weights, out_weights,
    keys, values, keys_t, queries_t, heads_t, partial, values_t,
):
    slab = pl.program_id(0)

    @pl.when(slab == 0)
    def _():
        for head in range(2):
            make_pairs(
                limits, head, normed, memory, weights[head], keys, values, keys_t, values_t.at[head]
            )

    source = normed[slab]
    total = None
    for head in range(2):
        heads, asked = attend_rows(source, weights[head], keys.at[head], values_t.at[head])
        heads_t[head] = heads
        queries_t[head] = asked
        term = dot(heads, out_weights[head], TN)
        total = term if total is None else total + term
    partial[0] = total.astype(BF)


def attend_one(limits, normed, memory, weights, out_weights):
    _, rows, width = normed.shape
    heads = weights.shape[0]
    return call(
        attend_one_body,
        "attend_one",
        (4,),
        [
            whole((4, rows, width)),
            whole((rows, width)),
            whole(weights.shape),
            whole(out_weights.shape),
        ],
        [
            whole((heads, 5, rows, PAD)),
            whole((heads, 5, rows, PAD)),
            whole((heads, 5, HD, rows)),
            pl.BlockSpec((heads, PAD, rows), lambda i, _: (0, 0, i)),
            pl.BlockSpec((heads, HD, rows), lambda i, _: (0, 0, i)),
            pl.BlockSpec((1, rows, width), lambda i, _: (i, 0, 0)),
        ],
        [
            shape_of((heads, 5, rows, PAD), BF),
            shape_of((heads, 5, rows, PAD), BF),
            shape_of((heads, 5, HD, rows), BF),
            shape_of((heads, PAD, 4 * rows), BF),
            shape_of((heads, HD, 4 * rows), BF),
            shape_of((4, rows, width), BF),
        ],
        scratch=[pltpu.VMEM((heads, 5, PAD, rows), BF)],
        prefetch=1,
        flops=heads * 4 * rows * 5 * rows * 1024,
    )(limits, normed, memory, weights, out_weights)


def attend_two_body(
    limits, normed, memory, pooled, weights, out_weights, skip,
    keys, values, keys_t, queries_t, heads_t, partial, values_t, total,
):
    head = pl.program_id(0)
    make_pairs(limits, 0, normed, memory, weights[0], keys, values, keys_t, values_t)
    heads, asked = attend_rows(pooled[...], weights[0], keys.at[0], values_t)
    heads_t[0] = heads
    queries_t[0] = asked

    @pl.when(head == 0)
    def _():
        total[...] = dot(pooled[...], skip[...])

    total[...] += dot(heads, out_weights[0], TN)

    @pl.when(head == pl.num_programs(0) - 1)
    def _():
        partial[...] = total[...].astype(BF)


def attend_two(limits, normed, memory, pooled, weights, out_weights, skip):
    _, rows, width = normed.shape
    heads = weights.shape[0]
    wide = out_weights.shape[2]

    def each(*shape):
        return pl.BlockSpec((1,) + shape, lambda h, _: (h,) + (0,) * len(shape))

    return call(
        attend_two_body,
        "attend_two",
        (heads,),
        [
            whole((4, rows, width)),
            whole((rows, width)),
            whole((rows, width)),
            each(*weights.shape[1:]),
            each(HD, wide),
            whole(skip.shape),
        ],
        [
            each(5, rows, PAD),
            each(5, rows, PAD),
            each(5, HD, rows),
            each(PAD, rows),
            each(HD, rows),
            whole((rows, wide)),
        ],
        [
            shape_of((heads, 5, rows, PAD), BF),
            shape_of((heads, 5, rows, PAD), BF),
            shape_of((heads, 5, HD, rows), BF),
            shape_of((heads, PAD, rows), BF),
            shape_of((heads, HD, rows), BF),
            shape_of((rows, wide), BF),
        ],
        scratch=[pltpu.VMEM((5, PAD, rows), BF), pltpu.VMEM((rows, wide), F32)],
        prefetch=1,
        flops=heads * rows * 5 * rows * 1024,
    )(limits, normed, memory, pooled, weights, out_weights, skip)


def grad_chunk(keys, values, keys_t, asked, given):
    chances = jnp.exp2(dot(keys, asked))
    spread = dot(values, given)
    grad_scores = (chances * spread).astype(BF)
    grad_values = dot(chances.astype(BF), given, NT)
    grad_keys = dot(grad_scores, asked, NT)
    return grad_keys, grad_values, dot(keys_t, grad_scores)


def given_rows(out_weights, grad, heads):
    back = dot(out_weights, grad, NT).astype(BF)
    inner = jnp.sum(back.astype(F32) * heads.astype(F32), 0, keepdims=True)
    high, middle, low = split_three(inner)
    index = lax.broadcasted_iota(jnp.int32, (PAD - HD, grad.shape[0]), 0)
    tail = jnp.where(index == 0, -high, jnp.where(index == 1, -middle, jnp.where(index == 2, -low, 0.0)))
    return jnp.concatenate([back, tail.astype(BF)], 0)


def back_two_body(
    after, grad_normed, cotangent, gain, normed, memory, pooled, weights, out_weights, skip,
    keys, values, keys_t, queries_t, heads_t,
    grad_rows, grad_memory, grad_weights, grad_out, grad_skip, grad_gain,
    branch, total, total_pool,
):
    head = pl.program_id(0)

    @pl.when(head == 0)
    def _():
        back, terms = norm_grads(after[...], gain[...], grad_normed[...].astype(F32))
        grad_gain[...] = jnp.sum(terms, 0, keepdims=True)
        branch[...] = (cotangent[0, 0] + back).astype(BF)
        grad_skip[...] = dot(pooled[...], branch[...], TN).astype(BF)
        total_pool[...] = dot(branch[...], skip[...], NT)
        total[...] = jnp.zeros_like(total)

    given = given_rows(out_weights[0], branch[...], heads_t[0])
    grad_out[0] = dot(heads_t[0], branch[...]).astype(BF)
    asked = queries_t[0]
    grad_query, grad_pair = None, None
    for chunk in range(5):
        grad_keys, grad_values, term = grad_chunk(
            keys[0, chunk], values[0, chunk], keys_t[0, chunk], asked, given
        )
        grad_query = term if grad_query is None else grad_query + term
        pair = jnp.concatenate([(grad_keys * LN2).astype(BF), grad_values.astype(BF)], 1)
        total[chunk] += dot(pair, weights[0, PAD:])
        source = normed[chunk] if chunk < 4 else memory[...]
        term = dot(pair, source, TN)
        grad_pair = term if grad_pair is None else grad_pair + term
    grad_query = (grad_query * SCALING).astype(BF)
    total_pool[...] += dot(grad_query, weights[0, :HD], TN)
    grad_weights[0, 0] = dot(grad_query, pooled[...]).astype(BF)
    grad_weights[0, 1] = grad_pair[:HD].astype(BF)
    grad_weights[0, 2] = grad_pair[PAD : PAD + HD].astype(BF)

    @pl.when(head == pl.num_programs(0) - 1)
    def _():
        for chunk in range(4):
            grad_rows[chunk] = (total[chunk] + 0.25 * total_pool[...]).astype(BF)
        grad_memory[...] = total[4].astype(BF)


def back_two(
    micro, after, grad_normed, cotangent, gain, normed, memory, pooled, weights, out_weights, skip, kept
):
    _, rows, width = normed.shape
    heads = weights.shape[0]
    wide = out_weights.shape[2]

    def each(*shape):
        return pl.BlockSpec((1,) + shape, lambda h, _: (h,) + (0,) * len(shape))

    def body(_, *refs):
        back_two_body(*refs)

    return call(
        body,
        "back_two",
        (heads,),
        [
            whole((rows, wide)),
            whole((rows, wide)),
            pl.BlockSpec((1, 1, rows, wide), lambda h, m: (m[0], 0, 0, 0)),
            whole((1, wide)),
            whole((4, rows, width)),
            whole((rows, width)),
            whole((rows, width)),
            each(*weights.shape[1:]),
            each(HD, wide),
            whole(skip.shape),
            each(5, rows, PAD),
            each(5, rows, PAD),
            each(5, HD, rows),
            each(PAD, rows),
            each(HD, rows),
        ],
        [
            whole((4, rows, width)),
            whole((rows, width)),
            each(3, HD, width),
            each(HD, wide),
            whole((width, wide)),
            whole((1, wide)),
        ],
        [
            shape_of((4, rows, width), BF),
            shape_of((rows, width), BF),
            shape_of((heads, 3, HD, width), BF),
            shape_of((heads, HD, wide), BF),
            shape_of((width, wide), BF),
            shape_of((1, wide), F32),
        ],
        scratch=[
            pltpu.VMEM((rows, wide), BF),
            pltpu.VMEM((5, rows, width), F32),
            pltpu.VMEM((rows, width), F32),
        ],
        prefetch=1,
        flops=heads * rows * 5 * rows * 2560,
    )(
        micro, after, grad_normed, cotangent, gain.reshape(1, -1), normed, memory, pooled, weights,
        out_weights, skip, *kept,
    )


def back_one_body(
    grad_two, after, own_part, other_part, gain, normed, memory, weights, out_weights,
    keys, values, keys_t, queries_t, heads_t,
    grad_one, grad_rows, grad_memory, grad_weights, grad_out, grad_gain,
    total, total_keys, total_values, total_query, total_out,
):
    slab = pl.program_id(0)

    @pl.when(slab == 0)
    def _():
        total_keys[...] = jnp.zeros_like(total_keys)
        total_values[...] = jnp.zeros_like(total_values)
        total_query[...] = jnp.zeros_like(total_query)
        total_out[...] = jnp.zeros_like(total_out)
        grad_gain[...] = jnp.zeros_like(grad_gain)

    arrived = own_part[0].astype(F32) + other_part[0].astype(F32)
    back, terms = norm_grads(after[0], gain[...], arrived)
    grad_gain[...] += jnp.sum(terms, 0, keepdims=True)
    state = grad_two[0] + back
    grad_one[0] = state
    branch = state.astype(BF)
    source = normed[slab]
    rows_total = None
    for head in range(2):
        given = given_rows(out_weights[head], branch, heads_t[head])
        total_out[head] += dot(heads_t[head], branch)
        asked = queries_t[head]
        grad_query = None
        for chunk in range(5):
            grad_keys, grad_values, term = grad_chunk(
                keys[head, chunk], values[head, chunk], keys_t[head, chunk], asked, given
            )
            total_keys[head, chunk] += grad_keys
            total_values[head, chunk] += grad_values
            grad_query = term if grad_query is None else grad_query + term
        grad_query = (grad_query * SCALING).astype(BF)
        term = dot(grad_query, weights[head, :HD], TN)
        rows_total = term if rows_total is None else rows_total + term
        total_query[head] += dot(grad_query, source)
    total[slab] = rows_total

    @pl.when(slab == pl.num_programs(0) - 1)
    def _():
        total[4] = jnp.zeros(total.shape[1:], F32)
        for head in range(2):
            grad_pair = None
            for chunk in range(5):
                pair = jnp.concatenate(
                    [
                        (total_keys[head, chunk] * LN2).astype(BF),
                        total_values[head, chunk].astype(BF),
                    ],
                    1,
                )
                total[chunk] += dot(pair, weights[head, PAD:])
                rows_here = normed[chunk] if chunk < 4 else memory[...]
                term = dot(pair, rows_here, TN)
                grad_pair = term if grad_pair is None else grad_pair + term
            grad_weights[head, 0] = total_query[head].astype(BF)
            grad_weights[head, 1] = grad_pair[:HD].astype(BF)
            grad_weights[head, 2] = grad_pair[PAD : PAD + HD].astype(BF)
            grad_out[head] = total_out[head].astype(BF)
        for chunk in range(4):
            grad_rows[chunk] = total[chunk].astype(BF)
        grad_memory[...] = total[4].astype(BF)


def back_one(
    grad_two, after, own_part, other_part, gain, normed, memory, weights, out_weights, kept
):
    _, rows, width = normed.shape
    heads = weights.shape[0]
    slab = pl.BlockSpec((1, rows, width), lambda i: (i, 0, 0))
    return call(
        back_one_body,
        "back_one",
        (4,),
        [
            slab,
            slab,
            slab,
            slab,
            whole((1, width)),
            whole((4, rows, width)),
            whole((rows, width)),
            whole(weights.shape),
            whole(out_weights.shape),
            whole((heads, 5, rows, PAD)),
            whole((heads, 5, rows, PAD)),
            whole((heads, 5, HD, rows)),
            pl.BlockSpec((heads, PAD, rows), lambda i: (0, 0, i)),
            pl.BlockSpec((heads, HD, rows), lambda i: (0, 0, i)),
        ],
        [
            slab,
            whole((4, rows, width)),
            whole((rows, width)),
            whole((heads, 3, HD, width)),
            whole((heads, HD, width)),
            whole((1, width)),
        ],
        [
            shape_of((4, rows, width), F32),
            shape_of((4, rows, width), BF),
            shape_of((rows, width), BF),
            shape_of((heads, 3, HD, width), BF),
            shape_of((heads, HD, width), BF),
            shape_of((1, width), F32),
        ],
        scratch=[
            pltpu.VMEM((5, rows, width), F32),
            pltpu.VMEM((heads, 5, rows, PAD), F32),
            pltpu.VMEM((heads, 5, rows, PAD), F32),
            pltpu.VMEM((heads, HD, width), F32),
            pltpu.VMEM((heads, HD, width), F32),
        ],
        flops=heads * 4 * rows * 5 * rows * 2560,
    )(
        grad_two, after, own_part, other_part, gain.reshape(1, -1), normed, memory, weights,
        out_weights, *kept,
    )


def flat(block):
    return block.reshape(block.shape[0] * block.shape[1], block.shape[2])


def hidden_one_body(_, x_ref, own_part, other_part, gain, w_in, w_out, after, partial, lanes):
    own = jnp.concatenate(slabs_of(x_ref[0, 0], lanes), 0)
    state = own + (flat(own_part[...]).astype(F32) + flat(other_part[...]).astype(F32))
    after[...] = state.reshape(after.shape)
    normed = (state * rms_factor(state) * gain[...]).astype(BF)
    active = gelu_only(dot(normed, w_in[...], NT)).astype(BF)
    partial[...] = dot(active, w_out[...]).astype(BF).reshape(partial.shape)


def hidden_one(micro, tokens, own_part, other_part, gain, w_in, w_out):
    _, rows, width = own_part.shape
    block = rows // 4
    strip = pl.BlockSpec((4, block, width), lambda i, m: (0, i, 0))
    return call(
        hidden_one_body,
        "hidden_one",
        (4,),
        [
            pl.BlockSpec((1, 1, 4 * block, width), lambda i, m: (m[0], 0, i, 0)),
            strip,
            strip,
            whole((1, width)),
            whole(w_in.shape),
            whole(w_out.shape),
        ],
        [strip, strip],
        [shape_of((4, rows, width), F32), shape_of((4, rows, width), BF)],
        scratch=[lane_scratch(4 * block, width)],
        prefetch=1,
        flops=4 * rows * width * w_in.shape[0] * 4,
    )(micro, tokens, own_part, other_part, gain.reshape(1, -1), w_in, w_out)


def norm_three_body(state, own_part, other_part, gain, after, normed, pooled):
    total = None
    for slab in range(4):
        values = state[slab] + (own_part[slab].astype(F32) + other_part[slab].astype(F32))
        after[slab] = values
        rows = (values * rms_factor(values) * gain[...]).astype(BF)
        normed[slab] = rows
        total = rows.astype(F32) if total is None else total + rows.astype(F32)
    pooled[...] = (total * 0.25).astype(BF)


def norm_three(state, own_part, other_part, gain):
    _, rows, width = state.shape
    block = rows // 4
    strip = pl.BlockSpec((4, block, width), lambda i: (0, i, 0))
    return call(
        norm_three_body,
        "norm_three",
        (4,),
        [strip, strip, strip, whole((1, width))],
        [strip, strip, pl.BlockSpec((block, width), lambda i: (i, 0))],
        [
            shape_of((4, rows, width), F32),
            shape_of((4, rows, width), BF),
            shape_of((rows, width), BF),
        ],
        flops=4 * rows * width * 8,
    )(state, own_part, other_part, gain.reshape(1, -1))


def hidden_one_back_body(
    after_two, own_part, other_part, memory_part, gain_three, after_one, gain_two, w_in, w_out,
    grad_two, partial, grad_in, grad_out, grad_gain, total_in, total_out,
):
    step = pl.program_id(0)

    @pl.when(step == 0)
    def _():
        total_in[...] = jnp.zeros_like(total_in)
        total_out[...] = jnp.zeros_like(total_out)
        grad_gain[...] = jnp.zeros_like(grad_gain)

    memory = memory_part[...].astype(F32) * 0.25
    arrived = flat(own_part[...]).astype(F32) + flat(other_part[...]).astype(F32)
    arrived = arrived + jnp.concatenate([memory] * 4, 0)
    back, terms = norm_grads(flat(after_two[...]), gain_three[...], arrived)
    grad_gain[...] += jnp.sum(terms, 0, keepdims=True)
    grad_two[...] = back.reshape(grad_two.shape)
    branch = back.astype(BF)
    state = flat(after_one[...])
    normed = (state * rms_factor(state) * gain_two[...]).astype(BF)
    active, slope = gelu_parts(dot(normed, w_in[...], NT))
    grad_pre = (slope * dot(branch, w_out[...], NT)).astype(BF)
    partial[...] = dot(grad_pre, w_in[...]).astype(BF).reshape(partial.shape)
    total_out[...] += dot(active.astype(BF), branch, TN)
    total_in[...] += dot(grad_pre, normed, TN)

    @pl.when(step == pl.num_programs(0) - 1)
    def _():
        grad_in[...] = total_in[...].astype(BF)
        grad_out[...] = total_out[...].astype(BF)


def hidden_one_back(
    after_two, own_part, other_part, memory_part, gain_three, after_one, gain_two, w_in, w_out
):
    _, rows, width = after_two.shape
    block = rows // 4
    hidden = w_in.shape[0]
    strip = pl.BlockSpec((4, block, width), lambda i: (0, i, 0))
    return call(
        hidden_one_back_body,
        "hidden_one_back",
        (4,),
        [
            strip,
            strip,
            strip,
            pl.BlockSpec((block, width), lambda i: (i, 0)),
            whole((1, width)),
            strip,
            whole((1, width)),
            whole(w_in.shape),
            whole(w_out.shape),
        ],
        [strip, strip, whole(w_in.shape), whole(w_out.shape), whole((1, width))],
        [
            shape_of((4, rows, width), F32),
            shape_of((4, rows, width), BF),
            shape_of(w_in.shape, BF),
            shape_of(w_out.shape, BF),
            shape_of((1, width), F32),
        ],
        scratch=[pltpu.VMEM((hidden, width), F32), pltpu.VMEM((hidden, width), F32)],
        flops=4 * rows * width * hidden * 10,
    )(
        after_two, own_part, other_part, memory_part, gain_three.reshape(1, -1), after_one,
        gain_two.reshape(1, -1), w_in, w_out,
    )


def norm_four_body(own_part, other_part, gain, after, normed):
    state = own_part[...].astype(F32) + other_part[...].astype(F32)
    after[...] = state
    normed[...] = (state * rms_factor(state) * gain[...]).astype(BF)


def norm_four(own_part, other_part, gain):
    rows, wide = own_part.shape
    strip = pl.BlockSpec((rows // 2, wide), lambda i: (i, 0))
    return call(
        norm_four_body,
        "norm_four",
        (2,),
        [strip, strip, whole((1, wide))],
        [strip, strip],
        [shape_of((rows, wide), F32), shape_of((rows, wide), BF)],
        flops=rows * wide * 8,
    )(own_part, other_part, gain.reshape(1, -1))


def hidden_two_body(_, normed, cotangent, w_in, w_out, active_ref, grad_pre_ref, grad_normed, result):
    active, slope = gelu_parts(dot(normed[...], w_in[...]))
    active = active.astype(BF)
    grad_pre = (slope * dot(cotangent[0, 0].astype(BF), w_out[...], NT)).astype(BF)
    grad_normed[...] = dot(grad_pre, w_in[...], NT).astype(BF)
    active_ref[...] = active
    grad_pre_ref[...] = grad_pre
    result[...] = dot(active, w_out[...]).astype(BF)


def hidden_two(micro, normed, cotangent, w_in, w_out):
    rows, wide = normed.shape
    hidden = w_in.shape[1]
    block = rows // 2
    strip = pl.BlockSpec((block, wide), lambda i, m: (i, 0))
    strip_hidden = pl.BlockSpec((block, hidden), lambda i, m: (i, 0))
    return call(
        hidden_two_body,
        "hidden_two",
        (2,),
        [
            strip,
            pl.BlockSpec((1, 1, block, wide), lambda i, m: (m[0], 0, i, 0)),
            whole(w_in.shape),
            whole(w_out.shape),
        ],
        [strip_hidden, strip_hidden, strip, strip],
        [
            shape_of((rows, hidden), BF),
            shape_of((rows, hidden), BF),
            shape_of((rows, wide), BF),
            shape_of((rows, wide), BF),
        ],
        prefetch=1,
        flops=rows * wide * hidden * 8,
    )(micro, normed, cotangent, w_in, w_out)


def hidden_two_weights_body(
    _, own_normed, own_active, own_pre, other_normed, other_active, other_pre, own_cot, other_cot,
    grad_in, grad_out,
):
    grad_in[...] = (
        dot(own_normed[...], own_pre[...], TN) + dot(other_normed[...], other_pre[...], TN)
    ).astype(BF)
    grad_out[...] = (
        dot(own_active[...], own_cot[0, 0].astype(BF), TN)
        + dot(other_active[...], other_cot[0, 0].astype(BF), TN)
    ).astype(BF)


def hidden_two_weights(micros, own, other, cotangent):
    rows, wide = own[0].shape
    hidden = own[1].shape[1]
    parts = 3
    column = pl.BlockSpec((rows, wide // parts), lambda i, m: (0, i))
    column_hidden = pl.BlockSpec((rows, hidden // parts), lambda i, m: (0, i))
    return call(
        hidden_two_weights_body,
        "hidden_two_weights",
        (parts,),
        [
            column,
            column_hidden,
            whole((rows, hidden)),
            column,
            column_hidden,
            whole((rows, hidden)),
            pl.BlockSpec((1, 1, rows, wide), lambda i, m: (m[0], 0, 0, 0)),
            pl.BlockSpec((1, 1, rows, wide), lambda i, m: (m[1], 0, 0, 0)),
        ],
        [
            pl.BlockSpec((wide // parts, hidden), lambda i, m: (i, 0)),
            pl.BlockSpec((hidden // parts, wide), lambda i, m: (i, 0)),
        ],
        [shape_of((wide, hidden), BF), shape_of((hidden, wide), BF)],
        prefetch=1,
        flops=rows * wide * hidden * 8,
    )(micros, *own, *other, cotangent, cotangent)


def exit_body(place, x_ref, grad_one, partial, memory_part, gain, grad_input, grad_gain, lanes):
    block = memory_part.shape[0]
    slabs = slabs_of(x_ref[0, 0], lanes)
    memory = memory_part[...].astype(F32) * 0.25
    total = None
    for slab in range(4):
        back, terms = norm_grads(slabs[slab], gain[...], partial[slab, 0].astype(F32) + memory)
        result = grad_one[slab] + back
        for part in range(lanes.shape[0]):
            lanes[part, pl.ds(slab, block, stride=4), :] = result[:, part * PAD : (part + 1) * PAD]
        terms = jnp.sum(terms, 0, keepdims=True)
        total = terms if total is None else total + terms
    for part in range(lanes.shape[0]):
        grad_input[:, part * PAD : (part + 1) * PAD] = lanes[part]
    grad_gain[...] = total


def exit_norm(place, tokens, grad_one, partial, memory_part, gain):
    length, width = tokens.shape[2:]
    share = length // 4
    block = share // 4
    return call(
        exit_body,
        "exit_norm",
        (1,),
        [
            pl.BlockSpec((1, 1, share, width), lambda i, p: (p[0], 0, p[1], 0)),
            pl.BlockSpec((4, block, width), lambda i, p: (0, p[1], 0)),
            pl.BlockSpec((4, 1, block, width), lambda i, p: (0, p[2], 0, 0)),
            pl.BlockSpec((block, width), lambda i, p: (p[1], 0)),
            whole((1, width)),
        ],
        [whole((share, width)), whole((1, width))],
        [shape_of((share, width), F32), shape_of((1, width), F32)],
        scratch=[lane_scratch(share, width)],
        prefetch=1,
        flops=share * width * 16,
    )(place, tokens, grad_one, partial, memory_part, gain.reshape(1, -1))


def swap(block, axis, bit):
    return lax.ppermute(block, axis, [(i, i ^ bit) for i in range(lax.axis_size(axis))])


def shifted(block, distance):
    devices = range(lax.axis_size("clip"))
    route = [(i - distance, i) for i in devices if i - distance in devices]
    return lax.ppermute(block, "clip", route)


def after(block, earlier):
    return lax.optimization_barrier((block, earlier))[0]


def in_order(core, mine, theirs):
    ordered = jnp.where(core == 0, jnp.stack([mine, theirs]), jnp.stack([theirs, mine]))
    return ordered.reshape((-1,) + mine.shape[1:])


def share_of(block, core):
    half = block.shape[0] // 2
    return lax.dynamic_slice_in_dim(block, core * half, half, 0)


def clip_sum(block):
    step = 1
    while step < lax.axis_size("clip"):
        block = block + swap(block, "clip", step)
        step *= 2
    return block


def with_partner(own, earlier=None):
    sent = own if earlier is None else after(own, earlier)
    return jnp.stack([own, swap(sent, "tensor", 2)])


def shifted_halves(core, block, distance):
    part = shifted(share_of(block, core), distance)
    return in_order(core, part, swap(part, "tensor", 1))


def chip_total(core, own, other):
    kept, sent = [], []
    for block in (own, other):
        kept.append(share_of(block, core))
        sent.append(share_of(block, 1 - core))
    got = swap(jnp.stack(sent), "tensor", 1)
    near = (kept[0].astype(F32) + got[0].astype(F32))
    far = (kept[1].astype(F32) + got[1].astype(F32)).astype(BF)
    return near + swap(far, "tensor", 2).astype(F32)


def pad_heads(turned):
    widths = [(0, 0)] * (turned.ndim - 2) + [(0, PAD - HD), (0, 0)]
    padded = jnp.pad(turned, widths)
    return padded.reshape(turned.shape[:-3] + (3 * PAD, turned.shape[-1]))


def per_device(
    tokens_in,
    gain_one,
    heads_in_one,
    heads_out_one,
    gain_two,
    hidden_in_one,
    hidden_out_one,
    gain_three,
    heads_in_two,
    skip_weight,
    heads_out_two,
    gain_four,
    hidden_in_two,
    hidden_out_two,
    resolution,
    continues,
    cotangent,
):
    clip_index = lax.axis_index("clip")
    part_index = lax.axis_index("tensor")
    chip, core = part_index // 2, part_index % 2
    micro = chip.astype(jnp.int32).reshape(1)
    other_micro = 1 - micro
    length, width = tokens_in.shape[2:]
    rows = length // 4
    wide = heads_out_two.shape[1]

    own_res = resolution[chip, clip_index]
    prev_res = resolution[chip, jnp.maximum(clip_index - 1, 0)]
    carried = (continues[chip, clip_index] == 1) & (clip_index > 0)
    own_len = jnp.where(own_res == 1, length, TOK_LOW)
    prev_len = jnp.where(carried, jnp.where(prev_res == 1, length, TOK_LOW), 0)
    limits = jnp.stack([own_len, prev_len]).astype(jnp.int32)

    turned_one = jnp.transpose(heads_in_one, (1, 2, 0))
    heads_one_w = with_partner(turned_one)
    weights_one = pad_heads(heads_one_w)
    out_one = with_partner(heads_out_one)
    in_w_one = jnp.transpose(hidden_in_one)
    hidden_pair = with_partner(jnp.stack([in_w_one, hidden_out_one]), heads_one_w)
    w_in_one = hidden_pair[:, 0].reshape(-1, width)
    w_out_one = hidden_pair[:, 1].reshape(-1, width)
    turned_two = jnp.transpose(heads_in_two, (1, 2, 0)).reshape(3, -1, HD, width)
    heads_two_w = with_partner(jnp.swapaxes(turned_two, 0, 1), hidden_pair)
    weights_two = pad_heads(heads_two_w.reshape((-1,) + heads_two_w.shape[2:]))
    skip_rows = skip_weight.shape[0]
    two_rows = with_partner(jnp.concatenate([skip_weight, heads_out_two], 0), heads_two_w)
    out_two = two_rows[:, skip_rows:].reshape(-1, HD, wide)
    skip = jnp.zeros((width, wide), BF)
    skip = lax.dynamic_update_slice(skip, two_rows[0, :skip_rows], (part_index * skip_rows, 0))
    skip = lax.dynamic_update_slice(skip, two_rows[1, :skip_rows], ((part_index ^ 2) * skip_rows, 0))

    normed_one, pooled_one = entry_norm(micro, tokens_in, gain_one)
    memory_one = shifted_halves(core, pooled_one, 1)
    *kept_one, attn_part = attend_one(limits, normed_one, memory_one, weights_one, out_one)
    after_one, ffn_part = hidden_one(
        micro, tokens_in, attn_part, swap(attn_part, "tensor", 1), gain_two, w_in_one, w_out_one
    )
    after_two, normed_three, pooled_three = norm_three(
        after_one, ffn_part, swap(ffn_part, "tensor", 1), gain_three
    )

    memory_two = shifted_halves(core, pooled_three, 1)
    *kept_two, branch_part = attend_two(
        limits, normed_three, memory_two, pooled_three, weights_two, out_two, skip
    )
    after_three, normed_four = norm_four(branch_part, swap(branch_part, "tensor", 1), gain_four)
    far_half = swap(share_of(normed_four, core), "tensor", 2)
    far_normed = in_order(core, far_half, swap(far_half, "tensor", 1))
    own_active, own_pre, own_grad, own_result = hidden_two(
        micro, normed_four, cotangent, hidden_in_two, hidden_out_two
    )
    far_active, far_pre, far_grad, far_result = hidden_two(
        other_micro, far_normed, cotangent, hidden_in_two, hidden_out_two
    )
    grad_half = chip_total(core, own_grad, far_grad).astype(BF)
    grad_normed_four = in_order(core, grad_half, swap(grad_half, "tensor", 1))
    w_hidden_two = hidden_two_weights(
        jnp.concatenate([micro, other_micro]),
        (normed_four, own_active, own_pre),
        (far_normed, far_active, far_pre),
        cotangent,
    )
    totals_hidden_two = lax.psum(tuple(w_hidden_two), "clip")

    result_half = chip_total(core, own_result, far_result) + share_of(after_three, core)
    result_half = result_half.astype(BF)
    far_result_half = swap(result_half, "tensor", 2)
    result_pair = jnp.where(
        chip == 0,
        jnp.stack([result_half, far_result_half]),
        jnp.stack([far_result_half, result_half]),
    )
    other_pair = swap(result_pair, "tensor", 1)
    output = jnp.where(
        core == 0,
        jnp.concatenate([result_pair, other_pair], 1),
        jnp.concatenate([other_pair, result_pair], 1),
    ).astype(F32)

    grad_rows_two, grad_memory_two, w_in_two, w_out_two, w_skip, w_gain_four = back_two(
        micro, after_three, grad_normed_four, cotangent, gain_four, normed_three, memory_two,
        pooled_three, weights_two, out_two, skip, kept_two,
    )
    memory_part = share_of(grad_memory_two, core).astype(F32) + swap(
        share_of(grad_memory_two, 1 - core), "tensor", 1
    ).astype(F32)
    memory_part = shifted(memory_part.astype(BF), -1)
    memory_back_two = in_order(core, memory_part, swap(memory_part, "tensor", 1))

    grad_two, grad_part_two, w_in_hidden, w_out_hidden, w_gain_three = hidden_one_back(
        after_two, grad_rows_two, swap(grad_rows_two, "tensor", 1), memory_back_two, gain_three,
        after_one, gain_two, w_in_one, w_out_one,
    )
    grad_one, grad_rows_one, grad_memory_one, w_heads_one, w_heads_out, w_gain_two = back_one(
        grad_two, after_one, grad_part_two, swap(grad_part_two, "tensor", 1), gain_two, normed_one,
        memory_one, weights_one, out_one, kept_one,
    )
    memory_part = share_of(grad_memory_one, core).astype(F32) + swap(
        share_of(grad_memory_one, 1 - core), "tensor", 1
    ).astype(F32)
    memory_part = shifted(memory_part.astype(BF), -1)
    memory_back_one = in_order(core, memory_part, swap(memory_part, "tensor", 1))
    by_share = grad_rows_one.reshape(4, 2, 2, rows // 4, width)
    mine = lax.dynamic_index_in_dim(by_share, core, 2, keepdims=False)
    theirs = lax.dynamic_index_in_dim(by_share, 1 - core, 2, keepdims=False)
    got = swap(theirs, "tensor", 1)
    mine = (mine.astype(F32) + got.astype(F32)).astype(BF)

    def leave(which):
        place = jnp.stack([chip, which * 2 + core, which]).astype(jnp.int32)
        return exit_norm(place, tokens_in, grad_one, mine, memory_back_one, gain_one)

    far_input, far_gain = leave(1 - chip)
    far_input = swap(far_input.astype(BF), "tensor", 2).astype(F32)
    near_input, near_gain = leave(chip)
    grad_input = jnp.where(
        chip == 0, jnp.stack([near_input, far_input]), jnp.stack([far_input, near_input])
    )

    def over_chips(block):
        return block[0].astype(F32) + swap(block[1], "tensor", 2).astype(F32)

    w_two = w_in_two.reshape((2, -1) + w_in_two.shape[1:])
    w_two = over_chips(w_two)
    skip_own = lax.dynamic_slice_in_dim(w_skip, part_index * skip_rows, skip_rows, 0)
    skip_sent = lax.dynamic_slice_in_dim(w_skip, (part_index ^ 2) * skip_rows, skip_rows, 0)
    w_rows = w_out_two.reshape(2, -1, wide)
    w_rows = over_chips(
        jnp.stack(
            [
                jnp.concatenate([skip_own, w_rows[0]], 0),
                jnp.concatenate([skip_sent, w_rows[1]], 0),
            ]
        )
    )
    totals_two = lax.psum((w_two.astype(BF), w_rows.astype(BF)), "clip")
    hidden_grads = jnp.stack([w_in_hidden, w_out_hidden]).reshape(2, 2, -1, width)
    hidden_grads = over_chips(jnp.swapaxes(hidden_grads, 0, 1))
    totals_hidden_one = clip_sum(hidden_grads.astype(BF))
    last = jnp.concatenate([w_heads_one.reshape(2, -1, width), w_heads_out], 1)
    totals_last = clip_sum(over_chips(last).astype(BF))
    w_gain_one = (far_gain + near_gain)
    w_gain_one = w_gain_one + swap(w_gain_one, "tensor", 1)
    gains = jnp.concatenate([w_gain_one, w_gain_two, w_gain_three, w_gain_four], 1)
    gains = clip_sum(gains + swap(gains, "tensor", 2))[0]

    grad_heads_in_two = jnp.transpose(
        jnp.swapaxes(totals_two[0], 0, 1).reshape(3, -1, width), (2, 0, 1)
    ).astype(F32)
    heads_in_rows = 3 * HD
    grad_heads_in_one = jnp.transpose(
        totals_last[:heads_in_rows].reshape(3, HD, width), (2, 0, 1)
    ).astype(F32)
    return (
        output[:, None],
        grad_input[:, None],
        gains[:width],
        grad_heads_in_one,
        totals_last[heads_in_rows:].astype(F32),
        gains[width : 2 * width],
        jnp.transpose(totals_hidden_one[0]).astype(F32),
        totals_hidden_one[1].astype(F32),
        gains[2 * width : 3 * width],
        grad_heads_in_two,
        totals_two[1][:skip_rows].astype(F32),
        totals_two[1][skip_rows:].astype(F32),
        gains[3 * width :],
        totals_hidden_two[0].astype(F32),
        totals_hidden_two[1].astype(F32),
    )


def solution(mesh):
    return jax.shard_map(
        per_device,
        mesh=mesh,
        in_specs=(
            P(None, "clip", None, None),
            P(),
            P(None, None, "tensor"),
            P("tensor", None),
            P(),
            P(None, "tensor"),
            P("tensor", None),
            P(),
            P(None, None, "tensor"),
            P("tensor", None),
            P("tensor", None),
            P(),
            P(None, "tensor"),
            P("tensor", None),
            P(),
            P(),
            P(None, "clip", None, None),
        ),
        out_specs=(
            P(None, "clip", None, None),
            P(None, "clip", "tensor", None),
            P(),
            P(None, None, "tensor"),
            P("tensor", None),
            P(),
            P(None, "tensor"),
            P("tensor", None),
            P(),
            P(None, None, "tensor"),
            P("tensor", None),
            P("tensor", None),
            P(),
            P(None, "tensor"),
            P("tensor", None),
        ),
        check_vma=False,
    )
```

```python
import functools

import jax
import jax.numpy as jnp
from jax import lax
from jax.experimental import pallas as pl
from jax.experimental.pallas import tpu as pltpu
from jax.sharding import PartitionSpec as P

HD = 96
PAD = 128
TOK_LOW = 1052
EPSILON = 1e-06
MASKED_SCORE = -1e30
LOG2E = 1.4426950408889634
LN2 = 0.6931471805599453
SCALING = HD ** (-0.5)
BF = jnp.bfloat16
F32 = jnp.float32
MIB = 2**20
LARGE_MIB = 60
SMALL_MIB = 28

NN = (((1,), (0,)), ((), ()))
NT = (((1,), (1,)), ((), ()))
TN = (((0,), (0,)), ((), ()))


def dot(left, right, form=NN):
    return lax.dot_general(left, right, form, preferred_element_type=F32)


def rms_factor(values):
    return lax.rsqrt(jnp.mean(values * values, -1, keepdims=True) + EPSILON)


def norm_grads(values, gain, grad):
    factor = rms_factor(values)
    scaled = values * factor
    term = grad * gain
    inner = jnp.mean(scaled * term, -1, keepdims=True)
    return factor * (term - scaled * inner), grad * scaled


def gelu_parts(values):
    root = 0.7978845608028654
    square = values * values
    tanh = jnp.tanh(values * (root + (root * 0.044715) * square))
    half = 0.5 + 0.5 * tanh
    slope = half + (0.5 * values) * (1.0 - tanh * tanh) * (root + (3 * root * 0.044715) * square)
    return values * half, slope


def gelu_only(values):
    root = 0.7978845608028654
    tanh = jnp.tanh(values * (root + (root * 0.044715) * (values * values)))
    return values * (0.5 + 0.5 * tanh)


def split_three(row):
    high = row.astype(BF).astype(F32)
    rest = row - high
    middle = rest.astype(BF).astype(F32)
    return high, middle, rest - middle


def call(body, name, grid, in_specs, out_specs, out_shape, scratch=(), prefetch=0, vmem=SMALL_MIB):
    return pl.pallas_call(
        body,
        name=name,
        grid_spec=pltpu.PrefetchScalarGridSpec(
            num_scalar_prefetch=prefetch,
            grid=grid,
            in_specs=in_specs,
            out_specs=out_specs,
            scratch_shapes=list(scratch),
        ),
        out_shape=out_shape,
        compiler_params=pltpu.CompilerParams(vmem_limit_bytes=vmem * MIB),
        cost_estimate=pl.CostEstimate(
            flops=MIB, bytes_accessed=MIB // 4, transcendentals=0
        ),
    )


def whole(shape):
    return pl.BlockSpec(shape, lambda *_: (0,) * len(shape))


def shape_of(shape, dtype):
    return jax.ShapeDtypeStruct(shape, dtype)


def lane_scratch(rows, width):
    return pltpu.VMEM((width // PAD, rows, PAD), F32)


def slabs_of(block, lanes):
    parts = lanes.shape[0]
    rows = block.shape[0] // 4
    for part in range(parts):
        lanes[part] = block[:, part * PAD : (part + 1) * PAD]
    return [
        jnp.concatenate([lanes[part, pl.ds(s, rows, stride=4), :] for part in range(parts)], 1)
        for s in range(4)
    ]


def entry_body(_, x_ref, gain_ref, normed_ref, pooled_ref, lanes):
    total = None
    slabs = slabs_of(x_ref[0, 0], lanes)
    for slab in range(4):
        values = slabs[slab]
        normed = (values * rms_factor(values) * gain_ref[...]).astype(BF)
        normed_ref[slab] = normed
        part = normed.astype(F32)
        total = part if total is None else total + part
    pooled_ref[...] = (total * 0.25).astype(BF)


def entry_norm(micro, tokens, gain):
    length, width = tokens.shape[2:]
    rows = length // 4
    block = rows // 4
    return call(
        entry_body,
        "entry_norm",
        (4,),
        [
            pl.BlockSpec((1, 1, 4 * block, width), lambda i, m: (m[0], 0, i, 0)),
            whole((1, width)),
        ],
        [
            pl.BlockSpec((4, block, width), lambda i, m: (0, i, 0)),
            pl.BlockSpec((block, width), lambda i, m: (i, 0)),
        ],
        [shape_of((4, rows, width), BF), shape_of((rows, width), BF)],
        scratch=[lane_scratch(4 * block, width)],
        prefetch=1,
    )(micro, tokens, gain.reshape(1, -1))


def make_pair(limit, offset, source, weights):
    rows = source.shape[0]
    place = lax.broadcasted_iota(jnp.int32, (rows, 1), 0) * 4 + offset
    lane = lax.broadcasted_iota(jnp.int32, (rows, PAD), 1)
    bias = jnp.where(place < limit, 0.0, MASKED_SCORE)
    both = dot(source, weights[PAD:], NT)
    keys = jnp.where(lane < HD, both[:, :PAD], jnp.where(lane == HD, bias, 1.0))
    values = jnp.where(lane < HD, both[:, PAD:], 1.0)
    turned = dot(weights[PAD:], source, NT)
    tail = jnp.ones((PAD - HD, rows), F32)
    values_t = jnp.concatenate([turned[PAD : PAD + HD], tail], 0)
    return keys.astype(BF), values.astype(BF), turned[:HD].astype(BF), values_t.astype(BF)


def own_pairs_body(limits, normed, weights, *results):
    parts = make_pair(limits[0], pl.program_id(0), normed[0], weights[0])
    for result, part in zip(results, parts):
        result[0, 0] = part


def pair_shapes(rows):
    return [(rows, PAD), (rows, PAD), (HD, rows), (PAD, rows)]


def own_pairs(limits, normed, weights):
    _, rows, width = normed.shape
    heads = weights.shape[0]
    return call(
        own_pairs_body,
        "own_pairs",
        (4, heads),
        [
            pl.BlockSpec((1, rows, width), lambda i, h, _: (i, 0, 0)),
            pl.BlockSpec((1, 3 * PAD, width), lambda i, h, _: (h, 0, 0)),
        ],
        [
            pl.BlockSpec((1, 1) + shape, lambda i, h, _: (h, i, 0, 0))
            for shape in pair_shapes(rows)
        ],
        [shape_of((heads, 4) + shape, BF) for shape in pair_shapes(rows)],
        prefetch=1,
    )(limits, normed, weights)


def query_tail(rows, parts):
    index = lax.broadcasted_iota(jnp.int32, (PAD - HD, rows), 0)
    tail = jnp.where(index == 0, 1.0, 0.0)
    for step, part in enumerate(parts):
        tail = jnp.where(index == step + 1, -part, tail)
    return tail.astype(BF)


def attend_rows(source, weights, keys, values_t):
    rows = source.shape[0]
    query = (dot(weights[:HD], source, NT) * (SCALING * LOG2E)).astype(BF)
    asked = jnp.concatenate([query, query_tail(rows, ())], 0)
    parts = range(rows // 256)
    scores = [
        dot(keys(chunk)[part * 256 : (part + 1) * 256], asked) for chunk in range(5) for part in parts
    ]
    top = functools.reduce(jnp.maximum, [jnp.max(item, 0, keepdims=True) for item in scores])
    result = None
    for chunk in range(5):
        for part in parts:
            raised = jnp.exp2(scores[chunk * len(parts) + part] - top).astype(BF)
            term = dot(values_t(chunk)[:, part * 256 : (part + 1) * 256], raised)
            result = term if result is None else result + term
    summed = result[HD : HD + 1]
    heads = (result[:HD] / summed).astype(BF)
    logsum = top + jnp.log2(summed)
    return heads, jnp.concatenate([query, query_tail(rows, split_three(logsum))], 0)


def chosen(own, memory, head):
    return lambda chunk: own[head, chunk] if chunk < 4 else memory[head]


def attend_one_body(
    limits, normed, memory, weights, out_weights, own_keys, own_values_t,
    keys, values, keys_t, queries_t, heads_t, partial, values_t,
):
    @pl.when(pl.program_id(0) == 0)
    def _():
        for head in range(2):
            parts = make_pair(limits[1], 0, memory[...], weights[head])
            keys[head], values[head], keys_t[head], values_t[head] = parts

    total = None
    for head in range(2):
        heads, asked = attend_rows(
            normed[0], weights[head], chosen(own_keys, keys, head),
            chosen(own_values_t, values_t, head),
        )
        heads_t[head] = heads
        queries_t[head] = asked
        term = dot(heads, out_weights[head], TN)
        total = term if total is None else total + term
    partial[0] = total.astype(BF)


def attend_one(limits, normed, memory, weights, out_weights, own_keys, own_values_t):
    _, rows, width = normed.shape
    heads = weights.shape[0]
    memory_shapes = [(heads,) + shape for shape in pair_shapes(rows)]
    return call(
        attend_one_body,
        "attend_one",
        (4,),
        [
            pl.BlockSpec((1, rows, width), lambda i, _: (i, 0, 0)),
            whole((rows, width)),
            whole(weights.shape),
            whole(out_weights.shape),
            whole(own_keys.shape),
            whole(own_values_t.shape),
        ],
        [whole(shape) for shape in memory_shapes[:3]]
        + [
            pl.BlockSpec((heads, PAD, rows), lambda i, _: (0, 0, i)),
            pl.BlockSpec((heads, HD, rows), lambda i, _: (0, 0, i)),
            pl.BlockSpec((1, rows, width), lambda i, _: (i, 0, 0)),
        ],
        [shape_of(shape, BF) for shape in memory_shapes[:3]]
        + [
            shape_of((heads, PAD, 4 * rows), BF),
            shape_of((heads, HD, 4 * rows), BF),
            shape_of((4, rows, width), BF),
        ],
        scratch=[pltpu.VMEM(memory_shapes[3], BF)],
        prefetch=1,
        vmem=LARGE_MIB,
    )(limits, normed, memory, weights, out_weights, own_keys, own_values_t)


def attend_two_body(
    limits, memory, pooled, weights, out_weights, skip, own_keys, own_values_t,
    keys, values, keys_t, queries_t, heads_t, partial, values_t, total,
):
    head = pl.program_id(0)
    keys[0], values[0], keys_t[0], values_t[0] = make_pair(limits[1], 0, memory[...], weights[0])
    heads, asked = attend_rows(
        pooled[...], weights[0], chosen(own_keys, keys, 0), chosen(own_values_t, values_t, 0)
    )
    heads_t[0] = heads
    queries_t[0] = asked

    @pl.when(head == 0)
    def _():
        total[...] = dot(pooled[...], skip[...])

    total[...] += dot(heads, out_weights[0], TN)

    @pl.when(head == pl.num_programs(0) - 1)
    def _():
        partial[...] = total[...].astype(BF)


def attend_two(limits, memory, pooled, weights, out_weights, skip, own_keys, own_values_t):
    rows, width = pooled.shape
    heads = weights.shape[0]
    wide = out_weights.shape[2]

    def each(*shape):
        return pl.BlockSpec((1,) + shape, lambda h, _: (h,) + (0,) * len(shape))

    results = pair_shapes(rows)[:3] + [(PAD, rows), (HD, rows)]
    return call(
        attend_two_body,
        "attend_two",
        (heads,),
        [
            whole((rows, width)),
            whole((rows, width)),
            each(*weights.shape[1:]),
            each(HD, wide),
            whole(skip.shape),
            each(4, rows, PAD),
            each(4, PAD, rows),
        ],
        [each(*shape) for shape in results] + [whole((rows, wide))],
        [shape_of((heads,) + shape, BF) for shape in results] + [shape_of((rows, wide), BF)],
        scratch=[pltpu.VMEM((1, PAD, rows), BF), pltpu.VMEM((rows, wide), F32)],
        prefetch=1,
        vmem=LARGE_MIB,
    )(limits, memory, pooled, weights, out_weights, skip, own_keys, own_values_t)


def grad_chunk(keys, values, keys_t, asked, given):
    chances = jnp.exp2(dot(keys, asked))
    spread = dot(values, given)
    grad_scores = (chances * spread).astype(BF)
    grad_values = dot(chances.astype(BF), given, NT)
    grad_keys = dot(grad_scores, asked, NT)
    return grad_keys, grad_values, dot(keys_t, grad_scores)


def given_rows(out_weights, grad, heads):
    back = dot(out_weights, grad, NT).astype(BF)
    inner = jnp.sum(back.astype(F32) * heads.astype(F32), 0, keepdims=True)
    high, middle, low = split_three(inner)
    index = lax.broadcasted_iota(jnp.int32, (PAD - HD, grad.shape[0]), 0)
    tail = jnp.where(index == 0, -high, jnp.where(index == 1, -middle, jnp.where(index == 2, -low, 0.0)))
    return jnp.concatenate([back, tail.astype(BF)], 0)


def pair_of(grad_keys, grad_values):
    return jnp.concatenate([(grad_keys * LN2).astype(BF), grad_values.astype(BF)], 1)


def plus(total, term):
    return term if total is None else total + term


class Kept:
    def __init__(self, refs, head):
        own_keys, own_values, own_keys_t, keys, values, keys_t, self.queries, self.heads = refs
        self.keys = chosen(own_keys, keys, head)
        self.values = chosen(own_values, values, head)
        self.keys_t = chosen(own_keys_t, keys_t, head)
        self.head = head

    def grads(self, chunk, given):
        return grad_chunk(
            self.keys(chunk), self.values(chunk), self.keys_t(chunk), self.queries[self.head], given
        )

    def given(self, out_weights, branch):
        return given_rows(out_weights[self.head], branch, self.heads[self.head])


def put_sides(target, columns):
    width = target.shape[1]
    for side in range(columns.shape[1] // width):
        target[side * HD : (side + 1) * HD] = columns[:, side * width : (side + 1) * width]


def two_first_body(
    _, after, grad_normed, cotangent, gain, normed, memory, pooled, weights, out_weights, skip, *refs
):
    kept, results, scratch = Kept(refs[:8], 0), refs[8:17], refs[17:]
    (branch, grad_gain, grad_skip, grad_rows, grad_pool, grad_memory, grad_weights,
     query_memory, pair_memory) = results
    total, = scratch
    step = pl.program_id(0)
    width = pooled.shape[1]

    @pl.when(step == 0)
    def _():
        back, terms = norm_grads(after[...], gain[...], grad_normed[...].astype(F32))
        grad_gain[...] = jnp.sum(terms, 0, keepdims=True)
        branch[...] = (cotangent[0, 0] + back).astype(BF)
        columns = dot(pooled[...], branch[...], TN).astype(BF)
        for share in range(grad_skip.shape[0]):
            put_sides(grad_skip.at[share], columns[share * HD : (share + 1) * HD])
        grad_pool[...] = dot(branch[...], skip[...], NT)
        total[...] = jnp.zeros_like(total)

    given = kept.given(out_weights, branch[...])

    @pl.when(step < 2)
    def _():
        grad_query, grad_pair = None, None
        for chunk in range(5):
            grad_keys, grad_values, term = kept.grads(chunk, given)
            grad_query = plus(grad_query, term)
            pair = pair_of(grad_keys, grad_values)
            total[chunk] += dot(pair, weights[0, PAD:])
            source = normed[chunk] if chunk < 4 else memory[...]
            grad_pair = plus(grad_pair, dot(pair, source, TN))
        grad_query = (grad_query * SCALING).astype(BF)
        grad_pool[...] += dot(grad_query, weights[0, :HD], TN)
        grad_weights[0, :HD] = dot(grad_query, pooled[...]).astype(BF)
        grad_weights[0, HD : 2 * HD] = grad_pair[:HD].astype(BF)
        grad_weights[0, 2 * HD : 3 * HD] = grad_pair[PAD : PAD + HD].astype(BF)
        columns = dot(kept.heads[0], branch[...]).astype(BF)
        put_sides(grad_weights.at[0, 3 * HD :], columns)

    @pl.when(step >= 2)
    def _():
        grad_keys, grad_values, term = kept.grads(4, given)
        query_memory[0] = term
        pair = pair_of(grad_keys, grad_values)
        total[4] += dot(pair, weights[0, PAD:])
        pair_memory[0] = dot(pair, memory[...], TN)

    @pl.when(step == 3)
    def _():
        for chunk in range(4):
            grad_rows[chunk] = total[chunk].astype(BF)
        grad_memory[...] = total[4].astype(BF)


def two_second_body(
    branch, normed, pooled, weights, out_weights, earlier_rows, earlier_pool, query_memory,
    pair_memory, *refs
):
    kept, (grad_rows, grad_weights, total, total_pool) = Kept(refs[:8], 0), refs[8:]
    step = pl.program_id(0)

    @pl.when(step == 0)
    def _():
        total_pool[...] = earlier_pool[...]
        for chunk in range(4):
            total[chunk] = earlier_rows[chunk].astype(F32)

    given = kept.given(out_weights, branch[...])
    grad_query, grad_pair = query_memory[0], pair_memory[0]
    for chunk in range(4):
        grad_keys, grad_values, term = kept.grads(chunk, given)
        grad_query = grad_query + term
        pair = pair_of(grad_keys, grad_values)
        total[chunk] += dot(pair, weights[0, PAD:])
        grad_pair = grad_pair + dot(pair, normed[chunk], TN)
    grad_query = (grad_query * SCALING).astype(BF)
    total_pool[...] += dot(grad_query, weights[0, :HD], TN)
    grad_weights[0, :HD] = dot(grad_query, pooled[...]).astype(BF)
    grad_weights[0, HD : 2 * HD] = grad_pair[:HD].astype(BF)
    grad_weights[0, 2 * HD : 3 * HD] = grad_pair[PAD : PAD + HD].astype(BF)
    put_sides(grad_weights.at[0, 3 * HD :], dot(kept.heads[0], branch[...]).astype(BF))

    @pl.when(step == pl.num_programs(0) - 1)
    def _():
        for chunk in range(4):
            grad_rows[chunk] = (total[chunk] + 0.25 * total_pool[...]).astype(BF)


def kept_specs(each, rows):
    pair = pair_shapes(rows)[:3]
    return [each(4, *shape) for shape in pair] + [each(*shape) for shape in pair]


def two_first(
    micro, after, grad_normed, cotangent, gain, normed, memory, pooled, weights, out_weights, skip, kept
):
    _, rows, width = normed.shape
    wide = out_weights.shape[2]
    sides = wide // width
    head_rows = (3 + sides) * HD

    def each(*shape):
        return pl.BlockSpec((1,) + shape, lambda h, _: ((h + 2) % 4,) + (0,) * len(shape))

    def early(*shape):
        return pl.BlockSpec((1,) + shape, lambda h, _: (jnp.minimum(h, 1),) + (0,) * len(shape))

    def late(*shape):
        return pl.BlockSpec((1,) + shape, lambda h, _: (jnp.maximum(h, 2) - 2,) + (0,) * len(shape))

    return call(
        two_first_body,
        "back_two_first",
        (4,),
        [
            whole((rows, wide)),
            whole((rows, wide)),
            pl.BlockSpec((1, 1, rows, wide), lambda h, m: (m[0], 0, 0, 0)),
            whole((1, wide)),
            whole((4, rows, width)),
            whole((rows, width)),
            whole((rows, width)),
            each(*weights.shape[1:]),
            each(HD, wide),
            whole(skip.shape),
        ]
        + kept_specs(each, rows)
        + [each(PAD, rows), each(HD, rows)],
        [
            whole((rows, wide)),
            whole((1, wide)),
            whole((width // HD, sides * HD, width)),
            whole((4, rows, width)),
            whole((rows, width)),
            whole((rows, width)),
            early(head_rows, width),
            late(HD, rows),
            late(2 * PAD, width),
        ],
        [
            shape_of((rows, wide), BF),
            shape_of((1, wide), F32),
            shape_of((width // HD, sides * HD, width), BF),
            shape_of((4, rows, width), BF),
            shape_of((rows, width), F32),
            shape_of((rows, width), BF),
            shape_of((2, head_rows, width), BF),
            shape_of((2, HD, rows), F32),
            shape_of((2, 2 * PAD, width), F32),
        ],
        scratch=[pltpu.VMEM((5, rows, width), F32)],
        prefetch=1,
        vmem=LARGE_MIB,
    )(
        micro, after, grad_normed, cotangent, gain.reshape(1, -1), normed, memory, pooled, weights,
        out_weights, skip, *kept,
    )


def two_second(
    branch, normed, pooled, weights, out_weights, earlier_rows, earlier_pool, query_memory,
    pair_memory, kept
):
    _, rows, width = normed.shape
    wide = out_weights.shape[2]
    head_rows = (3 + wide // width) * HD

    def each(*shape):
        return pl.BlockSpec((1,) + shape, lambda h: (h,) + (0,) * len(shape))

    return call(
        two_second_body,
        "back_two_second",
        (2,),
        [
            whole((rows, wide)),
            whole((4, rows, width)),
            whole((rows, width)),
            each(*weights.shape[1:]),
            each(HD, wide),
            whole((4, rows, width)),
            whole((rows, width)),
            each(HD, rows),
            each(2 * PAD, width),
        ]
        + kept_specs(each, rows)
        + [each(PAD, rows), each(HD, rows)],
        [whole((4, rows, width)), each(head_rows, width)],
        [shape_of((4, rows, width), BF), shape_of((2, head_rows, width), BF)],
        scratch=[pltpu.VMEM((4, rows, width), F32), pltpu.VMEM((rows, width), F32)],
        vmem=LARGE_MIB,
    )(
        branch, normed, pooled, weights, out_weights, earlier_rows, earlier_pool, query_memory,
        pair_memory, *kept,
    )


def one_first_body(
    grad_two, after, own_part, other_part, gain, normed, memory, weights, out_weights, *refs
):
    kept, near_kept = Kept(refs[:8], 1), Kept(refs[:8], 0)
    (grad_one, branch_ref, grad_gain, grad_rows, grad_memory, grad_weights, query_memory,
     pair_memory) = refs[8:16]
    total, total_keys, total_values, total_query, total_out, near_keys, near_values = refs[16:]
    slab = pl.program_id(0)

    @pl.when(slab == 0)
    def _():
        for item in (grad_gain, total_keys, total_values, total_query, total_out, near_keys, near_values):
            item[...] = jnp.zeros_like(item)

    arrived = own_part[0].astype(F32) + other_part[0].astype(F32)
    back, terms = norm_grads(after[0], gain[...], arrived)
    grad_gain[...] += jnp.sum(terms, 0, keepdims=True)
    state = grad_two[0] + back
    grad_one[0] = state
    branch = state.astype(BF)
    branch_ref[0] = branch
    given = kept.given(out_weights, branch)
    grad_query = None
    for chunk in range(5):
        grad_keys, grad_values, term = kept.grads(chunk, given)
        total_keys[chunk] += grad_keys
        total_values[chunk] += grad_values
        grad_query = plus(grad_query, term)
    grad_keys, grad_values, term = near_kept.grads(4, near_kept.given(out_weights, branch))
    near_keys[...] += grad_keys
    near_values[...] += grad_values
    query_memory[...] = term
    grad_query = (grad_query * SCALING).astype(BF)
    total_out[...] += dot(kept.heads[1], branch)
    total_query[...] += dot(grad_query, normed[slab])
    total[slab] = dot(grad_query, weights[1, :HD], TN)

    @pl.when(slab == pl.num_programs(0) - 1)
    def _():
        pair = pair_of(near_keys[...], near_values[...])
        pair_memory[...] = dot(pair, memory[...], TN)
        near_rows = dot(pair, weights[0, PAD:])
        grad_pair = None
        for chunk in range(5):
            pair = pair_of(total_keys[chunk], total_values[chunk])
            rows = dot(pair, weights[1, PAD:])
            source = normed[chunk] if chunk < 4 else memory[...]
            grad_pair = plus(grad_pair, dot(pair, source, TN))
            if chunk < 4:
                grad_rows[chunk] = (total[chunk] + rows).astype(BF)
            else:
                grad_memory[...] = (near_rows + rows).astype(BF)
        grad_weights[:HD] = total_query[...].astype(BF)
        grad_weights[HD : 2 * HD] = grad_pair[:HD].astype(BF)
        grad_weights[2 * HD : 3 * HD] = grad_pair[PAD : PAD + HD].astype(BF)
        grad_weights[3 * HD :] = total_out[...].astype(BF)


def one_second_body(
    branch_ref, normed, weights, out_weights, earlier_rows, query_memory, pair_memory, *refs
):
    kept, (grad_rows, grad_weights) = Kept(refs[:8], 0), refs[8:10]
    total, total_keys, total_values, total_query, total_out = refs[10:]
    slab = pl.program_id(0)

    @pl.when(slab == 0)
    def _():
        for item in (total_keys, total_values, total_query, total_out):
            item[...] = jnp.zeros_like(item)

    branch = branch_ref[0]
    given = kept.given(out_weights, branch)
    grad_query = query_memory[...]
    for chunk in range(4):
        grad_keys, grad_values, term = kept.grads(chunk, given)
        total_keys[chunk] += grad_keys
        total_values[chunk] += grad_values
        grad_query = grad_query + term
    grad_query = (grad_query * SCALING).astype(BF)
    total_out[...] += dot(kept.heads[0], branch)
    total_query[...] += dot(grad_query, normed[slab])
    total[slab] = dot(grad_query, weights[0, :HD], TN)

    @pl.when(slab == pl.num_programs(0) - 1)
    def _():
        grad_pair = pair_memory[...]
        for chunk in range(4):
            pair = pair_of(total_keys[chunk], total_values[chunk])
            rows = dot(pair, weights[0, PAD:]) + earlier_rows[chunk].astype(F32)
            grad_rows[chunk] = (total[chunk] + rows).astype(BF)
            grad_pair = grad_pair + dot(pair, normed[chunk], TN)
        grad_weights[:HD] = total_query[...].astype(BF)
        grad_weights[HD : 2 * HD] = grad_pair[:HD].astype(BF)
        grad_weights[2 * HD : 3 * HD] = grad_pair[PAD : PAD + HD].astype(BF)
        grad_weights[3 * HD :] = total_out[...].astype(BF)


def one_specs(rows):
    def heads(*shape):
        return whole((2,) + shape)

    return kept_specs(heads, rows) + [
        pl.BlockSpec((2, PAD, rows), lambda i: (0, 0, i)),
        pl.BlockSpec((2, HD, rows), lambda i: (0, 0, i)),
    ]


def one_scratch(rows, width, chunks):
    return [
        pltpu.VMEM((4, rows, width), F32),
        pltpu.VMEM((chunks, rows, PAD), F32),
        pltpu.VMEM((chunks, rows, PAD), F32),
        pltpu.VMEM((HD, width), F32),
        pltpu.VMEM((HD, width), F32),
    ]


def one_first(grad_two, after, own_part, other_part, gain, normed, memory, weights, out_weights, kept):
    _, rows, width = grad_two.shape
    slab = pl.BlockSpec((1, rows, width), lambda i: (i, 0, 0))
    return call(
        one_first_body,
        "back_one_first",
        (4,),
        [slab, slab, slab, slab, whole((1, width)), whole((4, rows, width)), whole((rows, width))]
        + [whole(weights.shape), whole(out_weights.shape)]
        + one_specs(rows),
        [
            slab,
            slab,
            whole((1, width)),
            whole((4, rows, width)),
            whole((rows, width)),
            whole((4 * HD, width)),
            pl.BlockSpec((HD, rows), lambda i: (0, i)),
            whole((2 * PAD, width)),
        ],
        [
            shape_of((4, rows, width), F32),
            shape_of((4, rows, width), BF),
            shape_of((1, width), F32),
            shape_of((4, rows, width), BF),
            shape_of((rows, width), BF),
            shape_of((4 * HD, width), BF),
            shape_of((HD, 4 * rows), F32),
            shape_of((2 * PAD, width), F32),
        ],
        scratch=one_scratch(rows, width, 5)
        + [pltpu.VMEM((rows, PAD), F32), pltpu.VMEM((rows, PAD), F32)],
        vmem=LARGE_MIB,
    )(
        grad_two, after, own_part, other_part, gain.reshape(1, -1), normed, memory, weights,
        out_weights, *kept,
    )


def one_second(branch, normed, weights, out_weights, earlier_rows, query_memory, pair_memory, kept):
    _, rows, width = branch.shape
    slab = pl.BlockSpec((1, rows, width), lambda i: (i, 0, 0))
    return call(
        one_second_body,
        "back_one_second",
        (4,),
        [
            slab,
            whole((4, rows, width)),
            whole(weights.shape),
            whole(out_weights.shape),
            whole((4, rows, width)),
            pl.BlockSpec((HD, rows), lambda i: (0, i)),
            whole((2 * PAD, width)),
        ]
        + one_specs(rows),
        [whole((4, rows, width)), whole((4 * HD, width))],
        [shape_of((4, rows, width), BF), shape_of((4 * HD, width), BF)],
        scratch=one_scratch(rows, width, 4),
        vmem=LARGE_MIB,
    )(branch, normed, weights, out_weights, earlier_rows, query_memory, pair_memory, *kept)


def flat(block):
    return block.reshape(block.shape[0] * block.shape[1], block.shape[2])


def hidden_one_body(_, x_ref, own_part, other_part, gain, w_in, w_out, after, partial, lanes):
    own = jnp.concatenate(slabs_of(x_ref[0, 0], lanes), 0)
    state = own + (flat(own_part[...]).astype(F32) + flat(other_part[...]).astype(F32))
    after[...] = state.reshape(after.shape)
    normed = (state * rms_factor(state) * gain[...]).astype(BF)
    active = gelu_only(dot(normed, w_in[...], NT)).astype(BF)
    partial[...] = dot(active, w_out[...]).astype(BF).reshape(partial.shape)


def hidden_one(micro, tokens, own_part, other_part, gain, w_in, w_out):
    _, rows, width = own_part.shape
    block = rows // 4
    strip = pl.BlockSpec((4, block, width), lambda i, m: (0, i, 0))
    return call(
        hidden_one_body,
        "hidden_one",
        (4,),
        [
            pl.BlockSpec((1, 1, 4 * block, width), lambda i, m: (m[0], 0, i, 0)),
            strip,
            strip,
            whole((1, width)),
            whole(w_in.shape),
            whole(w_out.shape),
        ],
        [strip, strip],
        [shape_of((4, rows, width), F32), shape_of((4, rows, width), BF)],
        scratch=[lane_scratch(4 * block, width)],
        prefetch=1,
    )(micro, tokens, own_part, other_part, gain.reshape(1, -1), w_in, w_out)


def norm_three_body(state, own_part, other_part, gain, after, normed, pooled):
    total = None
    for slab in range(4):
        values = state[slab] + (own_part[slab].astype(F32) + other_part[slab].astype(F32))
        after[slab] = values
        rows = (values * rms_factor(values) * gain[...]).astype(BF)
        normed[slab] = rows
        total = rows.astype(F32) if total is None else total + rows.astype(F32)
    pooled[...] = (total * 0.25).astype(BF)


def norm_three(state, own_part, other_part, gain):
    _, rows, width = state.shape
    block = rows // 4
    strip = pl.BlockSpec((4, block, width), lambda i: (0, i, 0))
    return call(
        norm_three_body,
        "norm_three",
        (4,),
        [strip, strip, strip, whole((1, width))],
        [strip, strip, pl.BlockSpec((block, width), lambda i: (i, 0))],
        [
            shape_of((4, rows, width), F32),
            shape_of((4, rows, width), BF),
            shape_of((rows, width), BF),
        ],
    )(state, own_part, other_part, gain.reshape(1, -1))


def hidden_one_back_body(
    after_two, own_part, other_part, memory_part, gain_three, after_one, gain_two, w_in, w_out,
    grad_two, partial, grad_in, grad_out, grad_gain, total_in, total_out,
):
    step = pl.program_id(0)

    @pl.when(step == 0)
    def _():
        total_in[...] = jnp.zeros_like(total_in)
        total_out[...] = jnp.zeros_like(total_out)
        grad_gain[...] = jnp.zeros_like(grad_gain)

    memory = memory_part[...].astype(F32) * 0.25
    arrived = flat(own_part[...]).astype(F32) + flat(other_part[...]).astype(F32)
    arrived = arrived + jnp.concatenate([memory] * 4, 0)
    back, terms = norm_grads(flat(after_two[...]), gain_three[...], arrived)
    grad_gain[...] += jnp.sum(terms, 0, keepdims=True)
    grad_two[...] = back.reshape(grad_two.shape)
    branch = back.astype(BF)
    state = flat(after_one[...])
    normed = (state * rms_factor(state) * gain_two[...]).astype(BF)
    active, slope = gelu_parts(dot(normed, w_in[...], NT))
    grad_pre = (slope * dot(branch, w_out[...], NT)).astype(BF)
    partial[...] = dot(grad_pre, w_in[...]).astype(BF).reshape(partial.shape)
    total_out[...] += dot(active.astype(BF), branch, TN)
    total_in[...] += dot(grad_pre, normed, TN)

    @pl.when(step == pl.num_programs(0) - 1)
    def _():
        grad_in[...] = total_in[...].astype(BF)
        grad_out[...] = total_out[...].astype(BF)


def hidden_one_back(
    after_two, own_part, other_part, memory_part, gain_three, after_one, gain_two, w_in, w_out
):
    _, rows, width = after_two.shape
    block = rows // 4
    hidden = w_in.shape[0]
    strip = pl.BlockSpec((4, block, width), lambda i: (0, i, 0))
    return call(
        hidden_one_back_body,
        "hidden_one_back",
        (4,),
        [
            strip,
            strip,
            strip,
            pl.BlockSpec((block, width), lambda i: (i, 0)),
            whole((1, width)),
            strip,
            whole((1, width)),
            whole(w_in.shape),
            whole(w_out.shape),
        ],
        [strip, strip, whole(w_in.shape), whole(w_out.shape), whole((1, width))],
        [
            shape_of((4, rows, width), F32),
            shape_of((4, rows, width), BF),
            shape_of(w_in.shape, BF),
            shape_of(w_out.shape, BF),
            shape_of((1, width), F32),
        ],
        scratch=[pltpu.VMEM((hidden, width), F32), pltpu.VMEM((hidden, width), F32)],
    )(
        after_two, own_part, other_part, memory_part, gain_three.reshape(1, -1), after_one,
        gain_two.reshape(1, -1), w_in, w_out,
    )


def norm_four_body(own_part, other_part, gain, after, normed):
    state = own_part[...].astype(F32) + other_part[...].astype(F32)
    after[...] = state
    normed[...] = (state * rms_factor(state) * gain[...]).astype(BF)


def norm_four(own_part, other_part, gain):
    rows, wide = own_part.shape
    strip = pl.BlockSpec((rows // 2, wide), lambda i: (i, 0))
    return call(
        norm_four_body,
        "norm_four",
        (2,),
        [strip, strip, whole((1, wide))],
        [strip, strip],
        [shape_of((rows, wide), F32), shape_of((rows, wide), BF)],
    )(own_part, other_part, gain.reshape(1, -1))


def hidden_two_body(_, normed, cotangent, w_in, w_out, active_ref, grad_pre_ref, grad_normed, result):
    active, slope = gelu_parts(dot(normed[...], w_in[...]))
    active = active.astype(BF)
    grad_pre = (slope * dot(cotangent[0, 0].astype(BF), w_out[...], NT)).astype(BF)
    grad_normed[...] = dot(grad_pre, w_in[...], NT).astype(BF)
    active_ref[...] = active
    grad_pre_ref[...] = grad_pre
    result[...] = dot(active, w_out[...]).astype(BF)


def hidden_two(micro, normed, cotangent, w_in, w_out):
    rows, wide = normed.shape
    hidden = w_in.shape[1]
    block = rows // 2
    strip = pl.BlockSpec((block, wide), lambda i, m: (i, 0))
    strip_hidden = pl.BlockSpec((block, hidden), lambda i, m: (i, 0))
    return call(
        hidden_two_body,
        "hidden_two",
        (2,),
        [
            strip,
            pl.BlockSpec((1, 1, block, wide), lambda i, m: (m[0], 0, i, 0)),
            whole(w_in.shape),
            whole(w_out.shape),
        ],
        [strip_hidden, strip_hidden, strip, strip],
        [
            shape_of((rows, hidden), BF),
            shape_of((rows, hidden), BF),
            shape_of((rows, wide), BF),
            shape_of((rows, wide), BF),
        ],
        prefetch=1,
    )(micro, normed, cotangent, w_in, w_out)


def hidden_two_weights_body(
    _, own_normed, own_active, own_pre, other_normed, other_active, other_pre, own_cot, other_cot,
    grad_in, grad_out,
):
    grad_in[...] = (
        dot(own_normed[...], own_pre[...], TN) + dot(other_normed[...], other_pre[...], TN)
    ).astype(BF)
    grad_out[...] = (
        dot(own_active[...], own_cot[0, 0].astype(BF), TN)
        + dot(other_active[...], other_cot[0, 0].astype(BF), TN)
    ).astype(BF)


def hidden_two_weights(micros, own, other, cotangent):
    rows, wide = own[0].shape
    hidden = own[1].shape[1]
    parts = 3
    column = pl.BlockSpec((rows, wide // parts), lambda i, m: (0, i))
    column_hidden = pl.BlockSpec((rows, hidden // parts), lambda i, m: (0, i))
    return call(
        hidden_two_weights_body,
        "hidden_two_weights",
        (parts,),
        [
            column,
            column_hidden,
            whole((rows, hidden)),
            column,
            column_hidden,
            whole((rows, hidden)),
            pl.BlockSpec((1, 1, rows, wide), lambda i, m: (m[0], 0, 0, 0)),
            pl.BlockSpec((1, 1, rows, wide), lambda i, m: (m[1], 0, 0, 0)),
        ],
        [
            pl.BlockSpec((wide // parts, hidden), lambda i, m: (i, 0)),
            pl.BlockSpec((hidden // parts, wide), lambda i, m: (i, 0)),
        ],
        [shape_of((wide, hidden), BF), shape_of((hidden, wide), BF)],
        prefetch=1,
    )(micros, *own, *other, cotangent, cotangent)


def exit_body(place, x_ref, grad_one, partial, memory_part, gain, grad_input, grad_gain, lanes):
    block = memory_part.shape[0]
    slabs = slabs_of(x_ref[0, 0], lanes)
    memory = memory_part[...].astype(F32) * 0.25
    total = None
    for slab in range(4):
        back, terms = norm_grads(slabs[slab], gain[...], partial[slab, 0].astype(F32) + memory)
        result = grad_one[slab] + back
        for part in range(lanes.shape[0]):
            lanes[part, pl.ds(slab, block, stride=4), :] = result[:, part * PAD : (part + 1) * PAD]
        terms = jnp.sum(terms, 0, keepdims=True)
        total = terms if total is None else total + terms
    for part in range(lanes.shape[0]):
        grad_input[:, part * PAD : (part + 1) * PAD] = lanes[part]
    grad_gain[...] = total


def exit_norm(place, tokens, grad_one, partial, memory_part, gain):
    length, width = tokens.shape[2:]
    share = length // 4
    block = share // 4
    return call(
        exit_body,
        "exit_norm",
        (1,),
        [
            pl.BlockSpec((1, 1, share, width), lambda i, p: (p[0], 0, p[1], 0)),
            pl.BlockSpec((4, block, width), lambda i, p: (0, p[1], 0)),
            pl.BlockSpec((4, 1, block, width), lambda i, p: (0, p[2], 0, 0)),
            pl.BlockSpec((block, width), lambda i, p: (p[1], 0)),
            whole((1, width)),
        ],
        [whole((share, width)), whole((1, width))],
        [shape_of((share, width), F32), shape_of((1, width), F32)],
        scratch=[lane_scratch(share, width)],
        prefetch=1,
    )(place, tokens, grad_one, partial, memory_part, gain.reshape(1, -1))


def swap(block, axis, bit):
    return lax.ppermute(block, axis, [(i, i ^ bit) for i in range(lax.axis_size(axis))])


def shifted(block, distance):
    devices = lax.axis_size("clip")
    return lax.ppermute(block, "clip", [(i, (i + distance) % devices) for i in range(devices)])


def after(block, earlier):
    return lax.optimization_barrier((block, earlier))[0]


def in_order(core, mine, theirs):
    ordered = jnp.where(core == 0, jnp.stack([mine, theirs]), jnp.stack([theirs, mine]))
    return ordered.reshape((-1,) + mine.shape[1:])


def share_of(block, core):
    half = block.shape[0] // 2
    return lax.dynamic_slice_in_dim(block, core * half, half, 0)


def together(results, *others):
    return lax.optimization_barrier((results,) + others)


def clip_sum(block):
    step = 1
    while step < lax.axis_size("clip"):
        block = block + swap(block, "clip", step)
        step *= 2
    return block


class ClipSum:
    def __init__(self, block):
        clips = lax.axis_size("clip")
        self.index = lax.axis_index("clip")
        steps = [2**k for k in range(clips.bit_length() - 1)]
        halved = steps[:2]
        self.todo = [("halve", step) for step in halved] + [("add", step) for step in steps[2:]]
        self.todo += [("join", step) for step in reversed(halved)]
        self.block = block
        self.send()

    @classmethod
    def resumed(cls, block, todo, got):
        self = cls.__new__(cls)
        self.index = lax.axis_index("clip")
        self.block, self.todo, self.got = block, list(todo), got
        return self

    def send(self):
        kind, step = self.todo[0]
        bit = self.index // step % 2
        sent = share_of(self.block, 1 - bit) if kind == "halve" else self.block
        self.got = swap(sent, "clip", step)

    def take(self):
        kind, step = self.todo.pop(0)
        bit = self.index // step % 2
        got, self.got = self.got, None
        if kind == "join":
            self.block = in_order(bit, self.block, got)
        else:
            kept = share_of(self.block, bit) if kind == "halve" else self.block
            self.block = (kept.astype(F32) + got.astype(F32)).astype(BF)

    def step(self):
        self.take()
        if self.todo:
            self.send()

    def finish(self):
        while self.todo:
            self.step()
        return self.block


def shifted_halves(core, block, distance):
    part = shifted(share_of(block, core), distance)
    return in_order(core, part, swap(part, "tensor", 1))


def chip_sums(core, own, other):
    sent = jnp.stack([share_of(own, 1 - core), share_of(other, 1 - core)])
    got = swap(sent, "tensor", 1).astype(F32)
    return (
        share_of(own, core).astype(F32) + got[0],
        (share_of(other, core).astype(F32) + got[1]).astype(BF),
    )


def memory_grads(core, partial):
    got = swap(share_of(partial, 1 - core), "tensor", 1)
    part = share_of(partial, core).astype(F32) + got.astype(F32)
    return shifted(part.astype(BF), -1)


def pad_heads(turned):
    widths = [(0, 0)] * (turned.ndim - 2) + [(0, PAD - HD), (0, 0)]
    padded = jnp.pad(turned, widths)
    return padded.reshape(turned.shape[:-3] + (3 * PAD, turned.shape[-1]))


def per_device(
    tokens_in,
    gain_one,
    heads_in_one,
    heads_out_one,
    gain_two,
    hidden_in_one,
    hidden_out_one,
    gain_three,
    heads_in_two,
    skip_weight,
    heads_out_two,
    gain_four,
    hidden_in_two,
    hidden_out_two,
    resolution,
    continues,
    cotangent,
):
    clip_index = lax.axis_index("clip")
    part_index = lax.axis_index("tensor")
    chip, core = part_index // 2, part_index % 2
    micro = chip.astype(jnp.int32).reshape(1)
    other_micro = 1 - micro
    length, width = tokens_in.shape[2:]
    rows = length // 4
    wide = heads_out_two.shape[1]

    own_res = resolution[chip, clip_index]
    prev_res = resolution[chip, jnp.maximum(clip_index - 1, 0)]
    carried = (continues[chip, clip_index] == 1) & (clip_index > 0)
    own_len = jnp.where(own_res == 1, length, TOK_LOW)
    prev_len = jnp.where(carried, jnp.where(prev_res == 1, length, TOK_LOW), 0)
    limits = jnp.stack([own_len, prev_len]).astype(jnp.int32)

    skip_rows = skip_weight.shape[0]
    heads_rows = 3 * HD
    own_one = jnp.concatenate(
        [jnp.transpose(heads_in_one, (1, 2, 0)).reshape(heads_rows, width), heads_out_one], 0
    )
    far_one = swap(own_one, "tensor", 2)
    both_one = jnp.stack([own_one, far_one])
    weights_one = pad_heads(both_one[:, :heads_rows].reshape(2, 3, HD, width))
    out_one = both_one[:, heads_rows:]
    own_hidden = jnp.stack([jnp.transpose(hidden_in_one), hidden_out_one])
    far_hidden = swap(after(own_hidden, far_one), "tensor", 2)
    own_two = jnp.transpose(heads_in_two, (1, 2, 0)).reshape(3, -1, HD, width)
    own_two = jnp.swapaxes(own_two, 0, 1)
    far_two = swap(after(own_two, far_one), "tensor", 2)

    normed_one, pooled_one = entry_norm(micro, tokens_in, gain_one)
    memory_one = shifted_halves(core, pooled_one, 1)
    *own_kept_one, own_values_t = own_pairs(limits, normed_one, weights_one)
    memory_one, own_kept_one = together(memory_one, own_kept_one)
    *kept_one, attn_part = attend_one(
        limits, normed_one, memory_one, weights_one, out_one, own_kept_one[0], own_values_t
    )
    kept_one = own_kept_one + kept_one
    attn_part, far_hidden, far_two = together(attn_part, far_hidden, far_two)
    w_in_one = jnp.concatenate([own_hidden[0], far_hidden[0]], 0)
    w_out_one = jnp.concatenate([own_hidden[1], far_hidden[1]], 0)
    weights_two = pad_heads(jnp.concatenate([own_two, far_two], 0))
    own_rows = jnp.concatenate([skip_weight, heads_out_two], 0)
    far_rows = swap(after(own_rows, far_two), "tensor", 2)
    after_one, ffn_part = hidden_one(
        micro, tokens_in, attn_part, swap(attn_part, "tensor", 1), gain_two, w_in_one, w_out_one
    )
    after_two, normed_three, pooled_three = norm_three(
        after_one, ffn_part, swap(ffn_part, "tensor", 1), gain_three
    )
    pooled_three, far_rows = together(pooled_three, far_rows)
    out_two = jnp.concatenate([own_rows[skip_rows:], far_rows[skip_rows:]], 0).reshape(-1, HD, wide)
    skip = jnp.zeros((width, wide), BF)
    skip = lax.dynamic_update_slice(skip, own_rows[:skip_rows], (part_index * skip_rows, 0))
    skip = lax.dynamic_update_slice(skip, far_rows[:skip_rows], ((part_index ^ 2) * skip_rows, 0))

    memory_two = shifted_halves(core, pooled_three, 1)
    *own_kept_two, own_values_t = own_pairs(limits, normed_three, weights_two)
    memory_two, own_kept_two = together(memory_two, own_kept_two)
    *kept_two, branch_part = attend_two(
        limits, memory_two, pooled_three, weights_two, out_two, skip, own_kept_two[0], own_values_t
    )
    kept_two = own_kept_two + kept_two
    after_three, normed_four = norm_four(branch_part, swap(branch_part, "tensor", 1), gain_four)
    far_half = swap(share_of(normed_four, core), "tensor", 2)
    own_active, own_pre, own_grad, own_result = hidden_two(
        micro, normed_four, cotangent, hidden_in_two, hidden_out_two
    )
    far_half, own_grad = together(far_half, own_grad)
    far_normed = in_order(core, far_half, swap(far_half, "tensor", 1))
    far_active, far_pre, far_grad, far_result = hidden_two(
        other_micro, far_normed, cotangent, hidden_in_two, hidden_out_two
    )
    near, far = chip_sums(core, own_grad, far_grad)
    far = swap(far, "tensor", 2)
    w_hidden_two = hidden_two_weights(
        jnp.concatenate([micro, other_micro]),
        (normed_four, own_active, own_pre),
        (far_normed, far_active, far_pre),
        cotangent,
    )
    far, w_hidden_two, own_result, far_result = together(far, w_hidden_two, own_result, far_result)
    grad_half = (near + far.astype(F32)).astype(BF)
    grad_normed_four = in_order(core, grad_half, swap(grad_half, "tensor", 1))
    totals_hidden_two = lax.psum(tuple(w_hidden_two), "clip")

    def backward():
        branch_two, w_gain_four, w_skip, *early, grad_memory_two, w_two_sent, query_two, pair_two = (
            two_first(
                micro, after_three, grad_normed_four, cotangent, gain_four, normed_three, memory_two,
                pooled_three, weights_two, out_two, skip, kept_two,
            )
        )
        memory_part = memory_grads(core, grad_memory_two)
        w_skip_own = lax.dynamic_index_in_dim(w_skip, part_index, 0, keepdims=False)
        w_skip_sent = lax.dynamic_index_in_dim(w_skip, part_index ^ 2, 0, keepdims=False)
        w_two_far = swap(
            jnp.concatenate([w_two_sent.reshape(-1, width), w_skip_sent], 0), "tensor", 2
        )
        grad_rows_two, w_two = two_second(
            branch_two, normed_three, pooled_three, weights_two, out_two, *early, query_two,
            pair_two, kept_two,
        )
        grad_rows_two, memory_part, w_two, w_two_far = together(
            grad_rows_two, memory_part, w_two, w_two_far
        )
        memory_back_two = in_order(core, memory_part, swap(memory_part, "tensor", 1))
        w_two = jnp.concatenate([w_two.reshape(-1, width), w_skip_own], 0)
        total_two = ClipSum((w_two.astype(F32) + w_two_far.astype(F32)).astype(BF))
        result_near, result_far = chip_sums(core, own_result, far_result)
        result_far = swap(after(result_far, w_two_far), "tensor", 2)

        grad_two, grad_part_two, w_in_hidden, w_out_hidden, w_gain_three = hidden_one_back(
            after_two, grad_rows_two, swap(grad_rows_two, "tensor", 1), memory_back_two, gain_three,
            after_one, gain_two, w_in_one, w_out_one,
        )
        grad_part_two, total_two.got, result_far, w_in_hidden, w_out_hidden = together(
            grad_part_two, total_two.got, result_far, w_in_hidden, w_out_hidden
        )
        total_two.step()
        w_hidden = jnp.stack([w_in_hidden, w_out_hidden]).reshape(2, 2, -1, width)
        w_hidden, w_hidden_sent = (w_hidden[:, k].reshape(-1, width) for k in (0, 1))
        w_hidden_far = swap(w_hidden_sent, "tensor", 2)
        result_half = result_near + result_far.astype(F32) + share_of(after_three, core)
        result_half = result_half.astype(BF)
        grad_one, branch_one, w_gain_two, early_rows, grad_memory_one, w_last_sent, *memory_terms = (
            one_first(
                grad_two, after_one, grad_part_two, swap(grad_part_two, "tensor", 1), gain_two,
                normed_one, memory_one, weights_one, out_one, kept_one,
            )
        )
        branch_one, total_two.got, w_hidden_far, w_last_sent = together(
            branch_one, total_two.got, w_hidden_far, w_last_sent
        )
        total_two.step()
        total_hidden = ClipSum((w_hidden.astype(F32) + w_hidden_far.astype(F32)).astype(BF))
        memory_part = memory_grads(core, grad_memory_one)
        w_last_far = swap(w_last_sent, "tensor", 2)
        far_result_half = swap(after(result_half, w_hidden_far), "tensor", 2)
        grad_rows_one, w_last = one_second(
            branch_one, normed_one, weights_one, out_one, early_rows, *memory_terms, kept_one
        )
        results = together(
            grad_rows_one, memory_part, total_two.got, total_hidden.got, w_last, w_last_far,
            far_result_half,
        )
        return results + (
            grad_one, total_two.block, total_hidden.block, result_half, w_gain_two, w_gain_three,
            w_gain_four,
        ), (total_two.todo, total_hidden.todo)

    shapes = jax.eval_shape(lambda: backward()[0])
    stages = []

    def present():
        results, left = backward()
        stages.append(left)
        return results

    def absent():
        return tuple(jnp.zeros(item.shape, item.dtype) for item in shapes)

    results = lax.cond(own_len > 0, present, absent)
    left = stages[-1]
    results, totals_hidden_two = together(results, totals_hidden_two)
    (grad_rows_one, memory_part, got_two, got_hidden, w_last, w_last_far, far_result_half,
     grad_one, block_two, block_hidden, result_half, w_gain_two, w_gain_three, w_gain_four) = results
    total_two = ClipSum.resumed(block_two, left[0], got_two)
    total_hidden = ClipSum.resumed(block_hidden, left[1], got_hidden)
    total_last = ClipSum((w_last.astype(F32) + w_last_far.astype(F32)).astype(BF))
    total_two.step()
    total_hidden.step()
    memory_back_one = in_order(core, memory_part, swap(memory_part, "tensor", 1))
    by_share = grad_rows_one.reshape(4, 2, 2, rows // 4, width)
    mine = lax.dynamic_index_in_dim(by_share, core, 2, keepdims=False)
    theirs = lax.dynamic_index_in_dim(by_share, 1 - core, 2, keepdims=False)
    got = swap(theirs, "tensor", 1)
    mine = (mine.astype(F32) + got.astype(F32)).astype(BF)

    def leave(which):
        place = jnp.stack([chip, which * 2 + core, which]).astype(jnp.int32)
        return exit_norm(place, tokens_in, grad_one, mine, memory_back_one, gain_one)

    far_input, far_gain = leave(1 - chip)
    far_input = swap(far_input.astype(BF), "tensor", 2)
    near_input, near_gain = leave(chip)
    far_result_half, near_input = together(far_result_half, near_input)
    far_input = far_input.astype(F32)
    grad_input = jnp.where(
        chip == 0, jnp.stack([near_input, far_input]), jnp.stack([far_input, near_input])
    )

    result_pair = jnp.where(
        chip == 0,
        jnp.stack([result_half, far_result_half]),
        jnp.stack([far_result_half, result_half]),
    )
    other_pair = swap(result_pair, "tensor", 1)
    output = jnp.where(
        core == 0,
        jnp.concatenate([result_pair, other_pair], 1),
        jnp.concatenate([other_pair, result_pair], 1),
    ).astype(F32)

    w_gain_one = far_gain + near_gain
    w_gain_one = w_gain_one + swap(w_gain_one, "tensor", 1)
    gains = jnp.concatenate([w_gain_one, w_gain_two, w_gain_three, w_gain_four], 1)
    gains = clip_sum(gains + swap(gains, "tensor", 2))[0]
    totals_last = total_last.finish()
    totals_two = total_two.finish()
    totals_hidden_one = total_hidden.finish()

    two_heads = heads_in_two.shape[2] // HD
    sides = wide // width
    per_head = totals_two[: -sides * skip_rows].reshape(two_heads, -1, width)
    grad_heads_in_two = jnp.transpose(
        jnp.swapaxes(per_head[:, :heads_rows].reshape(two_heads, 3, HD, width), 0, 1).reshape(
            3, -1, width
        ),
        (2, 0, 1),
    ).astype(F32)
    grad_heads_in_one = jnp.transpose(
        totals_last[:heads_rows].reshape(3, HD, width), (2, 0, 1)
    ).astype(F32)

    def unfold(block):
        block = block.reshape(-1, sides, HD, width).astype(F32)
        return jnp.concatenate([block[:, k] for k in range(sides)], 2).reshape(-1, wide)

    return (
        output[:, None],
        grad_input[:, None],
        gains[:width],
        grad_heads_in_one,
        totals_last[heads_rows:].astype(F32),
        gains[width : 2 * width],
        jnp.transpose(totals_hidden_one[:width]).astype(F32),
        totals_hidden_one[width:].astype(F32),
        gains[2 * width : 3 * width],
        grad_heads_in_two,
        unfold(totals_two[-sides * skip_rows :]),
        unfold(per_head[:, heads_rows:]),
        gains[3 * width :],
        totals_hidden_two[0].astype(F32),
        totals_hidden_two[1].astype(F32),
    )


def solution(mesh):
    return jax.shard_map(
        per_device,
        mesh=mesh,
        in_specs=(
            P(None, "clip", None, None),
            P(),
            P(None, None, "tensor"),
            P("tensor", None),
            P(),
            P(None, "tensor"),
            P("tensor", None),
            P(),
            P(None, None, "tensor"),
            P("tensor", None),
            P("tensor", None),
            P(),
            P(None, "tensor"),
            P("tensor", None),
            P(),
            P(),
            P(None, "clip", None, None),
        ),
        out_specs=(
            P(None, "clip", None, None),
            P(None, "clip", "tensor", None),
            P(),
            P(None, None, "tensor"),
            P("tensor", None),
            P(),
            P(None, "tensor"),
            P("tensor", None),
            P(),
            P(None, None, "tensor"),
            P("tensor", None),
            P("tensor", None),
            P(),
            P(None, "tensor"),
            P("tensor", None),
        ),
        check_vma=False,
    )
```

```python
import functools

import jax
import jax.numpy as jnp
from jax import lax
from jax.experimental import pallas as pl
from jax.experimental.pallas import tpu as pltpu
from jax.sharding import PartitionSpec as P

HD = 96
PAD = 128
TOK_LOW = 1052
EPSILON = 1e-06
MASKED_SCORE = -1e30
LOG2E = 1.4426950408889634
LN2 = 0.6931471805599453
SCALING = HD ** (-0.5)
BF = jnp.bfloat16
F32 = jnp.float32
MIB = 2**20
LARGE_MIB = 44
SMALL_MIB = 44
GAIN_ROWS = 16
PIECE = 256
HIDDEN_SLABS = 2

NN = (((1,), (0,)), ((), ()))
NT = (((1,), (1,)), ((), ()))
TN = (((0,), (0,)), ((), ()))


def dot(left, right, form=NN):
    return lax.dot_general(left, right, form, preferred_element_type=F32)


def rms_factor(values):
    return lax.rsqrt(jnp.mean(values * values, -1, keepdims=True) + EPSILON)


def norm_grads(values, gain, grad):
    factor = rms_factor(values)
    scaled = values * factor
    term = grad * gain
    inner = jnp.mean(scaled * term, -1, keepdims=True)
    return factor * (term - scaled * inner), grad * scaled


def gelu_parts(values):
    root = 0.7978845608028654
    square = values * values
    tanh = jnp.tanh(values * (root + (root * 0.044715) * square))
    half = 0.5 + 0.5 * tanh
    slope = half + (0.5 * values) * (1.0 - tanh * tanh) * (root + (3 * root * 0.044715) * square)
    return values * half, slope


def gelu_only(values):
    root = 0.7978845608028654
    tanh = jnp.tanh(values * (root + (root * 0.044715) * (values * values)))
    return values * (0.5 + 0.5 * tanh)


def split_three(row):
    high = row.astype(BF).astype(F32)
    rest = row - high
    middle = rest.astype(BF).astype(F32)
    return high, middle, rest - middle


def call(body, name, grid, in_specs, out_specs, out_shape, scratch=(), prefetch=0, vmem=SMALL_MIB, us=1):
    return pl.pallas_call(
        body,
        name=name,
        grid_spec=pltpu.PrefetchScalarGridSpec(
            num_scalar_prefetch=prefetch,
            grid=grid,
            in_specs=in_specs,
            out_specs=out_specs,
            scratch_shapes=list(scratch),
        ),
        out_shape=out_shape,
        compiler_params=pltpu.CompilerParams(vmem_limit_bytes=vmem * MIB),
        cost_estimate=pl.CostEstimate(
            flops=int(us * 1.15e9), bytes_accessed=MIB // 4, transcendentals=0
        ),
    )


def whole(shape):
    return pl.BlockSpec(shape, lambda *_: (0,) * len(shape))


def shape_of(shape, dtype):
    return jax.ShapeDtypeStruct(shape, dtype)


def lane_scratch(rows, width):
    return pltpu.VMEM((width // PAD, rows, PAD), F32)


def slabs_of(block, lanes):
    parts = lanes.shape[0]
    rows = block.shape[0] // 4
    for part in range(parts):
        lanes[part] = block[:, part * PAD : (part + 1) * PAD]
    return [
        jnp.concatenate([lanes[part, pl.ds(s, rows, stride=4), :] for part in range(parts)], 1)
        for s in range(4)
    ]


def half_rows(core, half):
    return pl.ds(pl.multiple_of(core * half, half), half)


def half_block(rows, width, steps):
    per_half = steps // 2

    def place(step, _, core):
        return jnp.clip(step - per_half * core[0], 0, per_half - 1), 0

    return pl.BlockSpec((rows // steps, width), place)


def keep_half(core, step, steps, target, block):
    @pl.when(step // (steps // 2) == core[0])
    def _():
        target[...] = block


def entry_body(_, core, x_ref, gain_ref, normed_ref, pooled_ref, half_ref, lanes):
    total = None
    slabs = slabs_of(x_ref[0, 0], lanes)
    for slab in range(4):
        values = slabs[slab]
        normed = (values * rms_factor(values) * gain_ref[...]).astype(BF)
        normed_ref[slab] = normed
        part = normed.astype(F32)
        total = part if total is None else total + part
    pooled = (total * 0.25).astype(BF)
    pooled_ref[...] = pooled
    keep_half(core, pl.program_id(0), 4, half_ref, pooled)


def entry_norm(micro, core, tokens, gain):
    length, width = tokens.shape[2:]
    rows = length // 4
    block = rows // 4
    return call(
        entry_body,
        "entry_norm",
        (4,),
        [
            pl.BlockSpec((1, 1, 4 * block, width), lambda i, m, c: (m[0], 0, i, 0)),
            whole((1, width)),
        ],
        [
            pl.BlockSpec((4, block, width), lambda i, *_: (0, i, 0)),
            pl.BlockSpec((block, width), lambda i, *_: (i, 0)),
            half_block(rows, width, 4),
        ],
        [
            shape_of((4, rows, width), BF),
            shape_of((rows, width), BF),
            shape_of((rows // 2, width), BF),
        ],
        scratch=[lane_scratch(4 * block, width)],
        prefetch=2,
        vmem=LARGE_MIB,
        us=4,
    )(micro, core, tokens, gain.reshape(1, -1))


def make_pair(limit, offset, source, weights):
    rows = source.shape[0]
    place = lax.broadcasted_iota(jnp.int32, (rows, 1), 0) * 4 + offset
    lane = lax.broadcasted_iota(jnp.int32, (rows, PAD), 1)
    bias = jnp.where(place < limit, 0.0, MASKED_SCORE)
    both = dot(source, weights[PAD:], NT)
    keys = jnp.where(lane < HD, both[:, :PAD], jnp.where(lane == HD, bias, 1.0))
    values = jnp.where(lane < HD, both[:, PAD:], 1.0)
    turned = dot(weights[PAD:], source, NT)
    tail = jnp.ones((PAD - HD, rows), F32)
    values_t = jnp.concatenate([turned[PAD : PAD + HD], tail], 0)
    return keys.astype(BF), values.astype(BF), turned[:HD].astype(BF), values_t.astype(BF)


def own_pairs_body(limits, normed, weights, *results):
    for head in range(weights.shape[0]):
        parts = make_pair(limits[0], pl.program_id(0), normed[0], weights[head])
        for result, part in zip(results, parts):
            result[head, 0] = part


def pair_shapes(rows):
    return [(rows, PAD), (rows, PAD), (HD, rows), (PAD, rows)]


def own_pairs(limits, normed, weights):
    _, rows, width = normed.shape
    heads = weights.shape[0]
    return call(
        own_pairs_body,
        "own_pairs",
        (4,),
        [pl.BlockSpec((1, rows, width), lambda i, _: (i, 0, 0)), whole(weights.shape)],
        [
            pl.BlockSpec((heads, 1) + shape, lambda i, _: (0, i, 0, 0))
            for shape in pair_shapes(rows)
        ],
        [shape_of((heads, 4) + shape, BF) for shape in pair_shapes(rows)],
        prefetch=1,
        us=6,
    )(limits, normed, weights)


def query_tail(rows, parts):
    index = lax.broadcasted_iota(jnp.int32, (PAD - HD, rows), 0)
    tail = jnp.where(index == 0, 1.0, 0.0)
    for step, part in enumerate(parts):
        tail = jnp.where(index == step + 1, -part, tail)
    return tail.astype(BF)


def ask(source, weights):
    query = (dot(weights[:HD], source, NT) * (SCALING * LOG2E)).astype(BF)
    return query, jnp.concatenate([query, query_tail(query.shape[1], ())], 0)


def score_rows(asked, keys):
    parts = range(asked.shape[1] // PIECE)
    return [
        dot(keys(chunk)[part * PIECE : (part + 1) * PIECE], asked)
        for chunk in range(5)
        for part in parts
    ]


def attend_rows(query, scores, values_t):
    rows = query.shape[1]
    parts = rows // PIECE
    top = functools.reduce(jnp.maximum, [jnp.max(item, 0, keepdims=True) for item in scores])
    result = None
    for index, item in enumerate(scores):
        raised = jnp.exp2(item - top).astype(BF)
        part = index % parts
        term = dot(values_t(index // parts)[:, part * PIECE : (part + 1) * PIECE], raised)
        result = term if result is None else result + term
    summed = result[HD : HD + 1]
    heads = (result[:HD] / summed).astype(BF)
    logsum = top + jnp.log2(summed)
    return heads, jnp.concatenate([query, query_tail(rows, split_three(logsum))], 0)


def chosen(own, memory, head):
    return lambda chunk: own[head, chunk] if chunk < 4 else memory[head]


def join_halves(core, mine, theirs, target):
    half = mine.shape[0]
    target[half_rows(core, half)] = mine[...]
    target[half_rows(1 - core, half)] = theirs[...]


def attend_one_body(
    limits, normed, mine, theirs, weights, out_weights, own_keys, own_values_t,
    memory, keys, values, keys_t, queries_t, heads_t, partial, values_t,
):
    @pl.when(pl.program_id(0) == 0)
    def _():
        join_halves(limits[2], mine, theirs, memory)
        for head in range(2):
            parts = make_pair(limits[1], 0, memory[...], weights[head])
            keys[head], values[head], keys_t[head], values_t[head] = parts

    total = None
    queries = [ask(normed[0], weights[head]) for head in range(2)]
    scores = [score_rows(queries[head][1], chosen(own_keys, keys, head)) for head in range(2)]
    for head in range(2):
        heads, asked = attend_rows(
            queries[head][0], scores[head], chosen(own_values_t, values_t, head)
        )
        heads_t[head] = heads
        queries_t[head] = asked
        term = dot(heads, out_weights[head], TN)
        total = term if total is None else total + term
    partial[0] = total.astype(BF)


def attend_one(limits, normed, mine, theirs, weights, out_weights, own_keys, own_values_t):
    _, rows, width = normed.shape
    heads = weights.shape[0]
    memory_shapes = [(heads,) + shape for shape in pair_shapes(rows)]
    return call(
        attend_one_body,
        "attend_one",
        (4,),
        [
            pl.BlockSpec((1, rows, width), lambda i, _: (i, 0, 0)),
            whole(mine.shape),
            whole(theirs.shape),
            whole(weights.shape),
            whole(out_weights.shape),
            whole(own_keys.shape),
            whole(own_values_t.shape),
        ],
        [whole((rows, width))]
        + [whole(shape) for shape in memory_shapes[:3]]
        + [
            pl.BlockSpec((heads, PAD, rows), lambda i, _: (0, 0, i)),
            pl.BlockSpec((heads, HD, rows), lambda i, _: (0, 0, i)),
            pl.BlockSpec((1, rows, width), lambda i, _: (i, 0, 0)),
        ],
        [shape_of((rows, width), BF)]
        + [shape_of(shape, BF) for shape in memory_shapes[:3]]
        + [
            shape_of((heads, PAD, 4 * rows), BF),
            shape_of((heads, HD, 4 * rows), BF),
            shape_of((4, rows, width), BF),
        ],
        scratch=[pltpu.VMEM(memory_shapes[3], BF)],
        prefetch=1,
        vmem=LARGE_MIB,
        us=22,
    )(limits, normed, mine, theirs, weights, out_weights, own_keys, own_values_t)


def attend_two_body(
    limits, mine, theirs, pooled, weights, out_weights, skip, own_keys, own_values_t,
    memory, keys, values, keys_t, queries_t, heads_t, partial, values_t, total,
):
    step = pl.program_id(0)

    @pl.when(step == 0)
    def _():
        join_halves(limits[2], mine, theirs, memory)
        total[...] = dot(pooled[...], skip[...])

    here = range(weights.shape[0])
    queries = [ask(pooled[...], weights[head]) for head in here]
    for head in here:
        keys[head], values[head], keys_t[head], values_t[head] = make_pair(
            limits[1], 0, memory[...], weights[head]
        )
    scores = [score_rows(queries[head][1], chosen(own_keys, keys, head)) for head in here]
    for head in here:
        heads, asked = attend_rows(
            queries[head][0], scores[head], chosen(own_values_t, values_t, head)
        )
        heads_t[head] = heads
        queries_t[head] = asked
        total[...] += dot(heads, out_weights[head], TN)

    @pl.when(step == pl.num_programs(0) - 1)
    def _():
        partial[...] = total[...].astype(BF)


def attend_two(limits, mine, theirs, pooled, weights, out_weights, skip, own_keys, own_values_t):
    rows, width = pooled.shape
    heads = weights.shape[0]
    wide = out_weights.shape[2]

    def each(*shape):
        return pl.BlockSpec((2,) + shape, lambda h, _: (h,) + (0,) * len(shape))

    results = pair_shapes(rows)[:3] + [(PAD, rows), (HD, rows)]
    return call(
        attend_two_body,
        "attend_two",
        (heads // 2,),
        [
            whole(mine.shape),
            whole(theirs.shape),
            whole((rows, width)),
            each(*weights.shape[1:]),
            each(HD, wide),
            whole(skip.shape),
            each(4, rows, PAD),
            each(4, PAD, rows),
        ],
        [whole((rows, width))] + [each(*shape) for shape in results] + [whole((rows, wide))],
        [shape_of((rows, width), BF)]
        + [shape_of((heads,) + shape, BF) for shape in results]
        + [shape_of((rows, wide), BF)],
        scratch=[pltpu.VMEM((2, PAD, rows), BF), pltpu.VMEM((rows, wide), F32)],
        prefetch=1,
        vmem=LARGE_MIB,
        us=16,
    )(limits, mine, theirs, pooled, weights, out_weights, skip, own_keys, own_values_t)


def grad_chunk(keys, values, keys_t, asked, given):
    chances = jnp.exp2(dot(keys, asked))
    spread = dot(values, given)
    grad_scores = (chances * spread).astype(BF)
    grad_values = dot(chances.astype(BF), given, NT)
    grad_keys = dot(grad_scores, asked, NT)
    return grad_keys, grad_values, dot(keys_t, grad_scores)


def given_rows(out_weights, grad, heads):
    back = dot(out_weights, grad, NT).astype(BF)
    inner = jnp.sum(back.astype(F32) * heads.astype(F32), 0, keepdims=True)
    high, middle, low = split_three(inner)
    index = lax.broadcasted_iota(jnp.int32, (PAD - HD, grad.shape[0]), 0)
    tail = jnp.where(index == 0, -high, jnp.where(index == 1, -middle, jnp.where(index == 2, -low, 0.0)))
    return jnp.concatenate([back, tail.astype(BF)], 0)


def pair_of(grad_keys, grad_values):
    return jnp.concatenate([(grad_keys * LN2).astype(BF), grad_values.astype(BF)], 1)


def plus(total, term):
    return term if total is None else total + term


class Kept:
    def __init__(self, refs, head):
        own_keys, own_values, own_keys_t, keys, values, keys_t, self.queries, self.heads = refs
        self.keys = chosen(own_keys, keys, head)
        self.values = chosen(own_values, values, head)
        self.keys_t = chosen(own_keys_t, keys_t, head)
        self.head = head

    def grads(self, chunk, given):
        return grad_chunk(
            self.keys(chunk), self.values(chunk), self.keys_t(chunk), self.queries[self.head], given
        )

    def given(self, out_weights, branch):
        return given_rows(out_weights[self.head], branch, self.heads[self.head])


def put_head(target, head, heads, grad_query, grad_pair, columns):
    width = target.shape[1]
    parts = [grad_query, grad_pair[:HD], grad_pair[PAD : PAD + HD]]
    sides = [columns[:, side : side + width] for side in range(0, columns.shape[1], width)]
    starts = [(index * heads + head) * HD for index in range(3)]
    starts += [(3 * heads + head * len(sides) + index) * HD for index in range(len(sides))]
    for start, part in zip(starts, parts + sides):
        target[pl.ds(pl.multiple_of(start, 32), HD)] = part.astype(BF)


def put_skip(target, start, columns, share):
    width = target.shape[1]
    for index, side in enumerate(range(0, columns.shape[1], width)):
        rows = columns[pl.ds(pl.multiple_of(share * HD, 32), HD), side : side + width]
        target[start + index * HD : start + (index + 1) * HD] = rows


def two_first_body(
    place, after, mine, theirs, cotangent, gain, normed, memory, pooled, weights, out_weights, skip,
    *refs
):
    kept, results, scratch = Kept(refs[:8], 0), refs[8:18], refs[18:]
    (branch, grad_gain, own_skip, grad_rows, grad_pool, memory_mine, memory_theirs, grad_weights,
     query_memory, pair_memory) = results
    total, columns = scratch
    step = pl.program_id(0)
    core, share = place[1], place[2]
    wide = after.shape[1]
    width = pooled.shape[1]
    sides = wide // width
    head_rows = (3 + sides) * HD

    @pl.when(step == 0)
    def _():
        first = jnp.where(core == 0, mine[...], theirs[...]).astype(F32)
        second = jnp.where(core == 0, theirs[...], mine[...]).astype(F32)
        arrived = jnp.concatenate([first, second], 0)
        back, terms = norm_grads(after[...], gain[...], arrived)
        grad_gain[...] = jnp.sum(terms, 0, keepdims=True)
        branch[...] = (cotangent[0, 0] + back).astype(BF)
        columns[...] = dot(pooled[...], branch[...], TN).astype(BF)
        put_skip(grad_weights, 2 * head_rows, columns, share ^ 2)
        put_skip(own_skip, 0, columns, share)
        grad_pool[...] = dot(branch[...], skip[...], NT)
        total[...] = jnp.zeros_like(total)

    given = kept.given(out_weights, branch[...])

    @pl.when(step < 2)
    def _():
        grad_query, grad_pair = None, None
        for chunk in range(5):
            grad_keys, grad_values, term = kept.grads(chunk, given)
            grad_query = plus(grad_query, term)
            pair = pair_of(grad_keys, grad_values)
            total[chunk] += dot(pair, weights[0, PAD:])
            source = normed[chunk] if chunk < 4 else memory[...]
            grad_pair = plus(grad_pair, dot(pair, source, TN))
        grad_query = (grad_query * SCALING).astype(BF)
        grad_pool[...] += dot(grad_query, weights[0, :HD], TN)
        put_head(
            grad_weights, step, 2, dot(grad_query, pooled[...]), grad_pair,
            dot(kept.heads[0], branch[...]),
        )

    @pl.when(step >= 2)
    def _():
        grad_keys, grad_values, term = kept.grads(4, given)
        query_memory[0] = term
        pair = pair_of(grad_keys, grad_values)
        total[4] += dot(pair, weights[0, PAD:])
        pair_memory[0] = dot(pair, memory[...], TN)

    @pl.when(step == 3)
    def _():
        half = memory_mine.shape[0]
        for chunk in range(4):
            grad_rows[chunk] = total[chunk].astype(BF)
        memory_mine[...] = total[4, half_rows(core, half)].astype(BF)
        memory_theirs[...] = total[4, half_rows(1 - core, half)].astype(BF)


def two_second_body(
    branch, normed, pooled, weights, out_weights, earlier_rows, earlier_pool, query_memory,
    pair_memory, own_skip, *refs
):
    kept, (grad_rows, grad_weights, total, total_pool) = Kept(refs[:8], 0), refs[8:]
    step = pl.program_id(0)
    head_rows = (grad_weights.shape[0] - own_skip.shape[0]) // 2

    @pl.when(step == 0)
    def _():
        grad_weights[2 * head_rows :] = own_skip[...]
        total_pool[...] = earlier_pool[...]
        for chunk in range(4):
            total[chunk] = earlier_rows[chunk].astype(F32)

    given = kept.given(out_weights, branch[...])
    grad_query, grad_pair = query_memory[0], pair_memory[0]
    for chunk in range(4):
        grad_keys, grad_values, term = kept.grads(chunk, given)
        grad_query = grad_query + term
        pair = pair_of(grad_keys, grad_values)
        total[chunk] += dot(pair, weights[0, PAD:])
        grad_pair = grad_pair + dot(pair, normed[chunk], TN)
    grad_query = (grad_query * SCALING).astype(BF)
    total_pool[...] += dot(grad_query, weights[0, :HD], TN)
    put_head(
        grad_weights, step, 2, dot(grad_query, pooled[...]), grad_pair,
        dot(kept.heads[0], branch[...]),
    )

    @pl.when(step == pl.num_programs(0) - 1)
    def _():
        for chunk in range(4):
            grad_rows[chunk] = (total[chunk] + 0.25 * total_pool[...]).astype(BF)


def kept_specs(each, rows, own=None):
    pair = pair_shapes(rows)[:3]
    return [(own or each)(4, *shape) for shape in pair] + [each(*shape) for shape in pair]


def two_first(
    place, after, mine, theirs, cotangent, gain, normed, memory, pooled, weights, out_weights, skip, kept
):
    _, rows, width = normed.shape
    wide = out_weights.shape[2]
    sides = wide // width
    all_rows = 2 * (3 + sides) * HD + sides * HD

    def each(*shape):
        return pl.BlockSpec((1,) + shape, lambda h, _: ((h + 2) % 4,) + (0,) * len(shape))

    def own(*shape):
        return pl.BlockSpec((1,) + shape, lambda h, _: (jnp.minimum(h, 1) + 2,) + (0,) * len(shape))

    def late(*shape):
        return pl.BlockSpec((1,) + shape, lambda h, _: (jnp.maximum(h, 2) - 2,) + (0,) * len(shape))

    return call(
        two_first_body,
        "back_two_first",
        (4,),
        [
            whole((rows, wide)),
            whole(mine.shape),
            whole(theirs.shape),
            pl.BlockSpec((1, 1, rows, wide), lambda h, m: (m[0], 0, 0, 0)),
            whole((1, wide)),
            whole((4, rows, width)),
            whole((rows, width)),
            whole((rows, width)),
            each(*weights.shape[1:]),
            each(HD, wide),
            whole(skip.shape),
        ]
        + kept_specs(each, rows, own)
        + [each(PAD, rows), each(HD, rows)],
        [
            whole((rows, wide)),
            whole((1, wide)),
            whole((sides * HD, width)),
            whole((4, rows, width)),
            whole((rows, width)),
            whole((rows // 2, width)),
            whole((rows // 2, width)),
            whole((all_rows, width)),
            late(HD, rows),
            late(2 * PAD, width),
        ],
        [
            shape_of((rows, wide), BF),
            shape_of((1, wide), F32),
            shape_of((sides * HD, width), BF),
            shape_of((4, rows, width), BF),
            shape_of((rows, width), F32),
            shape_of((rows // 2, width), BF),
            shape_of((rows // 2, width), BF),
            shape_of((all_rows, width), BF),
            shape_of((2, HD, rows), F32),
            shape_of((2, 2 * PAD, width), F32),
        ],
        scratch=[pltpu.VMEM((5, rows, width), F32), pltpu.VMEM((width, wide), BF)],
        prefetch=1,
        vmem=LARGE_MIB,
        us=23,
    )(
        place, after, mine, theirs, cotangent, gain.reshape(1, -1), normed, memory, pooled, weights,
        out_weights, skip, *kept,
    )


def two_second(
    branch, normed, pooled, weights, out_weights, earlier_rows, earlier_pool, query_memory,
    pair_memory, own_skip, kept
):
    _, rows, width = normed.shape
    wide = out_weights.shape[2]
    all_rows = 2 * (3 + wide // width) * HD + own_skip.shape[0]

    def each(*shape):
        return pl.BlockSpec((1,) + shape, lambda h: (h,) + (0,) * len(shape))

    return call(
        two_second_body,
        "back_two_second",
        (2,),
        [
            whole((rows, wide)),
            whole((4, rows, width)),
            whole((rows, width)),
            each(*weights.shape[1:]),
            each(HD, wide),
            whole((4, rows, width)),
            whole((rows, width)),
            each(HD, rows),
            each(2 * PAD, width),
            whole(own_skip.shape),
        ]
        + kept_specs(each, rows)
        + [each(PAD, rows), each(HD, rows)],
        [whole((4, rows, width)), whole((all_rows, width))],
        [shape_of((4, rows, width), BF), shape_of((all_rows, width), BF)],
        scratch=[pltpu.VMEM((4, rows, width), F32), pltpu.VMEM((rows, width), F32)],
        vmem=LARGE_MIB,
        us=14,
    )(
        branch, normed, pooled, weights, out_weights, earlier_rows, earlier_pool, query_memory,
        pair_memory, own_skip, *kept,
    )


def one_first_body(
    core, grad_two, after, own_part, other_part, gain, normed, memory, weights, out_weights, *refs
):
    kept, near_kept = Kept(refs[:8], 1), Kept(refs[:8], 0)
    (grad_one, branch_ref, grad_gain, grad_rows, memory_mine, memory_theirs, grad_weights,
     query_memory, pair_memory, memory_gain) = refs[8:18]
    total, total_keys, total_values, total_query, total_out, near_keys, near_values, rows_memory = (
        refs[18:]
    )
    slab = pl.program_id(0)

    @pl.when(slab == 0)
    def _():
        for item in (grad_gain, total_keys, total_values, total_query, total_out, near_keys, near_values):
            item[...] = jnp.zeros_like(item)

    arrived = own_part[0].astype(F32) + other_part[0].astype(F32)
    back, terms = norm_grads(after[0], gain[...], arrived)
    grad_gain[...] += jnp.sum(terms, 0, keepdims=True)
    state = grad_two[0] + back
    grad_one[0] = state
    branch = state.astype(BF)
    branch_ref[0] = branch
    given = kept.given(out_weights, branch)
    grad_query = None
    for chunk in range(5):
        grad_keys, grad_values, term = kept.grads(chunk, given)
        total_keys[chunk] += grad_keys
        total_values[chunk] += grad_values
        grad_query = plus(grad_query, term)
    grad_keys, grad_values, term = near_kept.grads(4, near_kept.given(out_weights, branch))
    near_keys[...] += grad_keys
    near_values[...] += grad_values
    query_memory[...] = term
    grad_query = (grad_query * SCALING).astype(BF)
    total_out[...] += dot(kept.heads[1], branch)
    total_query[...] += dot(grad_query, normed[slab])
    total[slab] = dot(grad_query, weights[1, :HD], TN)

    @pl.when(slab == pl.num_programs(0) - 1)
    def _():
        pair = pair_of(near_keys[...], near_values[...])
        pair_memory[...] = dot(pair, memory[...], TN)
        near_rows = dot(pair, weights[0, PAD:])
        grad_pair = None
        for chunk in range(5):
            pair = pair_of(total_keys[chunk], total_values[chunk])
            rows = dot(pair, weights[1, PAD:])
            source = normed[chunk] if chunk < 4 else memory[...]
            grad_pair = plus(grad_pair, dot(pair, source, TN))
            if chunk < 4:
                grad_rows[chunk] = (total[chunk] + rows).astype(BF)
            else:
                rows = near_rows + rows
                memory_gain[...] = jnp.sum(rows * memory[...].astype(F32), 0, keepdims=True)
                rows_memory[...] = rows
        half = memory_mine.shape[0]
        memory_mine[...] = rows_memory[half_rows(core[0], half)].astype(BF)
        memory_theirs[...] = rows_memory[half_rows(1 - core[0], half)].astype(BF)
        grad_weights[:HD] = total_query[...].astype(BF)
        grad_weights[HD : 2 * HD] = grad_pair[:HD].astype(BF)
        grad_weights[2 * HD : 3 * HD] = grad_pair[PAD : PAD + HD].astype(BF)
        grad_weights[3 * HD : 4 * HD] = total_out[...].astype(BF)
        grad_weights[4 * HD :] = jnp.zeros_like(grad_weights[4 * HD :])


def one_second_body(
    core, branch_ref, normed, weights, out_weights, earlier_rows, query_memory, pair_memory,
    memory_gain, gain, other_gains, *refs
):
    kept, (mine, theirs, grad_weights) = Kept(refs[:8], 0), refs[8:11]
    total, total_keys, total_values, total_query, total_out = refs[11:]
    slab = pl.program_id(0)

    @pl.when(slab == 0)
    def _():
        for item in (total_keys, total_values, total_query, total_out):
            item[...] = jnp.zeros_like(item)

    branch = branch_ref[0]
    given = kept.given(out_weights, branch)
    grad_query = query_memory[...]
    for chunk in range(4):
        grad_keys, grad_values, term = kept.grads(chunk, given)
        total_keys[chunk] += grad_keys
        total_values[chunk] += grad_values
        grad_query = grad_query + term
    grad_query = (grad_query * SCALING).astype(BF)
    total_out[...] += dot(kept.heads[0], branch)
    total_query[...] += dot(grad_query, normed[slab])
    total[slab] = dot(grad_query, weights[0, :HD], TN)

    @pl.when(slab == pl.num_programs(0) - 1)
    def _():
        grad_pair = pair_memory[...]
        gain_terms = memory_gain[...]
        share = mine.shape[2]
        for chunk in range(4):
            pair = pair_of(total_keys[chunk], total_values[chunk])
            rows = dot(pair, weights[0, PAD:]) + earlier_rows[chunk].astype(F32)
            rows = total[chunk] + rows
            gain_terms += jnp.sum(rows * normed[chunk].astype(F32), 0, keepdims=True)
            total[chunk] = rows
            for chip in range(mine.shape[1]):
                for target, which in ((mine, core[0]), (theirs, 1 - core[0])):
                    start = pl.multiple_of((2 * chip + which) * share, share)
                    target[chunk, chip] = total[chunk, pl.ds(start, share)].astype(BF)
            grad_pair = grad_pair + dot(pair, normed[chunk], TN)
        gains = jnp.concatenate([gain_terms / gain[...], other_gains[1:]], 0)
        grad_weights[4 * HD :] = gains.astype(BF)
        grad_weights[:HD] = total_query[...].astype(BF)
        grad_weights[HD : 2 * HD] = grad_pair[:HD].astype(BF)
        grad_weights[2 * HD : 3 * HD] = grad_pair[PAD : PAD + HD].astype(BF)
        grad_weights[3 * HD : 4 * HD] = total_out[...].astype(BF)


def one_specs(rows):
    def heads(*shape):
        return whole((2,) + shape)

    return kept_specs(heads, rows) + [
        pl.BlockSpec((2, PAD, rows), lambda i, *_: (0, 0, i)),
        pl.BlockSpec((2, HD, rows), lambda i, *_: (0, 0, i)),
    ]


def one_scratch(rows, width, chunks):
    return [
        pltpu.VMEM((4, rows, width), F32),
        pltpu.VMEM((chunks, rows, PAD), F32),
        pltpu.VMEM((chunks, rows, PAD), F32),
        pltpu.VMEM((HD, width), F32),
        pltpu.VMEM((HD, width), F32),
    ]


def one_first(
    core, grad_two, after, own_part, other_part, gain, normed, memory, weights, out_weights, kept
):
    _, rows, width = grad_two.shape
    slab = pl.BlockSpec((1, rows, width), lambda i, *_: (i, 0, 0))
    return call(
        one_first_body,
        "back_one_first",
        (4,),
        [slab, slab, slab, slab, whole((1, width)), whole((4, rows, width)), whole((rows, width))]
        + [whole(weights.shape), whole(out_weights.shape)]
        + one_specs(rows),
        [
            slab,
            slab,
            whole((1, width)),
            whole((4, rows, width)),
            whole((rows // 2, width)),
            whole((rows // 2, width)),
            whole((4 * HD + GAIN_ROWS, width)),
            pl.BlockSpec((HD, rows), lambda i, *_: (0, i)),
            whole((2 * PAD, width)),
            whole((1, width)),
        ],
        [
            shape_of((4, rows, width), F32),
            shape_of((4, rows, width), BF),
            shape_of((1, width), F32),
            shape_of((4, rows, width), BF),
            shape_of((rows // 2, width), BF),
            shape_of((rows // 2, width), BF),
            shape_of((4 * HD + GAIN_ROWS, width), BF),
            shape_of((HD, 4 * rows), F32),
            shape_of((2 * PAD, width), F32),
            shape_of((1, width), F32),
        ],
        scratch=one_scratch(rows, width, 5)
        + [pltpu.VMEM((rows, PAD), F32), pltpu.VMEM((rows, PAD), F32), pltpu.VMEM((rows, width), F32)],
        prefetch=1,
        vmem=LARGE_MIB,
        us=27,
    )(
        core, grad_two, after, own_part, other_part, gain.reshape(1, -1), normed, memory, weights,
        out_weights, *kept,
    )


def one_second(
    core, branch, normed, weights, out_weights, earlier_rows, query_memory, pair_memory, memory_gain,
    gain, other_gains, kept
):
    _, rows, width = branch.shape
    slab = pl.BlockSpec((1, rows, width), lambda i, *_: (i, 0, 0))
    leaving = (4, 2, rows // 4, width)
    return call(
        one_second_body,
        "back_one_second",
        (4,),
        [
            slab,
            whole((4, rows, width)),
            whole(weights.shape),
            whole(out_weights.shape),
            whole((4, rows, width)),
            pl.BlockSpec((HD, rows), lambda i, *_: (0, i)),
            whole((2 * PAD, width)),
            whole((1, width)),
            whole((1, width)),
            whole(other_gains.shape),
        ]
        + one_specs(rows),
        [whole(leaving), whole(leaving), whole((4 * HD + other_gains.shape[0], width))],
        [
            shape_of(leaving, BF),
            shape_of(leaving, BF),
            shape_of((4 * HD + other_gains.shape[0], width), BF),
        ],
        scratch=one_scratch(rows, width, 4),
        prefetch=1,
        vmem=LARGE_MIB,
        us=18,
    )(
        core, branch, normed, weights, out_weights, earlier_rows, query_memory, pair_memory,
        memory_gain, gain.reshape(1, -1), other_gains, *kept,
    )


def flat(block):
    return block.reshape(block.shape[0] * block.shape[1], block.shape[2])


def hidden_one_body(_, x_ref, own_part, other_part, gain, w_in, w_out, after, partial, lanes):
    tokens = slabs_of(x_ref[0, 0], lanes)
    for pair in range(0, 4, HIDDEN_SLABS):
        slabs = slice(pair, pair + HIDDEN_SLABS)
        state = flat(own_part[slabs].astype(F32) + other_part[slabs].astype(F32))
        state = state + jnp.concatenate(tokens[slabs], 0)
        after[slabs] = state.reshape(HIDDEN_SLABS, -1, state.shape[1])
        normed = (state * rms_factor(state) * gain[...]).astype(BF)
        active = gelu_only(dot(normed, w_in[...], NT)).astype(BF)
        partial[slabs] = dot(active, w_out[...]).astype(BF).reshape(HIDDEN_SLABS, -1, state.shape[1])


def hidden_one(micro, tokens, own_part, other_part, gain, w_in, w_out):
    _, rows, width = own_part.shape
    block = rows // 4
    strip = pl.BlockSpec((4, block, width), lambda i, m: (0, i, 0))
    return call(
        hidden_one_body,
        "hidden_one",
        (4,),
        [
            pl.BlockSpec((1, 1, 4 * block, width), lambda i, m: (m[0], 0, i, 0)),
            strip,
            strip,
            whole((1, width)),
            whole(w_in.shape),
            whole(w_out.shape),
        ],
        [strip, strip],
        [shape_of((4, rows, width), F32), shape_of((4, rows, width), BF)],
        scratch=[lane_scratch(4 * block, width)],
        prefetch=1,
        vmem=LARGE_MIB,
        us=7,
    )(micro, tokens, own_part, other_part, gain.reshape(1, -1), w_in, w_out)


def norm_three_body(_, core, state, own_part, other_part, gain, after, normed, pooled_ref, half_ref):
    total = None
    for slab in range(4):
        values = state[slab] + (own_part[slab].astype(F32) + other_part[slab].astype(F32))
        after[slab] = values
        rows = (values * rms_factor(values) * gain[...]).astype(BF)
        normed[slab] = rows
        total = rows.astype(F32) if total is None else total + rows.astype(F32)
    pooled = (total * 0.25).astype(BF)
    pooled_ref[...] = pooled
    keep_half(core, pl.program_id(0), 4, half_ref, pooled)


def norm_three(micro, core, state, own_part, other_part, gain):
    _, rows, width = state.shape
    block = rows // 4
    strip = pl.BlockSpec((4, block, width), lambda i, *_: (0, i, 0))
    return call(
        norm_three_body,
        "norm_three",
        (4,),
        [strip, strip, strip, whole((1, width))],
        [
            strip,
            strip,
            pl.BlockSpec((block, width), lambda i, *_: (i, 0)),
            half_block(rows, width, 4),
        ],
        [
            shape_of((4, rows, width), F32),
            shape_of((4, rows, width), BF),
            shape_of((rows, width), BF),
            shape_of((rows // 2, width), BF),
        ],
        prefetch=2,
        us=5,
    )(micro, core, state, own_part, other_part, gain.reshape(1, -1))


def hidden_one_back_body(
    core, after_two, own_part, other_part, mine, theirs, gain_three, after_one, gain_two, w_in, w_out,
    grad_two, partial, grad_own, grad_sent, grad_gain, total_in, total_out,
):
    step = pl.program_id(0)

    @pl.when(step == 0)
    def _():
        total_in[...] = jnp.zeros_like(total_in)
        total_out[...] = jnp.zeros_like(total_out)
        grad_gain[...] = jnp.zeros_like(grad_gain)

    memory = jnp.where(step // 2 == core[0], mine[...], theirs[...]).astype(F32) * 0.25
    width = memory.shape[1]
    for pair in range(0, 4, HIDDEN_SLABS):
        slabs = slice(pair, pair + HIDDEN_SLABS)
        arrived = own_part[slabs].astype(F32) + other_part[slabs].astype(F32) + memory[None]
        back, terms = norm_grads(flat(after_two[slabs]), gain_three[...], flat(arrived))
        grad_gain[...] += jnp.sum(terms, 0, keepdims=True)
        grad_two[slabs] = back.reshape(HIDDEN_SLABS, -1, width)
        branch = back.astype(BF)
        state = flat(after_one[slabs])
        normed = (state * rms_factor(state) * gain_two[...]).astype(BF)
        active, slope = gelu_parts(dot(normed, w_in[...], NT))
        grad_pre = (slope * dot(branch, w_out[...], NT)).astype(BF)
        partial[slabs] = dot(grad_pre, w_in[...]).astype(BF).reshape(HIDDEN_SLABS, -1, width)
        total_out[...] += dot(active.astype(BF), branch, TN)
        total_in[...] += dot(grad_pre, normed, TN)

    @pl.when(step == pl.num_programs(0) - 1)
    def _():
        share = total_in.shape[0] // 2
        for target, start in ((grad_own, 0), (grad_sent, share)):
            target[:share] = jnp.transpose(total_in[start : start + share]).astype(BF)
            target[share:] = total_out[start : start + share].astype(BF)


def hidden_one_back(
    core, after_two, own_part, other_part, mine, theirs, gain_three, after_one, gain_two, w_in, w_out
):
    _, rows, width = after_two.shape
    block = rows // 4
    hidden = w_in.shape[0]
    strip = pl.BlockSpec((4, block, width), lambda i, *_: (0, i, 0))
    memory = pl.BlockSpec((block, width), lambda i, *_: (i % 2, 0))
    return call(
        hidden_one_back_body,
        "hidden_one_back",
        (4,),
        [
            strip,
            strip,
            strip,
            memory,
            memory,
            whole((1, width)),
            strip,
            whole((1, width)),
            whole(w_in.shape),
            whole(w_out.shape),
        ],
        [strip, strip, whole(w_in.shape), whole(w_out.shape), whole((1, width))],
        [
            shape_of((4, rows, width), F32),
            shape_of((4, rows, width), BF),
            shape_of(w_in.shape, BF),
            shape_of(w_out.shape, BF),
            shape_of((1, width), F32),
        ],
        scratch=[pltpu.VMEM((hidden, width), F32), pltpu.VMEM((hidden, width), F32)],
        prefetch=1,
        us=15,
    )(
        core, after_two, own_part, other_part, mine, theirs, gain_three.reshape(1, -1), after_one,
        gain_two.reshape(1, -1), w_in, w_out,
    )


def norm_four_body(core, own_part, other_part, gain, after, normed_ref, half_ref):
    state = own_part[...].astype(F32) + other_part[...].astype(F32)
    after[...] = state
    normed = (state * rms_factor(state) * gain[...]).astype(BF)
    normed_ref[...] = normed

    @pl.when(pl.program_id(0) == core[0])
    def _():
        half_ref[...] = normed


def norm_four(core, own_part, other_part, gain):
    rows, wide = own_part.shape
    half = rows // 2
    strip = pl.BlockSpec((half, wide), lambda i, _: (i, 0))
    return call(
        norm_four_body,
        "norm_four",
        (2,),
        [strip, strip, whole((1, wide))],
        [strip, strip, whole((half, wide))],
        [shape_of((rows, wide), F32), shape_of((rows, wide), BF), shape_of((half, wide), BF)],
        prefetch=1,
        us=2,
    )(core, own_part, other_part, gain.reshape(1, -1))


def hidden_two_body(
    place, first, second, cotangent, w_in, w_out,
    normed_ref, active_ref, grad_pre_ref, grad_mine, grad_theirs, result_mine, result_theirs,
):
    mine = pl.program_id(0) == place[1]
    normed = jnp.where(mine, first[...], second[...])
    normed_ref[...] = normed
    active, slope = gelu_parts(dot(normed, w_in[...]))
    active = active.astype(BF)
    grad_pre = (slope * dot(cotangent[0, 0].astype(BF), w_out[...], NT)).astype(BF)
    grad_normed = dot(grad_pre, w_in[...], NT).astype(BF)
    active_ref[...] = active
    grad_pre_ref[...] = grad_pre
    result = dot(active, w_out[...]).astype(BF)

    @pl.when(mine)
    def _():
        grad_mine[...] = grad_normed
        result_mine[...] = result

    @pl.when(jnp.logical_not(mine))
    def _():
        grad_theirs[...] = grad_normed
        result_theirs[...] = result


def hidden_two(place, first, second, cotangent, w_in, w_out):
    wide, hidden = w_in.shape
    rows = cotangent.shape[2]
    half = rows // 2
    given = pl.BlockSpec((half, wide), lambda i, p: (i if first is second else 0, 0))
    strip = pl.BlockSpec((half, wide), lambda i, p: (i, 0))
    strip_hidden = pl.BlockSpec((half, hidden), lambda i, p: (i, 0))
    return call(
        hidden_two_body,
        "hidden_two",
        (2,),
        [
            given,
            given,
            pl.BlockSpec((1, 1, half, wide), lambda i, p: (p[0], 0, i, 0)),
            whole(w_in.shape),
            whole(w_out.shape),
        ],
        [strip, strip_hidden, strip_hidden] + [whole((half, wide))] * 4,
        [shape_of((rows, wide), BF), shape_of((rows, hidden), BF), shape_of((rows, hidden), BF)]
        + [shape_of((half, wide), BF)] * 4,
        prefetch=1,
        us=5,
    )(place, first, second, cotangent, w_in, w_out)


def hidden_two_weights_body(
    _, own_normed, own_active, own_pre, other_normed, other_active, other_pre, own_cot, other_cot,
    grad_in, grad_out,
):
    grad_in[...] = (
        dot(own_normed[...], own_pre[...], TN) + dot(other_normed[...], other_pre[...], TN)
    ).astype(BF)
    grad_out[...] = (
        dot(own_active[...], own_cot[0, 0].astype(BF), TN)
        + dot(other_active[...], other_cot[0, 0].astype(BF), TN)
    ).astype(BF)


def hidden_two_weights(micros, own, other, cotangent):
    rows, wide = own[0].shape
    hidden = own[1].shape[1]
    parts = 3
    column = pl.BlockSpec((rows, wide // parts), lambda i, m: (0, i))
    column_hidden = pl.BlockSpec((rows, hidden // parts), lambda i, m: (0, i))
    return call(
        hidden_two_weights_body,
        "hidden_two_weights",
        (parts,),
        [
            column,
            column_hidden,
            whole((rows, hidden)),
            column,
            column_hidden,
            whole((rows, hidden)),
            pl.BlockSpec((1, 1, rows, wide), lambda i, m: (m[0], 0, 0, 0)),
            pl.BlockSpec((1, 1, rows, wide), lambda i, m: (m[1], 0, 0, 0)),
        ],
        [
            pl.BlockSpec((wide // parts, hidden), lambda i, m: (i, 0)),
            pl.BlockSpec((hidden // parts, wide), lambda i, m: (i, 0)),
        ],
        [shape_of((wide, hidden), BF), shape_of((hidden, wide), BF)],
        prefetch=1,
        us=5,
    )(micros, *own, *other, cotangent, cotangent)


def exit_body(place, x_ref, grad_one, partial, got, mine, theirs, gain, grad_input, lanes):
    block = mine.shape[0]
    slabs = slabs_of(x_ref[0, 0], lanes)
    memory = jnp.where(place[2] == place[3], mine[...], theirs[...]).astype(F32) * 0.25
    for slab in range(4):
        arrived = partial[slab, 0].astype(F32) + got[slab, 0].astype(F32) + memory
        back, _ = norm_grads(slabs[slab], gain[...], arrived)
        result = grad_one[slab] + back
        for part in range(lanes.shape[0]):
            lanes[part, pl.ds(slab, block, stride=4), :] = result[:, part * PAD : (part + 1) * PAD]
    for part in range(lanes.shape[0]):
        columns = lanes[part].astype(grad_input.dtype)
        grad_input[:, part * PAD : (part + 1) * PAD] = columns


def exit_norm(place, tokens, grad_one, partial, got, mine, theirs, gain, dtype):
    length, width = tokens.shape[2:]
    share = length // 4
    block = share // 4
    leaving = pl.BlockSpec((4, 1, block, width), lambda i, p: (0, p[2], 0, 0))
    memory = pl.BlockSpec((block, width), lambda i, p: (p[3], 0))
    return call(
        exit_body,
        "exit_norm",
        (1,),
        [
            pl.BlockSpec((1, 1, share, width), lambda i, p: (p[0], 0, p[1], 0)),
            pl.BlockSpec((4, block, width), lambda i, p: (0, p[1], 0)),
            leaving,
            leaving,
            memory,
            memory,
            whole((1, width)),
        ],
        whole((share, width)),
        shape_of((share, width), dtype),
        scratch=[lane_scratch(share, width)],
        prefetch=1,
        vmem=LARGE_MIB,
        us=4,
    )(place, tokens, grad_one, partial, got, mine, theirs, gain.reshape(1, -1))


def swap(block, axis, bit):
    return lax.ppermute(block, axis, [(i, i ^ bit) for i in range(lax.axis_size(axis))])


def shifted(block, distance):
    devices = lax.axis_size("clip")
    return lax.ppermute(block, "clip", [(i, (i + distance) % devices) for i in range(devices)])


def after(block, earlier):
    return lax.optimization_barrier((block, earlier))[0]


def in_order(core, mine, theirs):
    ordered = jnp.where(core == 0, jnp.stack([mine, theirs]), jnp.stack([theirs, mine]))
    return ordered.reshape((-1,) + mine.shape[1:])


def share_of(block, core):
    half = block.shape[0] // 2
    return lax.dynamic_slice_in_dim(block, core * half, half, 0)


def together(results, *others):
    return lax.optimization_barrier((results,) + others)


class ClipSum:
    def __init__(self, block, halvings=1):
        clips = lax.axis_size("clip")
        self.index = lax.axis_index("clip")
        steps = [2**k for k in range(clips.bit_length() - 1)]
        halved = steps[:halvings]
        self.todo = [("halve", step) for step in halved] + [("add", step) for step in steps[halvings:]]
        self.todo += [("join", step) for step in reversed(halved)]
        self.block = block
        self.send()

    @classmethod
    def resumed(cls, block, todo, got):
        self = cls.__new__(cls)
        self.index = lax.axis_index("clip")
        self.block, self.todo, self.got = block, list(todo), got
        return self

    def send(self):
        kind, step = self.todo[0]
        bit = self.index // step % 2
        sent = share_of(self.block, 1 - bit) if kind == "halve" else self.block
        self.got = swap(sent, "clip", step)

    def take(self):
        kind, step = self.todo.pop(0)
        bit = self.index // step % 2
        got, self.got = self.got, None
        if kind == "join":
            self.block = in_order(bit, self.block, got)
        else:
            kept = share_of(self.block, bit) if kind == "halve" else self.block
            self.block = plus_rounded(kept, got)

    def step(self):
        self.take()
        if self.todo:
            self.send()

def plus_rounded(own, got):
    return (own.astype(F32) + got.astype(F32)).astype(BF)


def pad_heads(turned):
    widths = [(0, 0)] * (turned.ndim - 2) + [(0, PAD - HD), (0, 0)]
    padded = jnp.pad(turned, widths)
    return padded.reshape(turned.shape[:-3] + (3 * PAD, turned.shape[-1]))


def per_device(
    tokens_in,
    gain_one,
    heads_in_one,
    heads_out_one,
    gain_two,
    hidden_in_one,
    hidden_out_one,
    gain_three,
    heads_in_two,
    skip_weight,
    heads_out_two,
    gain_four,
    hidden_in_two,
    hidden_out_two,
    resolution,
    continues,
    cotangent,
):
    clip_index = lax.axis_index("clip")
    part_index = lax.axis_index("tensor")
    chip, core = part_index // 2, part_index % 2
    micro = chip.astype(jnp.int32).reshape(1)
    core_index = core.astype(jnp.int32).reshape(1)
    length, width = tokens_in.shape[2:]
    rows = length // 4
    wide = heads_out_two.shape[1]

    own_res = resolution[chip, clip_index]
    prev_res = resolution[chip, jnp.maximum(clip_index - 1, 0)]
    carried = (continues[chip, clip_index] == 1) & (clip_index > 0)
    own_len = jnp.where(own_res == 1, length, TOK_LOW)
    prev_len = jnp.where(carried, jnp.where(prev_res == 1, length, TOK_LOW), 0)
    limits = jnp.stack([own_len, prev_len, core]).astype(jnp.int32)

    skip_rows = skip_weight.shape[0]
    heads_rows = 3 * HD
    own_one = jnp.concatenate(
        [jnp.transpose(heads_in_one, (1, 2, 0)).reshape(heads_rows, width), heads_out_one], 0
    )
    far_one = swap(own_one, "tensor", 2)
    own_hidden = jnp.stack([jnp.transpose(hidden_in_one), hidden_out_one])
    own_two = jnp.transpose(heads_in_two, (1, 2, 0)).reshape(3, -1, HD, width)
    own_two = jnp.swapaxes(own_two, 0, 1)

    normed_one, _, pooled_half = entry_norm(micro, core_index, tokens_in, gain_one)
    pooled_half, own_hidden, own_two, far_one = together(pooled_half, own_hidden, own_two, far_one)
    memory_mine = shifted(pooled_half, 1)
    far_hidden = swap(own_hidden, "tensor", 2)
    far_two = swap(own_two, "tensor", 2)
    both_one = jnp.stack([own_one, far_one])
    weights_one = pad_heads(both_one[:, :heads_rows].reshape(2, 3, HD, width))
    out_one = both_one[:, heads_rows:]
    *own_kept_one, own_values_t = own_pairs(limits, normed_one, weights_one)
    memory_mine, own_kept_one = together(memory_mine, own_kept_one)
    memory_theirs = swap(memory_mine, "tensor", 1)
    memory_one, *kept_one, attn_part = attend_one(
        limits, normed_one, memory_mine, memory_theirs, weights_one, out_one, own_kept_one[0],
        own_values_t,
    )
    kept_one = own_kept_one + kept_one
    attn_part, far_hidden, far_two = together(attn_part, far_hidden, far_two)
    w_in_one = jnp.concatenate([own_hidden[0], far_hidden[0]], 0)
    w_out_one = jnp.concatenate([own_hidden[1], far_hidden[1]], 0)
    weights_two = pad_heads(jnp.concatenate([own_two, far_two], 0))
    own_rows = jnp.concatenate([skip_weight, heads_out_two], 0)
    far_rows = swap(after(own_rows, far_two), "tensor", 2)
    after_one, ffn_part = hidden_one(
        micro, tokens_in, attn_part, swap(attn_part, "tensor", 1), gain_two, w_in_one, w_out_one
    )
    after_two, normed_three, pooled_three, pooled_half = norm_three(
        micro, core_index, after_one, ffn_part, swap(ffn_part, "tensor", 1), gain_three
    )
    pooled_half, far_rows = together(pooled_half, far_rows)
    out_two = jnp.concatenate([own_rows[skip_rows:], far_rows[skip_rows:]], 0).reshape(-1, HD, wide)
    skip = jnp.zeros((width, wide), BF)
    skip = lax.dynamic_update_slice(skip, own_rows[:skip_rows], (part_index * skip_rows, 0))
    skip = lax.dynamic_update_slice(skip, far_rows[:skip_rows], ((part_index ^ 2) * skip_rows, 0))

    memory_mine = shifted(pooled_half, 1)
    *own_kept_two, own_values_t = own_pairs(limits, normed_three, weights_two)
    memory_mine, own_kept_two = together(memory_mine, own_kept_two)
    memory_theirs = swap(memory_mine, "tensor", 1)
    memory_two, *kept_two, branch_part = attend_two(
        limits, memory_mine, memory_theirs, pooled_three, weights_two, out_two, skip,
        own_kept_two[0], own_values_t,
    )
    kept_two = own_kept_two + kept_two
    after_three, normed_four, normed_half = norm_four(
        core_index, branch_part, swap(branch_part, "tensor", 1), gain_four
    )
    far_mine = swap(normed_half, "tensor", 2)
    near_place = jnp.stack([chip, core]).astype(jnp.int32)
    far_place = jnp.stack([1 - chip, core]).astype(jnp.int32)
    *own_ffn, own_mine, own_theirs, result_mine, result_theirs = hidden_two(
        near_place, normed_four, normed_four, cotangent, hidden_in_two, hidden_out_two
    )
    far_mine, own_theirs = together(far_mine, own_theirs)
    far_theirs = swap(far_mine, "tensor", 1)
    own_got = swap(own_theirs, "tensor", 1)
    *far_ffn, far_grad_mine, far_grad_theirs, far_result_mine, far_result_theirs = hidden_two(
        far_place, far_mine, far_theirs, cotangent, hidden_in_two, hidden_out_two
    )
    far_sum = plus_rounded(far_grad_mine, swap(far_grad_theirs, "tensor", 1))
    far_sum = swap(far_sum, "tensor", 2)
    w_hidden_two = hidden_two_weights(
        jnp.concatenate([micro, 1 - micro]), own_ffn, far_ffn, cotangent
    )
    far_sum, own_got, w_hidden_two = together(far_sum, own_got, w_hidden_two)
    grad_mine = own_mine.astype(F32) + own_got.astype(F32) + far_sum.astype(F32)
    grad_mine = grad_mine.astype(BF)
    grad_theirs = swap(grad_mine, "tensor", 1)
    early_totals = lax.psum(tuple(w_hidden_two), "clip")
    sides = wide // width
    in_rows = heads_in_two.shape[2] * 3

    def turned(block):
        return jnp.transpose(block.reshape(3, -1, width), (2, 0, 1)).astype(F32)

    def unfold(block):
        block = block.reshape(-1, sides, HD, width).astype(F32)
        return jnp.concatenate([block[:, k] for k in range(sides)], 2).reshape(-1, wide)

    left = []

    def backward():
        place = jnp.stack([chip, core, part_index]).astype(jnp.int32)
        (branch_two, w_gain_four, w_skip, *early, memory_kept, memory_sent, w_two_sent, query_two,
         pair_two) = two_first(
            place, after_three, grad_mine, grad_theirs, cotangent, gain_four, normed_three,
            memory_two, pooled_three, weights_two, out_two, skip, kept_two,
        )
        memory_part = shifted(plus_rounded(memory_kept, swap(memory_sent, "tensor", 1)), -1)
        w_two_far = swap(w_two_sent, "tensor", 2)
        grad_rows_two, w_two = two_second(
            branch_two, normed_three, pooled_three, weights_two, out_two, *early, query_two,
            pair_two, w_skip, kept_two,
        )
        grad_rows_two, memory_part, w_two, w_two_far = together(
            grad_rows_two, memory_part, w_two, w_two_far
        )
        got_rows_two = swap(grad_rows_two, "tensor", 1)
        memory_theirs = swap(memory_part, "tensor", 1)
        total_two = ClipSum(plus_rounded(w_two, w_two_far))
        result_far = plus_rounded(far_result_mine, swap(far_result_theirs, "tensor", 1))
        result_far = swap(result_far, "tensor", 2)
        result_got = swap(result_theirs, "tensor", 1)

        grad_two, grad_part_two, w_hidden, w_hidden_sent, w_gain_three = hidden_one_back(
            core_index, after_two, grad_rows_two, got_rows_two, memory_part,
            memory_theirs, gain_three, after_one, gain_two, w_in_one, w_out_one,
        )
        grad_part_two, total_two.got, result_far, result_got, w_hidden, w_hidden_sent = together(
            grad_part_two, total_two.got, result_far, result_got, w_hidden, w_hidden_sent
        )
        total_two.step()
        w_hidden_far = swap(w_hidden_sent, "tensor", 2)
        result_half = result_mine.astype(F32) + result_got.astype(F32) + result_far.astype(F32)
        result_half = (result_half + share_of(after_three, core)).astype(BF)
        (grad_one, branch_one, w_gain_two, early_rows, memory_kept, memory_sent, w_last_sent,
         *memory_terms) = one_first(
            core_index, grad_two, after_one, grad_part_two, swap(grad_part_two, "tensor", 1),
            gain_two, normed_one, memory_one, weights_one, out_one, kept_one,
        )
        branch_one, total_two.got, w_hidden_far, w_last_sent = together(
            branch_one, total_two.got, w_hidden_far, w_last_sent
        )
        total_two.step()
        total_hidden = ClipSum(plus_rounded(w_hidden, w_hidden_far), 2)
        memory_last = shifted(plus_rounded(memory_kept, swap(memory_sent, "tensor", 1)), -1)
        w_last_far = swap(w_last_sent, "tensor", 2)
        far_result_half = swap(after(result_half, w_hidden_far), "tensor", 2)
        gains = jnp.concatenate([w_gain_two, w_gain_three, w_gain_four], 1).reshape(-1, width) * 0.5
        gains = jnp.pad(gains, ((1, GAIN_ROWS - 1 - gains.shape[0]), (0, 0)))
        leaving, leaving_sent, w_last = one_second(
            core_index, branch_one, normed_one, weights_one, out_one, early_rows, *memory_terms,
            gain_one, gains, kept_one,
        )
        (leaving, leaving_sent, memory_last, total_two.got, total_hidden.got, w_last, w_last_far,
         far_result_half) = together(
            leaving, leaving_sent, memory_last, total_two.got, total_hidden.got, w_last, w_last_far,
            far_result_half,
        )
        left[:] = [total_two.todo, total_hidden.todo]
        return (
            leaving, leaving_sent, memory_last, total_two.got, total_hidden.got, w_last, w_last_far,
            far_result_half, grad_one, total_two.block, total_hidden.block, result_half,
        )

    shapes = jax.eval_shape(backward)

    def absent():
        return tuple(jnp.zeros(item.shape, item.dtype) for item in shapes)

    results = lax.cond(own_len > 0, backward, absent)
    results, early_totals = together(results, early_totals)
    (leaving, leaving_sent, memory_last, got_two, got_hidden, w_last, w_last_far, far_result_half,
     grad_one, block_two, block_hidden, result_half) = results
    total_two = ClipSum.resumed(block_two, left[0], got_two)
    total_hidden = ClipSum.resumed(block_hidden, left[1], got_hidden)
    leaving_got = swap(leaving_sent, "tensor", 1)
    memory_theirs = swap(memory_last, "tensor", 1)
    total_last = ClipSum(plus_rounded(w_last, w_last_far))
    total_hidden.step()

    def leave(which, dtype):
        place = jnp.stack([chip, which * 2 + core, which, core]).astype(jnp.int32)
        return exit_norm(
            place, tokens_in, grad_one, leaving, leaving_got, memory_last, memory_theirs, gain_one,
            dtype,
        )

    def move_on(beside_it, *sums):
        sums = [item for item in sums if item.todo]
        beside_it, *arrived = together(beside_it, *[item.got for item in sums])
        for item, got in zip(sums, arrived):
            item.got = got
            item.step()
        return beside_it

    far_input = move_on(leave(1 - chip, BF), total_last, total_hidden, total_two)
    far_input = swap(far_input, "tensor", 2)
    near_input = move_on(leave(chip, F32), total_last, total_hidden)
    far_input = move_on(far_input, total_last, total_hidden, total_two)
    while total_two.todo:
        far_input = move_on(far_input, total_two)
    totals_two = total_two.block
    grad_heads_in_two = turned(totals_two[:in_rows])
    grad_rows = unfold(totals_two[in_rows:])
    far_input = far_input.astype(F32)
    grad_input = jnp.where(
        chip == 0, jnp.stack([near_input, far_input]), jnp.stack([far_input, near_input])
    )
    result_pair = jnp.where(
        chip == 0,
        jnp.stack([result_half, far_result_half]),
        jnp.stack([far_result_half, result_half]),
    )
    other_pair = swap(result_pair, "tensor", 1)
    output = jnp.where(
        core == 0,
        jnp.concatenate([result_pair, other_pair], 1),
        jnp.concatenate([other_pair, result_pair], 1),
    ).astype(F32)
    early = [item.astype(F32) for item in early_totals]
    output, grad_input, grad_heads_in_two, grad_rows, early = move_on(
        (output, grad_input, grad_heads_in_two, grad_rows, early), total_last, total_hidden
    )
    while total_last.todo or total_hidden.todo:
        output = move_on(output, total_last, total_hidden)
    totals_last, totals_hidden_one = total_last.block, total_hidden.block
    gains = totals_last[4 * HD :].astype(F32)
    gains = gains + swap(gains, "tensor", 1)
    gains = (gains + swap(gains, "tensor", 2)).reshape(-1)
    return (
        output[:, None],
        grad_input[:, None],
        gains[:width],
        turned(totals_last[:heads_rows]),
        totals_last[heads_rows : 4 * HD].astype(F32),
        gains[width : 2 * width],
        totals_hidden_one[:width].astype(F32),
        totals_hidden_one[width:].astype(F32),
        gains[2 * width : 3 * width],
        grad_heads_in_two,
        grad_rows[-skip_rows:],
        grad_rows[:-skip_rows],
        gains[3 * width : 3 * width + wide],
        *early,
    )

def solution(mesh):
    return jax.shard_map(
        per_device,
        mesh=mesh,
        in_specs=(
            P(None, "clip", None, None),
            P(),
            P(None, None, "tensor"),
            P("tensor", None),
            P(),
            P(None, "tensor"),
            P("tensor", None),
            P(),
            P(None, None, "tensor"),
            P("tensor", None),
            P("tensor", None),
            P(),
            P(None, "tensor"),
            P("tensor", None),
            P(),
            P(),
            P(None, "clip", None, None),
        ),
        out_specs=(
            P(None, "clip", None, None),
            P(None, "clip", "tensor", None),
            P(),
            P(None, None, "tensor"),
            P("tensor", None),
            P(),
            P(None, "tensor"),
            P("tensor", None),
            P(),
            P(None, None, "tensor"),
            P("tensor", None),
            P("tensor", None),
            P(),
            P(None, "tensor"),
            P("tensor", None),
        ),
        check_vma=False,
    )
```

```python
import functools

import jax
import jax.numpy as jnp
from jax import lax
from jax.experimental import pallas as pl
from jax.experimental.pallas import tpu as pltpu
from jax.sharding import PartitionSpec as P

HD = 96
PAD = 128
TOK_LOW = 1052
EPSILON = 1e-06
MASKED_SCORE = -1e30
LOG2E = 1.4426950408889634
LN2 = 0.6931471805599453
SCALING = HD ** (-0.5)
BF = jnp.bfloat16
F32 = jnp.float32
MIB = 2**20
LARGE_MIB = 44
SMALL_MIB = 44
FFN_MIB = 20
COST = 1.0
GAIN_ROWS = 16
PIECE = 256
HIDDEN_SLABS = 2

NN = (((1,), (0,)), ((), ()))
NT = (((1,), (1,)), ((), ()))
TN = (((0,), (0,)), ((), ()))


def dot(left, right, form=NN):
    return lax.dot_general(left, right, form, preferred_element_type=F32)


def rms_factor(values):
    return lax.rsqrt(jnp.mean(values * values, -1, keepdims=True) + EPSILON)


def norm_grads(values, gain, grad):
    factor = rms_factor(values)
    scaled = values * factor
    term = grad * gain
    inner = jnp.mean(scaled * term, -1, keepdims=True)
    return factor * (term - scaled * inner), grad * scaled


def gelu_parts(values):
    root = 0.7978845608028654
    square = values * values
    tanh = jnp.tanh(values * (root + (root * 0.044715) * square))
    half = 0.5 + 0.5 * tanh
    slope = half + (0.5 * values) * (1.0 - tanh * tanh) * (root + (3 * root * 0.044715) * square)
    return values * half, slope


def gelu_only(values):
    root = 0.7978845608028654
    tanh = jnp.tanh(values * (root + (root * 0.044715) * (values * values)))
    return values * (0.5 + 0.5 * tanh)


def split_three(row):
    high = row.astype(BF).astype(F32)
    rest = row - high
    middle = rest.astype(BF).astype(F32)
    return high, middle, rest - middle


def call(body, name, grid, in_specs, out_specs, out_shape, scratch=(), prefetch=0, vmem=SMALL_MIB, us=1):
    return pl.pallas_call(
        body,
        name=name,
        grid_spec=pltpu.PrefetchScalarGridSpec(
            num_scalar_prefetch=prefetch,
            grid=grid,
            in_specs=in_specs,
            out_specs=out_specs,
            scratch_shapes=list(scratch),
        ),
        out_shape=out_shape,
        compiler_params=pltpu.CompilerParams(vmem_limit_bytes=vmem * MIB),
        cost_estimate=pl.CostEstimate(
            flops=int(us * COST * 1.15e9), bytes_accessed=MIB // 4, transcendentals=0
        ),
    )


def whole(shape):
    return pl.BlockSpec(shape, lambda *_: (0,) * len(shape))


def shape_of(shape, dtype):
    return jax.ShapeDtypeStruct(shape, dtype)


def in_hbm(shape, dtype):
    return pltpu.HBM(shape, dtype)


def lane_scratch(rows, width):
    return pltpu.VMEM((width // PAD, rows, PAD), F32)


def slabs_of(block, lanes):
    parts = lanes.shape[0]
    rows = block.shape[0] // 4
    for part in range(parts):
        lanes[part] = block[:, part * PAD : (part + 1) * PAD]
    return [
        jnp.concatenate([lanes[part, pl.ds(s, rows, stride=4), :] for part in range(parts)], 1)
        for s in range(4)
    ]


def half_rows(core, half):
    return pl.ds(pl.multiple_of(core * half, half), half)


def half_block(rows, width, steps):
    per_half = steps // 2

    def place(step, _, core):
        return jnp.clip(step - per_half * core[0], 0, per_half - 1), 0

    return pl.BlockSpec((rows // steps, width), place)


def keep_half(core, step, steps, target, block):
    @pl.when(step // (steps // 2) == core[0])
    def _():
        target[...] = block


def entry_body(_, core, x_ref, gain_ref, normed_ref, pooled_ref, half_ref, lanes):
    total = None
    slabs = slabs_of(x_ref[0, 0], lanes)
    for slab in range(4):
        values = slabs[slab]
        normed = (values * rms_factor(values) * gain_ref[...]).astype(BF)
        normed_ref[slab] = normed
        part = normed.astype(F32)
        total = part if total is None else total + part
    pooled = (total * 0.25).astype(BF)
    pooled_ref[...] = pooled
    keep_half(core, pl.program_id(0), 4, half_ref, pooled)


def entry_norm(micro, core, tokens, gain):
    length, width = tokens.shape[2:]
    rows = length // 4
    block = rows // 4
    return call(
        entry_body,
        "entry_norm",
        (4,),
        [
            pl.BlockSpec((1, 1, 4 * block, width), lambda i, m, c: (m[0], 0, i, 0)),
            whole((1, width)),
        ],
        [
            pl.BlockSpec((4, block, width), lambda i, *_: (0, i, 0)),
            pl.BlockSpec((block, width), lambda i, *_: (i, 0)),
            half_block(rows, width, 4),
        ],
        [
            shape_of((4, rows, width), BF),
            shape_of((rows, width), BF),
            shape_of((rows // 2, width), BF),
        ],
        scratch=[lane_scratch(4 * block, width)],
        prefetch=2,
        vmem=LARGE_MIB,
        us=4,
    )(micro, core, tokens, gain.reshape(1, -1))


def own_limit(place, resolution, length):
    return jnp.where(resolution[place[1], place[0]] == 1, length, TOK_LOW)


def memory_limit(place, resolution, carried, length):
    before = resolution[place[1], jnp.maximum(place[0] - 1, 0)]
    usable = (carried[place[1], place[0]] == 1) & (place[0] > 0)
    return jnp.where(usable, jnp.where(before == 1, length, TOK_LOW), 0)


def make_pair(limit, offset, source, weights):
    rows = source.shape[0]
    place = lax.broadcasted_iota(jnp.int32, (rows, 1), 0) * 4 + offset
    lane = lax.broadcasted_iota(jnp.int32, (rows, PAD), 1)
    bias = jnp.where(place < limit, 0.0, MASKED_SCORE)
    both = dot(source, weights[PAD:], NT)
    keys = jnp.where(lane < HD, both[:, :PAD], jnp.where(lane == HD, bias, 1.0))
    values = jnp.where(lane < HD, both[:, PAD:], 1.0)
    return keys.astype(BF), values.astype(BF)


def own_pairs_body(place, resolution, _, normed, weights, *results):
    limit = own_limit(place, resolution, 4 * normed.shape[1])
    for head in range(weights.shape[0]):
        parts = make_pair(limit, pl.program_id(0), normed[0], weights[head])
        for result, part in zip(results, parts):
            result[head, 0] = part


def pair_shapes(rows):
    return [(rows, PAD), (rows, PAD)]


def own_pairs(limits, normed, weights):
    _, rows, width = normed.shape
    heads = weights.shape[0]
    return call(
        own_pairs_body,
        "own_pairs",
        (4,),
        [pl.BlockSpec((1, rows, width), lambda i, *_: (i, 0, 0)), whole(weights.shape)],
        [
            pl.BlockSpec((heads, 1) + shape, lambda i, *_: (0, i, 0, 0))
            for shape in pair_shapes(rows)
        ],
        [shape_of((heads, 4) + shape, BF) for shape in pair_shapes(rows)],
        prefetch=3,
        us=6,
    )(*limits, normed, weights)


def query_tail(rows, parts):
    index = lax.broadcasted_iota(jnp.int32, (PAD - HD, rows), 0)
    tail = jnp.where(index == 0, 1.0, 0.0)
    for step, part in enumerate(parts):
        tail = jnp.where(index == step + 1, -part, tail)
    return tail.astype(BF)


def ask(source, weights):
    query = (dot(weights[:HD], source, NT) * (SCALING * LOG2E)).astype(BF)
    return query, jnp.concatenate([query, query_tail(query.shape[1], ())], 0)


def score_rows(asked, keys):
    parts = range(asked.shape[1] // PIECE)
    return [
        dot(keys(chunk)[part * PIECE : (part + 1) * PIECE], asked)
        for chunk in range(5)
        for part in parts
    ]


def attend_rows(query, scores, values):
    rows = query.shape[1]
    parts = rows // PIECE
    top = functools.reduce(jnp.maximum, [jnp.max(item, 0, keepdims=True) for item in scores])
    result = None
    for index, item in enumerate(scores):
        raised = jnp.exp2(item - top).astype(BF)
        part = index % parts
        term = dot(values(index // parts)[part * PIECE : (part + 1) * PIECE], raised, TN)
        result = term if result is None else result + term
    summed = result[HD : HD + 1]
    heads = (result[:HD] / summed).astype(BF)
    logsum = top + jnp.log2(summed)
    return heads, jnp.concatenate([query, query_tail(rows, split_three(logsum))], 0)


def chosen(own, memory, head):
    return lambda chunk: own[head, chunk] if chunk < 4 else memory[head]


def join_halves(core, mine, theirs, target):
    half = mine.shape[0]
    target[half_rows(core, half)] = mine[...]
    target[half_rows(1 - core, half)] = theirs[...]


def attend_one_body(
    place, resolution, carried, normed, mine, theirs, weights, out_weights, own_keys, own_values,
    memory, keys, values, queries_t, heads_t, partial,
):
    @pl.when(pl.program_id(0) == 0)
    def _():
        join_halves(place[2], mine, theirs, memory)
        limit = memory_limit(place, resolution, carried, 4 * memory.shape[0])
        for head in range(2):
            keys[head], values[head] = make_pair(limit, 0, memory[...], weights[head])

    total = None
    queries = [ask(normed[0], weights[head]) for head in range(2)]
    scores = [score_rows(queries[head][1], chosen(own_keys, keys, head)) for head in range(2)]
    for head in range(2):
        heads, asked = attend_rows(
            queries[head][0], scores[head], chosen(own_values, values, head)
        )
        heads_t[head] = heads
        queries_t[head] = asked
        term = dot(heads, out_weights[head], TN)
        total = term if total is None else total + term
    partial[0] = total.astype(BF)


def attend_one(limits, normed, mine, theirs, weights, out_weights, own_keys, own_values):
    _, rows, width = normed.shape
    heads = weights.shape[0]
    memory_shapes = [(heads,) + shape for shape in pair_shapes(rows)]
    return call(
        attend_one_body,
        "attend_one",
        (4,),
        [
            pl.BlockSpec((1, rows, width), lambda i, *_: (i, 0, 0)),
            whole(mine.shape),
            whole(theirs.shape),
            whole(weights.shape),
            whole(out_weights.shape),
            whole(own_keys.shape),
            whole(own_values.shape),
        ],
        [whole((rows, width))]
        + [whole(shape) for shape in memory_shapes]
        + [
            pl.BlockSpec((heads, PAD, rows), lambda i, *_: (0, 0, i)),
            pl.BlockSpec((heads, HD, rows), lambda i, *_: (0, 0, i)),
            pl.BlockSpec((1, rows, width), lambda i, *_: (i, 0, 0)),
        ],
        [shape_of((rows, width), BF)]
        + [shape_of(shape, BF) for shape in memory_shapes]
        + [
            shape_of((heads, PAD, 4 * rows), BF),
            shape_of((heads, HD, 4 * rows), BF),
            shape_of((4, rows, width), BF),
        ],
        prefetch=3,
        vmem=LARGE_MIB,
        us=22,
    )(*limits, normed, mine, theirs, weights, out_weights, own_keys, own_values)


def attend_two_body(
    place, resolution, carried, mine, theirs, pooled, weights, out_weights, skip, own_keys, own_values,
    memory, keys, values, queries_t, heads_t, partial, total,
):
    step = pl.program_id(0)

    @pl.when(step == 0)
    def _():
        join_halves(place[2], mine, theirs, memory)
        total[...] = dot(pooled[...], skip[...])

    limit = memory_limit(place, resolution, carried, 4 * memory.shape[0])
    here = range(weights.shape[0])
    queries = [ask(pooled[...], weights[head]) for head in here]
    for head in here:
        keys[head], values[head] = make_pair(limit, 0, memory[...], weights[head])
    scores = [score_rows(queries[head][1], chosen(own_keys, keys, head)) for head in here]
    for head in here:
        heads, asked = attend_rows(
            queries[head][0], scores[head], chosen(own_values, values, head)
        )
        heads_t[head] = heads
        queries_t[head] = asked
        total[...] += dot(heads, out_weights[head], TN)

    @pl.when(step == pl.num_programs(0) - 1)
    def _():
        partial[...] = total[...].astype(BF)


def attend_two(limits, mine, theirs, pooled, weights, out_weights, skip, own_keys, own_values):
    rows, width = pooled.shape
    heads = weights.shape[0]
    wide = out_weights.shape[2]

    def each(*shape):
        return pl.BlockSpec((2,) + shape, lambda h, *_: (h,) + (0,) * len(shape))

    results = pair_shapes(rows) + [(PAD, rows), (HD, rows)]
    return call(
        attend_two_body,
        "attend_two",
        (heads // 2,),
        [
            whole(mine.shape),
            whole(theirs.shape),
            whole((rows, width)),
            each(*weights.shape[1:]),
            each(HD, wide),
            whole(skip.shape),
            each(4, rows, PAD),
            each(4, rows, PAD),
        ],
        [whole((rows, width))] + [each(*shape) for shape in results] + [whole((rows, wide))],
        [shape_of((rows, width), BF)]
        + [shape_of((heads,) + shape, BF) for shape in results]
        + [shape_of((rows, wide), BF)],
        scratch=[pltpu.VMEM((rows, wide), F32)],
        prefetch=3,
        vmem=LARGE_MIB,
        us=16,
    )(*limits, mine, theirs, pooled, weights, out_weights, skip, own_keys, own_values)


def grad_chunk(keys, values, asked, given):
    chances = jnp.exp2(dot(keys, asked))
    spread = dot(values, given)
    grad_scores = (chances * spread).astype(BF)
    grad_values = dot(chances.astype(BF), given, NT)
    grad_keys = dot(grad_scores, asked, NT)
    return grad_keys, grad_values, dot(keys, grad_scores, TN)[:HD]


def given_rows(out_weights, grad, heads):
    back = dot(out_weights, grad, NT).astype(BF)
    inner = jnp.sum(back.astype(F32) * heads.astype(F32), 0, keepdims=True)
    high, middle, low = split_three(inner)
    index = lax.broadcasted_iota(jnp.int32, (PAD - HD, grad.shape[0]), 0)
    tail = jnp.where(index == 0, -high, jnp.where(index == 1, -middle, jnp.where(index == 2, -low, 0.0)))
    return jnp.concatenate([back, tail.astype(BF)], 0)


def pair_of(grad_keys, grad_values):
    return jnp.concatenate([(grad_keys * LN2).astype(BF), grad_values.astype(BF)], 1)


def plus(total, term):
    return term if total is None else total + term


class Kept:
    def __init__(self, refs, head):
        own_keys, own_values, keys, values, self.queries, self.heads = refs
        self.keys = chosen(own_keys, keys, head)
        self.values = chosen(own_values, values, head)
        self.head = head

    def grads(self, chunk, given):
        return grad_chunk(
            self.keys(chunk), self.values(chunk), self.queries[self.head], given
        )

    def given(self, out_weights, branch):
        return given_rows(out_weights[self.head], branch, self.heads[self.head])


def put_head(target, head, heads, grad_query, grad_pair, columns):
    width = target.shape[1]
    parts = [grad_query, grad_pair[:HD], grad_pair[PAD : PAD + HD]]
    sides = [columns[:, side : side + width] for side in range(0, columns.shape[1], width)]
    starts = [(index * heads + head) * HD for index in range(3)]
    starts += [(3 * heads + head * len(sides) + index) * HD for index in range(len(sides))]
    for start, part in zip(starts, parts + sides):
        target[pl.ds(pl.multiple_of(start, 32), HD)] = part.astype(BF)


def put_skip(target, start, columns, share):
    width = target.shape[1]
    for index, side in enumerate(range(0, columns.shape[1], width)):
        rows = columns[pl.ds(pl.multiple_of(share * HD, 32), HD), side : side + width]
        target[start + index * HD : start + (index + 1) * HD] = rows


def two_first_body(
    place, after, mine, theirs, cotangent, gain, normed, memory, pooled, weights, out_weights, skip,
    *refs
):
    kept, results, scratch = Kept(refs[:6], 0), refs[6:16], refs[16:]
    (branch, grad_gain, own_skip, grad_rows, grad_pool, memory_mine, memory_theirs, grad_weights,
     query_memory, pair_memory) = results
    total, columns = scratch
    step = pl.program_id(0)
    core, share = place[1], place[2]
    wide = after.shape[1]
    width = pooled.shape[1]
    sides = wide // width
    head_rows = (3 + sides) * HD

    @pl.when(step == 0)
    def _():
        first = jnp.where(core == 0, mine[...], theirs[...]).astype(F32)
        second = jnp.where(core == 0, theirs[...], mine[...]).astype(F32)
        arrived = jnp.concatenate([first, second], 0)
        back, terms = norm_grads(after[...], gain[...], arrived)
        grad_gain[...] = jnp.sum(terms, 0, keepdims=True)
        branch[...] = (cotangent[0, 0] + back).astype(BF)
        columns[...] = dot(pooled[...], branch[...], TN).astype(BF)
        put_skip(grad_weights, 2 * head_rows, columns, share ^ 2)
        put_skip(own_skip, 0, columns, share)
        grad_pool[...] = dot(branch[...], skip[...], NT)
        total[...] = jnp.zeros_like(total)

    given = kept.given(out_weights, branch[...])

    @pl.when(step < 2)
    def _():
        grad_query, grad_pair = None, None
        for chunk in range(5):
            grad_keys, grad_values, term = kept.grads(chunk, given)
            grad_query = plus(grad_query, term)
            pair = pair_of(grad_keys, grad_values)
            total[chunk] += dot(pair, weights[0, PAD:])
            source = normed[chunk] if chunk < 4 else memory[...]
            grad_pair = plus(grad_pair, dot(pair, source, TN))
        grad_query = (grad_query * SCALING).astype(BF)
        grad_pool[...] += dot(grad_query, weights[0, :HD], TN)
        put_head(
            grad_weights, step, 2, dot(grad_query, pooled[...]), grad_pair,
            dot(kept.heads[0], branch[...]),
        )

    @pl.when(step >= 2)
    def _():
        grad_keys, grad_values, term = kept.grads(4, given)
        query_memory[0] = term
        pair = pair_of(grad_keys, grad_values)
        total[4] += dot(pair, weights[0, PAD:])
        pair_memory[0] = dot(pair, memory[...], TN)

    @pl.when(step == 3)
    def _():
        half = memory_mine.shape[0]
        for chunk in range(4):
            grad_rows[chunk] = total[chunk].astype(BF)
        memory_mine[...] = total[4, half_rows(core, half)].astype(BF)
        memory_theirs[...] = total[4, half_rows(1 - core, half)].astype(BF)


def two_second_body(
    branch, normed, pooled, weights, out_weights, earlier_rows, earlier_pool, query_memory,
    pair_memory, own_skip, *refs
):
    kept, (grad_rows, grad_weights, total, total_pool) = Kept(refs[:6], 0), refs[6:]
    step = pl.program_id(0)
    head_rows = (grad_weights.shape[0] - own_skip.shape[0]) // 2

    @pl.when(step == 0)
    def _():
        grad_weights[2 * head_rows :] = own_skip[...]
        total_pool[...] = earlier_pool[...]
        for chunk in range(4):
            total[chunk] = earlier_rows[chunk].astype(F32)

    given = kept.given(out_weights, branch[...])
    grad_query, grad_pair = query_memory[0], pair_memory[0]
    for chunk in range(4):
        grad_keys, grad_values, term = kept.grads(chunk, given)
        grad_query = grad_query + term
        pair = pair_of(grad_keys, grad_values)
        total[chunk] += dot(pair, weights[0, PAD:])
        grad_pair = grad_pair + dot(pair, normed[chunk], TN)
    grad_query = (grad_query * SCALING).astype(BF)
    total_pool[...] += dot(grad_query, weights[0, :HD], TN)
    put_head(
        grad_weights, step, 2, dot(grad_query, pooled[...]), grad_pair,
        dot(kept.heads[0], branch[...]),
    )

    @pl.when(step == pl.num_programs(0) - 1)
    def _():
        for chunk in range(4):
            grad_rows[chunk] = (total[chunk] + 0.25 * total_pool[...]).astype(BF)


def kept_specs(each, rows, own=None):
    pair = pair_shapes(rows)
    return [(own or each)(4, *shape) for shape in pair] + [each(*shape) for shape in pair]


def two_first(
    place, after, mine, theirs, cotangent, gain, normed, memory, pooled, weights, out_weights, skip, kept
):
    _, rows, width = normed.shape
    wide = out_weights.shape[2]
    sides = wide // width
    all_rows = 2 * (3 + sides) * HD + sides * HD

    def each(*shape):
        return pl.BlockSpec((1,) + shape, lambda h, _: ((h + 2) % 4,) + (0,) * len(shape))

    def own(*shape):
        return pl.BlockSpec((1,) + shape, lambda h, _: (jnp.minimum(h, 1) + 2,) + (0,) * len(shape))

    def late(*shape):
        return pl.BlockSpec((1,) + shape, lambda h, _: (jnp.maximum(h, 2) - 2,) + (0,) * len(shape))

    return call(
        two_first_body,
        "back_two_first",
        (4,),
        [
            whole((rows, wide)),
            whole(mine.shape),
            whole(theirs.shape),
            pl.BlockSpec((1, 1, rows, wide), lambda h, m: (m[0], 0, 0, 0)),
            whole((1, wide)),
            whole((4, rows, width)),
            whole((rows, width)),
            whole((rows, width)),
            each(*weights.shape[1:]),
            each(HD, wide),
            whole(skip.shape),
        ]
        + kept_specs(each, rows, own)
        + [each(PAD, rows), each(HD, rows)],
        [
            whole((rows, wide)),
            whole((1, wide)),
            whole((sides * HD, width)),
            whole((4, rows, width)),
            whole((rows, width)),
            whole((rows // 2, width)),
            whole((rows // 2, width)),
            whole((all_rows, width)),
            late(HD, rows),
            late(2 * PAD, width),
        ],
        [
            shape_of((rows, wide), BF),
            shape_of((1, wide), F32),
            shape_of((sides * HD, width), BF),
            shape_of((4, rows, width), BF),
            shape_of((rows, width), F32),
            shape_of((rows // 2, width), BF),
            shape_of((rows // 2, width), BF),
            shape_of((all_rows, width), BF),
            shape_of((2, HD, rows), F32),
            shape_of((2, 2 * PAD, width), F32),
        ],
        scratch=[pltpu.VMEM((5, rows, width), F32), pltpu.VMEM((width, wide), BF)],
        prefetch=1,
        vmem=LARGE_MIB,
        us=23,
    )(
        place, after, mine, theirs, cotangent, gain.reshape(1, -1), normed, memory, pooled, weights,
        out_weights, skip, *kept,
    )


def two_second(
    branch, normed, pooled, weights, out_weights, earlier_rows, earlier_pool, query_memory,
    pair_memory, own_skip, kept
):
    _, rows, width = normed.shape
    wide = out_weights.shape[2]
    all_rows = 2 * (3 + wide // width) * HD + own_skip.shape[0]

    def each(*shape):
        return pl.BlockSpec((1,) + shape, lambda h: (h,) + (0,) * len(shape))

    return call(
        two_second_body,
        "back_two_second",
        (2,),
        [
            whole((rows, wide)),
            whole((4, rows, width)),
            whole((rows, width)),
            each(*weights.shape[1:]),
            each(HD, wide),
            whole((4, rows, width)),
            whole((rows, width)),
            each(HD, rows),
            each(2 * PAD, width),
            whole(own_skip.shape),
        ]
        + kept_specs(each, rows)
        + [each(PAD, rows), each(HD, rows)],
        [whole((4, rows, width)), whole((all_rows, width))],
        [shape_of((4, rows, width), BF), shape_of((all_rows, width), BF)],
        scratch=[pltpu.VMEM((4, rows, width), F32), pltpu.VMEM((rows, width), F32)],
        vmem=LARGE_MIB,
        us=14,
    )(
        branch, normed, pooled, weights, out_weights, earlier_rows, earlier_pool, query_memory,
        pair_memory, own_skip, *kept,
    )


def one_first_body(
    core, grad_two, after, own_part, other_part, gain, normed, memory, weights, out_weights, *refs
):
    kept, near_kept = Kept(refs[:6], 1), Kept(refs[:6], 0)
    (grad_one, branch_ref, grad_gain, grad_rows, memory_mine, memory_theirs, grad_weights,
     query_memory, pair_memory, memory_gain) = refs[6:16]
    total, total_keys, total_values, total_query, total_out, near_keys, near_values, rows_memory = (
        refs[16:]
    )
    slab = pl.program_id(0)

    @pl.when(slab == 0)
    def _():
        for item in (grad_gain, total_keys, total_values, total_query, total_out, near_keys, near_values):
            item[...] = jnp.zeros_like(item)

    arrived = own_part[0].astype(F32) + other_part[0].astype(F32)
    back, terms = norm_grads(after[0], gain[...], arrived)
    grad_gain[...] += jnp.sum(terms, 0, keepdims=True)
    state = grad_two[0] + back
    grad_one[0] = state
    branch = state.astype(BF)
    branch_ref[0] = branch
    given = kept.given(out_weights, branch)
    grad_query = None
    for chunk in range(5):
        grad_keys, grad_values, term = kept.grads(chunk, given)
        total_keys[chunk] += grad_keys
        total_values[chunk] += grad_values
        grad_query = plus(grad_query, term)
    grad_keys, grad_values, term = near_kept.grads(4, near_kept.given(out_weights, branch))
    near_keys[...] += grad_keys
    near_values[...] += grad_values
    query_memory[...] = term
    grad_query = (grad_query * SCALING).astype(BF)
    total_out[...] += dot(kept.heads[1], branch)
    total_query[...] += dot(grad_query, normed[slab])
    total[slab] = dot(grad_query, weights[1, :HD], TN)

    @pl.when(slab == pl.num_programs(0) - 1)
    def _():
        pair = pair_of(near_keys[...], near_values[...])
        pair_memory[...] = dot(pair, memory[...], TN)
        near_rows = dot(pair, weights[0, PAD:])
        grad_pair = None
        for chunk in range(5):
            pair = pair_of(total_keys[chunk], total_values[chunk])
            rows = dot(pair, weights[1, PAD:])
            source = normed[chunk] if chunk < 4 else memory[...]
            grad_pair = plus(grad_pair, dot(pair, source, TN))
            if chunk < 4:
                grad_rows[chunk] = (total[chunk] + rows).astype(BF)
            else:
                rows = near_rows + rows
                memory_gain[...] = jnp.sum(rows * memory[...].astype(F32), 0, keepdims=True)
                rows_memory[...] = rows
        half = memory_mine.shape[0]
        memory_mine[...] = rows_memory[half_rows(core[0], half)].astype(BF)
        memory_theirs[...] = rows_memory[half_rows(1 - core[0], half)].astype(BF)
        grad_weights[:HD] = total_query[...].astype(BF)
        grad_weights[HD : 2 * HD] = grad_pair[:HD].astype(BF)
        grad_weights[2 * HD : 3 * HD] = grad_pair[PAD : PAD + HD].astype(BF)
        grad_weights[3 * HD : 4 * HD] = total_out[...].astype(BF)
        grad_weights[4 * HD :] = jnp.zeros_like(grad_weights[4 * HD :])


def one_second_body(
    core, branch_ref, normed, weights, out_weights, earlier_rows, query_memory, pair_memory,
    memory_gain, gain, other_gains, *refs
):
    kept, (mine, theirs, grad_weights) = Kept(refs[:6], 0), refs[6:9]
    total, total_keys, total_values, total_query, total_out = refs[9:]
    slab = pl.program_id(0)

    @pl.when(slab == 0)
    def _():
        for item in (total_keys, total_values, total_query, total_out):
            item[...] = jnp.zeros_like(item)

    branch = branch_ref[0]
    given = kept.given(out_weights, branch)
    grad_query = query_memory[...]
    for chunk in range(4):
        grad_keys, grad_values, term = kept.grads(chunk, given)
        total_keys[chunk] += grad_keys
        total_values[chunk] += grad_values
        grad_query = grad_query + term
    grad_query = (grad_query * SCALING).astype(BF)
    total_out[...] += dot(kept.heads[0], branch)
    total_query[...] += dot(grad_query, normed[slab])
    total[slab] = dot(grad_query, weights[0, :HD], TN)

    @pl.when(slab == pl.num_programs(0) - 1)
    def _():
        grad_pair = pair_memory[...]
        gain_terms = memory_gain[...]
        share = mine.shape[2]
        for chunk in range(4):
            pair = pair_of(total_keys[chunk], total_values[chunk])
            rows = dot(pair, weights[0, PAD:]) + earlier_rows[chunk].astype(F32)
            rows = total[chunk] + rows
            gain_terms += jnp.sum(rows * normed[chunk].astype(F32), 0, keepdims=True)
            total[chunk] = rows
            for chip in range(mine.shape[1]):
                for target, which in ((mine, core[0]), (theirs, 1 - core[0])):
                    start = pl.multiple_of((2 * chip + which) * share, share)
                    target[chunk, chip] = total[chunk, pl.ds(start, share)].astype(BF)
            grad_pair = grad_pair + dot(pair, normed[chunk], TN)
        gains = jnp.concatenate([gain_terms / gain[...], other_gains[1:]], 0)
        grad_weights[4 * HD :] = gains.astype(BF)
        grad_weights[:HD] = total_query[...].astype(BF)
        grad_weights[HD : 2 * HD] = grad_pair[:HD].astype(BF)
        grad_weights[2 * HD : 3 * HD] = grad_pair[PAD : PAD + HD].astype(BF)
        grad_weights[3 * HD : 4 * HD] = total_out[...].astype(BF)


def one_specs(rows):
    def heads(*shape):
        return whole((2,) + shape)

    return kept_specs(heads, rows) + [
        pl.BlockSpec((2, PAD, rows), lambda i, *_: (0, 0, i)),
        pl.BlockSpec((2, HD, rows), lambda i, *_: (0, 0, i)),
    ]


def one_scratch(rows, width, chunks):
    return [
        pltpu.VMEM((4, rows, width), F32),
        pltpu.VMEM((chunks, rows, PAD), F32),
        pltpu.VMEM((chunks, rows, PAD), F32),
        pltpu.VMEM((HD, width), F32),
        pltpu.VMEM((HD, width), F32),
    ]


def one_first(
    core, grad_two, after, own_part, other_part, gain, normed, memory, weights, out_weights, kept
):
    _, rows, width = grad_two.shape
    slab = pl.BlockSpec((1, rows, width), lambda i, *_: (i, 0, 0))
    return call(
        one_first_body,
        "back_one_first",
        (4,),
        [slab, slab, slab, slab, whole((1, width)), whole((4, rows, width)), whole((rows, width))]
        + [whole(weights.shape), whole(out_weights.shape)]
        + one_specs(rows),
        [
            slab,
            slab,
            whole((1, width)),
            whole((4, rows, width)),
            whole((rows // 2, width)),
            whole((rows // 2, width)),
            whole((4 * HD + GAIN_ROWS, width)),
            pl.BlockSpec((HD, rows), lambda i, *_: (0, i)),
            whole((2 * PAD, width)),
            whole((1, width)),
        ],
        [
            shape_of((4, rows, width), F32),
            shape_of((4, rows, width), BF),
            shape_of((1, width), F32),
            shape_of((4, rows, width), BF),
            shape_of((rows // 2, width), BF),
            shape_of((rows // 2, width), BF),
            shape_of((4 * HD + GAIN_ROWS, width), BF),
            in_hbm((HD, 4 * rows), F32),
            shape_of((2 * PAD, width), F32),
            shape_of((1, width), F32),
        ],
        scratch=one_scratch(rows, width, 5)
        + [pltpu.VMEM((rows, PAD), F32), pltpu.VMEM((rows, PAD), F32), pltpu.VMEM((rows, width), F32)],
        prefetch=1,
        vmem=LARGE_MIB,
        us=27,
    )(
        core, grad_two, after, own_part, other_part, gain.reshape(1, -1), normed, memory, weights,
        out_weights, *kept,
    )


def one_second(
    core, branch, normed, weights, out_weights, earlier_rows, query_memory, pair_memory, memory_gain,
    gain, other_gains, kept
):
    _, rows, width = branch.shape
    slab = pl.BlockSpec((1, rows, width), lambda i, *_: (i, 0, 0))
    leaving = (4, 2, rows // 4, width)
    return call(
        one_second_body,
        "back_one_second",
        (4,),
        [
            slab,
            whole((4, rows, width)),
            whole(weights.shape),
            whole(out_weights.shape),
            whole((4, rows, width)),
            pl.BlockSpec((HD, rows), lambda i, *_: (0, i)),
            whole((2 * PAD, width)),
            whole((1, width)),
            whole((1, width)),
            whole(other_gains.shape),
        ]
        + one_specs(rows),
        [whole(leaving), whole(leaving), whole((4 * HD + other_gains.shape[0], width))],
        [
            shape_of(leaving, BF),
            shape_of(leaving, BF),
            shape_of((4 * HD + other_gains.shape[0], width), BF),
        ],
        scratch=one_scratch(rows, width, 4),
        prefetch=1,
        vmem=LARGE_MIB,
        us=18,
    )(
        core, branch, normed, weights, out_weights, earlier_rows, query_memory, pair_memory,
        memory_gain, gain.reshape(1, -1), other_gains, *kept,
    )


def flat(block):
    return block.reshape(block.shape[0] * block.shape[1], block.shape[2])


def hidden_one_body(_, x_ref, own_part, other_part, gain, w_in, w_out, after, partial, lanes):
    tokens = slabs_of(x_ref[0, 0], lanes)
    for pair in range(0, 4, HIDDEN_SLABS):
        slabs = slice(pair, pair + HIDDEN_SLABS)
        state = flat(own_part[slabs].astype(F32) + other_part[slabs].astype(F32))
        state = state + jnp.concatenate(tokens[slabs], 0)
        after[slabs] = state.reshape(HIDDEN_SLABS, -1, state.shape[1])
        normed = (state * rms_factor(state) * gain[...]).astype(BF)
        active = gelu_only(dot(normed, w_in[...], NT)).astype(BF)
        partial[slabs] = dot(active, w_out[...]).astype(BF).reshape(HIDDEN_SLABS, -1, state.shape[1])


def hidden_one(micro, tokens, own_part, other_part, gain, w_in, w_out):
    _, rows, width = own_part.shape
    block = rows // 4
    strip = pl.BlockSpec((4, block, width), lambda i, m: (0, i, 0))
    return call(
        hidden_one_body,
        "hidden_one",
        (4,),
        [
            pl.BlockSpec((1, 1, 4 * block, width), lambda i, m: (m[0], 0, i, 0)),
            strip,
            strip,
            whole((1, width)),
            whole(w_in.shape),
            whole(w_out.shape),
        ],
        [strip, strip],
        [shape_of((4, rows, width), F32), shape_of((4, rows, width), BF)],
        scratch=[lane_scratch(4 * block, width)],
        prefetch=1,
        vmem=LARGE_MIB,
        us=7,
    )(micro, tokens, own_part, other_part, gain.reshape(1, -1), w_in, w_out)


def norm_three_body(_, core, state, own_part, other_part, gain, after, normed, pooled_ref, half_ref):
    total = None
    for slab in range(4):
        values = state[slab] + (own_part[slab].astype(F32) + other_part[slab].astype(F32))
        after[slab] = values
        rows = (values * rms_factor(values) * gain[...]).astype(BF)
        normed[slab] = rows
        total = rows.astype(F32) if total is None else total + rows.astype(F32)
    pooled = (total * 0.25).astype(BF)
    pooled_ref[...] = pooled
    keep_half(core, pl.program_id(0), 4, half_ref, pooled)


def norm_three(micro, core, state, own_part, other_part, gain):
    _, rows, width = state.shape
    block = rows // 4
    strip = pl.BlockSpec((4, block, width), lambda i, *_: (0, i, 0))
    return call(
        norm_three_body,
        "norm_three",
        (4,),
        [strip, strip, strip, whole((1, width))],
        [
            strip,
            strip,
            pl.BlockSpec((block, width), lambda i, *_: (i, 0)),
            half_block(rows, width, 4),
        ],
        [
            shape_of((4, rows, width), F32),
            shape_of((4, rows, width), BF),
            shape_of((rows, width), BF),
            shape_of((rows // 2, width), BF),
        ],
        prefetch=2,
        us=5,
    )(micro, core, state, own_part, other_part, gain.reshape(1, -1))


def hidden_one_back_body(
    core, after_two, own_part, other_part, mine, theirs, gain_three, after_one, gain_two, w_in, w_out,
    grad_two, partial, grad_own, grad_sent, grad_gain, total_in, total_out,
):
    step = pl.program_id(0)

    @pl.when(step == 0)
    def _():
        total_in[...] = jnp.zeros_like(total_in)
        total_out[...] = jnp.zeros_like(total_out)
        grad_gain[...] = jnp.zeros_like(grad_gain)

    memory = jnp.where(step // 2 == core[0], mine[...], theirs[...]).astype(F32) * 0.25
    width = memory.shape[1]
    for pair in range(0, 4, HIDDEN_SLABS):
        slabs = slice(pair, pair + HIDDEN_SLABS)
        arrived = own_part[slabs].astype(F32) + other_part[slabs].astype(F32) + memory[None]
        back, terms = norm_grads(flat(after_two[slabs]), gain_three[...], flat(arrived))
        grad_gain[...] += jnp.sum(terms, 0, keepdims=True)
        grad_two[slabs] = back.reshape(HIDDEN_SLABS, -1, width)
        branch = back.astype(BF)
        state = flat(after_one[slabs])
        normed = (state * rms_factor(state) * gain_two[...]).astype(BF)
        active, slope = gelu_parts(dot(normed, w_in[...], NT))
        grad_pre = (slope * dot(branch, w_out[...], NT)).astype(BF)
        partial[slabs] = dot(grad_pre, w_in[...]).astype(BF).reshape(HIDDEN_SLABS, -1, width)
        total_out[...] += dot(active.astype(BF), branch, TN)
        total_in[...] += dot(grad_pre, normed, TN)

    @pl.when(step == pl.num_programs(0) - 1)
    def _():
        share = total_in.shape[0] // 2
        for target, start in ((grad_own, 0), (grad_sent, share)):
            target[:share] = jnp.transpose(total_in[start : start + share]).astype(BF)
            target[share:] = total_out[start : start + share].astype(BF)


def hidden_one_back(
    core, after_two, own_part, other_part, mine, theirs, gain_three, after_one, gain_two, w_in, w_out
):
    _, rows, width = after_two.shape
    block = rows // 4
    hidden = w_in.shape[0]
    strip = pl.BlockSpec((4, block, width), lambda i, *_: (0, i, 0))
    memory = pl.BlockSpec((block, width), lambda i, *_: (i % 2, 0))
    return call(
        hidden_one_back_body,
        "hidden_one_back",
        (4,),
        [
            strip,
            strip,
            strip,
            memory,
            memory,
            whole((1, width)),
            strip,
            whole((1, width)),
            whole(w_in.shape),
            whole(w_out.shape),
        ],
        [strip, strip, whole(w_in.shape), whole(w_out.shape), whole((1, width))],
        [
            in_hbm((4, rows, width), F32),
            shape_of((4, rows, width), BF),
            shape_of(w_in.shape, BF),
            shape_of(w_out.shape, BF),
            shape_of((1, width), F32),
        ],
        scratch=[pltpu.VMEM((hidden, width), F32), pltpu.VMEM((hidden, width), F32)],
        prefetch=1,
        us=15,
    )(
        core, after_two, own_part, other_part, mine, theirs, gain_three.reshape(1, -1), after_one,
        gain_two.reshape(1, -1), w_in, w_out,
    )


def norm_four_body(core, own_part, other_part, gain, after, normed_ref, half_ref):
    state = own_part[...].astype(F32) + other_part[...].astype(F32)
    after[...] = state
    normed = (state * rms_factor(state) * gain[...]).astype(BF)
    normed_ref[...] = normed

    @pl.when(pl.program_id(0) == core[0])
    def _():
        half_ref[...] = normed


def norm_four(core, own_part, other_part, gain):
    rows, wide = own_part.shape
    half = rows // 2
    strip = pl.BlockSpec((half, wide), lambda i, _: (i, 0))
    return call(
        norm_four_body,
        "norm_four",
        (2,),
        [strip, strip, whole((1, wide))],
        [strip, strip, whole((half, wide))],
        [shape_of((rows, wide), F32), shape_of((rows, wide), BF), shape_of((half, wide), BF)],
        prefetch=1,
        us=2,
        vmem=FFN_MIB,
    )(core, own_part, other_part, gain.reshape(1, -1))


def hidden_two_body(
    place, first, second, cotangent, w_in, w_out,
    normed_ref, active_ref, grad_pre_ref, grad_mine, grad_theirs, result_mine, result_theirs,
):
    mine = pl.program_id(0) == place[1]
    normed = jnp.where(mine, first[...], second[...])
    normed_ref[...] = normed
    active, slope = gelu_parts(dot(normed, w_in[...]))
    active = active.astype(BF)
    grad_pre = (slope * dot(cotangent[0, 0].astype(BF), w_out[...], NT)).astype(BF)
    grad_normed = dot(grad_pre, w_in[...], NT).astype(BF)
    active_ref[...] = active
    grad_pre_ref[...] = grad_pre
    result = dot(active, w_out[...]).astype(BF)

    @pl.when(mine)
    def _():
        grad_mine[...] = grad_normed
        result_mine[...] = result

    @pl.when(jnp.logical_not(mine))
    def _():
        grad_theirs[...] = grad_normed
        result_theirs[...] = result


def hidden_two(place, first, second, cotangent, w_in, w_out):
    wide, hidden = w_in.shape
    rows = cotangent.shape[2]
    half = rows // 2
    given = pl.BlockSpec((half, wide), lambda i, p: (i if first is second else 0, 0))
    strip = pl.BlockSpec((half, wide), lambda i, p: (i, 0))
    strip_hidden = pl.BlockSpec((half, hidden), lambda i, p: (i, 0))
    return call(
        hidden_two_body,
        "hidden_two",
        (2,),
        [
            given,
            given,
            pl.BlockSpec((1, 1, half, wide), lambda i, p: (p[0], 0, i, 0)),
            whole(w_in.shape),
            whole(w_out.shape),
        ],
        [strip, strip_hidden, strip_hidden] + [whole((half, wide))] * 4,
        [in_hbm((rows, wide), BF), in_hbm((rows, hidden), BF), in_hbm((rows, hidden), BF)]
        + [shape_of((half, wide), BF)] * 2
        + [in_hbm((half, wide), BF)] * 2,
        prefetch=1,
        us=5,
        vmem=FFN_MIB,
    )(place, first, second, cotangent, w_in, w_out)


def hidden_two_weights_body(
    _, own_normed, own_active, own_pre, other_normed, other_active, other_pre, own_cot, other_cot,
    grad_in, grad_out,
):
    grad_in[...] = (
        dot(own_normed[...], own_pre[...], TN) + dot(other_normed[...], other_pre[...], TN)
    ).astype(BF)
    grad_out[...] = (
        dot(own_active[...], own_cot[0, 0].astype(BF), TN)
        + dot(other_active[...], other_cot[0, 0].astype(BF), TN)
    ).astype(BF)


def hidden_two_weights(micros, own, other, cotangent):
    rows, wide = own[0].shape
    hidden = own[1].shape[1]
    parts = 3
    column = pl.BlockSpec((rows, wide // parts), lambda i, m: (0, i))
    column_hidden = pl.BlockSpec((rows, hidden // parts), lambda i, m: (0, i))
    return call(
        hidden_two_weights_body,
        "hidden_two_weights",
        (parts,),
        [
            column,
            column_hidden,
            whole((rows, hidden)),
            column,
            column_hidden,
            whole((rows, hidden)),
            pl.BlockSpec((1, 1, rows, wide), lambda i, m: (m[0], 0, 0, 0)),
            pl.BlockSpec((1, 1, rows, wide), lambda i, m: (m[1], 0, 0, 0)),
        ],
        [
            pl.BlockSpec((wide // parts, hidden), lambda i, m: (i, 0)),
            pl.BlockSpec((hidden // parts, wide), lambda i, m: (i, 0)),
        ],
        [shape_of((wide, hidden), BF), shape_of((hidden, wide), BF)],
        prefetch=1,
        us=5,
        vmem=FFN_MIB,
    )(micros, *own, *other, cotangent, cotangent)


def exit_body(place, x_ref, grad_one, partial, got, mine, theirs, gain, grad_input, lanes):
    block = mine.shape[0]
    slabs = slabs_of(x_ref[0, 0], lanes)
    memory = jnp.where(place[2] == place[3], mine[...], theirs[...]).astype(F32) * 0.25
    for slab in range(4):
        arrived = partial[slab, 0].astype(F32) + got[slab, 0].astype(F32) + memory
        back, _ = norm_grads(slabs[slab], gain[...], arrived)
        result = grad_one[slab] + back
        for part in range(lanes.shape[0]):
            lanes[part, pl.ds(slab, block, stride=4), :] = result[:, part * PAD : (part + 1) * PAD]
    for part in range(lanes.shape[0]):
        columns = lanes[part].astype(grad_input.dtype)
        grad_input[:, part * PAD : (part + 1) * PAD] = columns


def exit_norm(place, tokens, grad_one, partial, got, mine, theirs, gain, dtype):
    length, width = tokens.shape[2:]
    share = length // 4
    block = share // 4
    leaving = pl.BlockSpec((4, 1, block, width), lambda i, p: (0, p[2], 0, 0))
    memory = pl.BlockSpec((block, width), lambda i, p: (p[3], 0))
    return call(
        exit_body,
        "exit_norm",
        (1,),
        [
            pl.BlockSpec((1, 1, share, width), lambda i, p: (p[0], 0, p[1], 0)),
            pl.BlockSpec((4, block, width), lambda i, p: (0, p[1], 0)),
            leaving,
            leaving,
            memory,
            memory,
            whole((1, width)),
        ],
        whole((share, width)),
        shape_of((share, width), dtype),
        scratch=[lane_scratch(share, width)],
        prefetch=1,
        vmem=LARGE_MIB,
        us=4,
    )(place, tokens, grad_one, partial, got, mine, theirs, gain.reshape(1, -1))


def swap(block, axis, bit):
    return lax.ppermute(block, axis, [(i, i ^ bit) for i in range(lax.axis_size(axis))])


def shifted(block, distance):
    devices = lax.axis_size("clip")
    return lax.ppermute(block, "clip", [(i, (i + distance) % devices) for i in range(devices)])


def after(block, earlier):
    return lax.optimization_barrier((block, earlier))[0]


def in_order(core, mine, theirs):
    ordered = jnp.where(core == 0, jnp.stack([mine, theirs]), jnp.stack([theirs, mine]))
    return ordered.reshape((-1,) + mine.shape[1:])


def share_of(block, core):
    half = block.shape[0] // 2
    return lax.dynamic_slice_in_dim(block, core * half, half, 0)


def together(results, *others):
    return lax.optimization_barrier((results,) + others)


class ClipSum:
    def __init__(self, block, halvings=1):
        clips = lax.axis_size("clip")
        self.index = lax.axis_index("clip")
        steps = [2**k for k in range(clips.bit_length() - 1)]
        halved = steps[:halvings]
        self.todo = [("halve", step) for step in halved] + [("add", step) for step in steps[halvings:]]
        self.todo += [("join", step) for step in reversed(halved)]
        self.block = block
        self.send()

    @classmethod
    def resumed(cls, block, todo, got):
        self = cls.__new__(cls)
        self.index = lax.axis_index("clip")
        self.block, self.todo, self.got = block, list(todo), got
        return self

    def send(self):
        kind, step = self.todo[0]
        bit = self.index // step % 2
        sent = share_of(self.block, 1 - bit) if kind == "halve" else self.block
        self.got = swap(sent, "clip", step)

    def take(self):
        kind, step = self.todo.pop(0)
        bit = self.index // step % 2
        got, self.got = self.got, None
        if kind == "join":
            self.block = in_order(bit, self.block, got)
        else:
            kept = share_of(self.block, bit) if kind == "halve" else self.block
            self.block = plus_rounded(kept, got)

    def step(self):
        self.take()
        if self.todo:
            self.send()

def plus_rounded(own, got):
    return (own.astype(F32) + got.astype(F32)).astype(BF)


def pad_heads(turned):
    widths = [(0, 0)] * (turned.ndim - 2) + [(0, PAD - HD), (0, 0)]
    padded = jnp.pad(turned, widths)
    return padded.reshape(turned.shape[:-3] + (3 * PAD, turned.shape[-1]))


def per_device(
    tokens_in,
    gain_one,
    heads_in_one,
    heads_out_one,
    gain_two,
    hidden_in_one,
    hidden_out_one,
    gain_three,
    heads_in_two,
    skip_weight,
    heads_out_two,
    gain_four,
    hidden_in_two,
    hidden_out_two,
    resolution,
    continues,
    cotangent,
):
    clip_index = lax.axis_index("clip")
    part_index = lax.axis_index("tensor")
    chip, core = part_index // 2, part_index % 2
    micro = chip.astype(jnp.int32).reshape(1)
    core_index = core.astype(jnp.int32).reshape(1)
    length, width = tokens_in.shape[2:]
    rows = length // 4
    wide = heads_out_two.shape[1]

    limits = (jnp.stack([clip_index, chip, core]).astype(jnp.int32), resolution, continues)

    skip_rows = skip_weight.shape[0]
    heads_rows = 3 * HD
    own_one = jnp.concatenate(
        [jnp.transpose(heads_in_one, (1, 2, 0)).reshape(heads_rows, width), heads_out_one], 0
    )
    far_one = swap(own_one, "tensor", 2)
    own_hidden = jnp.stack([jnp.transpose(hidden_in_one), hidden_out_one])
    own_two = jnp.transpose(heads_in_two, (1, 2, 0)).reshape(3, -1, HD, width)
    own_two = jnp.swapaxes(own_two, 0, 1)

    normed_one, _, pooled_half = entry_norm(micro, core_index, tokens_in, gain_one)
    pooled_half, own_hidden, own_two, far_one = together(pooled_half, own_hidden, own_two, far_one)
    memory_mine = shifted(pooled_half, 1)
    far_hidden = swap(own_hidden, "tensor", 2)
    both_one = jnp.stack([own_one, far_one])
    weights_one = pad_heads(both_one[:, :heads_rows].reshape(2, 3, HD, width))
    out_one = both_one[:, heads_rows:]
    own_kept_one = list(own_pairs(limits, normed_one, weights_one))
    memory_mine, own_kept_one = together(memory_mine, own_kept_one)
    memory_theirs = swap(memory_mine, "tensor", 1)
    memory_one, *kept_one, attn_part = attend_one(
        limits, normed_one, memory_mine, memory_theirs, weights_one, out_one, *own_kept_one,
    )
    kept_one = own_kept_one + kept_one
    attn_part, far_hidden = together(attn_part, far_hidden)
    far_two = swap(after(own_two, far_hidden), "tensor", 2)
    w_in_one = jnp.concatenate([own_hidden[0], far_hidden[0]], 0)
    w_out_one = jnp.concatenate([own_hidden[1], far_hidden[1]], 0)
    after_one, ffn_part = hidden_one(
        micro, tokens_in, attn_part, swap(attn_part, "tensor", 1), gain_two, w_in_one, w_out_one
    )
    ffn_part, far_two = together(ffn_part, far_two)
    weights_two = pad_heads(jnp.concatenate([own_two, far_two], 0))
    own_rows = jnp.concatenate([skip_weight, heads_out_two], 0)
    far_rows = swap(after(own_rows, far_two), "tensor", 2)
    after_two, normed_three, pooled_three, pooled_half = norm_three(
        micro, core_index, after_one, ffn_part, swap(ffn_part, "tensor", 1), gain_three
    )

    memory_mine = shifted(pooled_half, 1)
    own_kept_two = list(own_pairs(limits, normed_three, weights_two))
    memory_mine, own_kept_two, far_rows = together(memory_mine, own_kept_two, far_rows)
    out_two = jnp.concatenate([own_rows[skip_rows:], far_rows[skip_rows:]], 0).reshape(-1, HD, wide)
    skip = jnp.zeros((width, wide), BF)
    skip = lax.dynamic_update_slice(skip, own_rows[:skip_rows], (part_index * skip_rows, 0))
    skip = lax.dynamic_update_slice(skip, far_rows[:skip_rows], ((part_index ^ 2) * skip_rows, 0))
    memory_theirs = swap(memory_mine, "tensor", 1)
    memory_two, *kept_two, branch_part = attend_two(
        limits, memory_mine, memory_theirs, pooled_three, weights_two, out_two, skip,
        *own_kept_two,
    )
    kept_two = own_kept_two + kept_two
    after_three, normed_four, normed_half = norm_four(
        core_index, branch_part, swap(branch_part, "tensor", 1), gain_four
    )
    far_mine = swap(normed_half, "tensor", 2)
    near_place = jnp.stack([chip, core]).astype(jnp.int32)
    far_place = jnp.stack([1 - chip, core]).astype(jnp.int32)
    *own_ffn, own_mine, own_theirs, result_mine, result_theirs = hidden_two(
        near_place, normed_four, normed_four, cotangent, hidden_in_two, hidden_out_two
    )
    far_mine, own_theirs = together(far_mine, own_theirs)
    far_theirs = swap(far_mine, "tensor", 1)
    own_got = swap(own_theirs, "tensor", 1)
    *far_ffn, far_grad_mine, far_grad_theirs, far_result_mine, far_result_theirs = hidden_two(
        far_place, far_mine, far_theirs, cotangent, hidden_in_two, hidden_out_two
    )
    far_sum = plus_rounded(far_grad_mine, swap(far_grad_theirs, "tensor", 1))
    far_sum = swap(far_sum, "tensor", 2)
    w_hidden_two = hidden_two_weights(
        jnp.concatenate([micro, 1 - micro]), own_ffn, far_ffn, cotangent
    )
    far_sum, own_got, w_hidden_two = together(far_sum, own_got, w_hidden_two)
    grad_mine = own_mine.astype(F32) + own_got.astype(F32) + far_sum.astype(F32)
    grad_mine = grad_mine.astype(BF)
    grad_theirs = swap(grad_mine, "tensor", 1)
    early_totals = lax.psum(tuple(w_hidden_two), "clip")
    sides = wide // width
    in_rows = heads_in_two.shape[2] * 3

    def turned(block):
        return jnp.transpose(block.reshape(3, -1, width), (2, 0, 1)).astype(F32)

    def unfold(block):
        block = block.reshape(-1, sides, HD, width).astype(F32)
        return jnp.concatenate([block[:, k] for k in range(sides)], 2).reshape(-1, wide)

    left = []

    def backward():
        place = jnp.stack([chip, core, part_index]).astype(jnp.int32)
        (branch_two, w_gain_four, w_skip, *early, memory_kept, memory_sent, w_two_sent, query_two,
         pair_two) = two_first(
            place, after_three, grad_mine, grad_theirs, cotangent, gain_four, normed_three,
            memory_two, pooled_three, weights_two, out_two, skip, kept_two,
        )
        memory_part = shifted(plus_rounded(memory_kept, swap(memory_sent, "tensor", 1)), -1)
        w_two_far = swap(w_two_sent, "tensor", 2)
        grad_rows_two, w_two = two_second(
            branch_two, normed_three, pooled_three, weights_two, out_two, *early, query_two,
            pair_two, w_skip, kept_two,
        )
        grad_rows_two, memory_part, w_two, w_two_far = together(
            grad_rows_two, memory_part, w_two, w_two_far
        )
        got_rows_two = swap(grad_rows_two, "tensor", 1)
        memory_theirs = swap(memory_part, "tensor", 1)
        total_two = ClipSum(plus_rounded(w_two, w_two_far))
        result_far = plus_rounded(far_result_mine, swap(far_result_theirs, "tensor", 1))
        result_far = swap(result_far, "tensor", 2)
        result_got = swap(result_theirs, "tensor", 1)

        grad_two, grad_part_two, w_hidden, w_hidden_sent, w_gain_three = hidden_one_back(
            core_index, after_two, grad_rows_two, got_rows_two, memory_part,
            memory_theirs, gain_three, after_one, gain_two, w_in_one, w_out_one,
        )
        grad_part_two, total_two.got, result_far, result_got, w_hidden, w_hidden_sent = together(
            grad_part_two, total_two.got, result_far, result_got, w_hidden, w_hidden_sent
        )
        total_two.step()
        w_hidden_far = swap(w_hidden_sent, "tensor", 2)
        result_half = result_mine.astype(F32) + result_got.astype(F32) + result_far.astype(F32)
        result_half = (result_half + share_of(after_three, core)).astype(BF)
        (grad_one, branch_one, w_gain_two, early_rows, memory_kept, memory_sent, w_last_sent,
         *memory_terms) = one_first(
            core_index, grad_two, after_one, grad_part_two, swap(grad_part_two, "tensor", 1),
            gain_two, normed_one, memory_one, weights_one, out_one, kept_one,
        )
        branch_one, total_two.got, w_hidden_far, w_last_sent = together(
            branch_one, total_two.got, w_hidden_far, w_last_sent
        )
        total_two.step()
        total_hidden = ClipSum(plus_rounded(w_hidden, w_hidden_far), 2)
        memory_last = shifted(plus_rounded(memory_kept, swap(memory_sent, "tensor", 1)), -1)
        w_last_far = swap(w_last_sent, "tensor", 2)
        far_result_half = swap(after(result_half, w_hidden_far), "tensor", 2)
        gains = jnp.concatenate([w_gain_two, w_gain_three, w_gain_four], 1).reshape(-1, width) * 0.5
        gains = jnp.pad(gains, ((1, GAIN_ROWS - 1 - gains.shape[0]), (0, 0)))
        leaving, leaving_sent, w_last = one_second(
            core_index, branch_one, normed_one, weights_one, out_one, early_rows, *memory_terms,
            gain_one, gains, kept_one,
        )
        (leaving, leaving_sent, memory_last, total_two.got, total_hidden.got, w_last, w_last_far,
         far_result_half) = together(
            leaving, leaving_sent, memory_last, total_two.got, total_hidden.got, w_last, w_last_far,
            far_result_half,
        )
        left[:] = [total_two.todo, total_hidden.todo]
        return (
            leaving, leaving_sent, memory_last, total_two.got, total_hidden.got, w_last, w_last_far,
            far_result_half, grad_one, total_two.block, total_hidden.block, result_half,
        )

    shapes = jax.eval_shape(backward)

    def absent():
        return tuple(jnp.zeros(item.shape, item.dtype) for item in shapes)

    results = lax.cond(clip_index < tokens_in.shape[0] * lax.axis_size("clip"), backward, absent)
    results, early_totals = together(results, early_totals)
    (leaving, leaving_sent, memory_last, got_two, got_hidden, w_last, w_last_far, far_result_half,
     grad_one, block_two, block_hidden, result_half) = results
    total_two = ClipSum.resumed(block_two, left[0], got_two)
    total_hidden = ClipSum.resumed(block_hidden, left[1], got_hidden)
    leaving_got = swap(leaving_sent, "tensor", 1)
    memory_theirs = swap(memory_last, "tensor", 1)
    total_last = ClipSum(plus_rounded(w_last, w_last_far))
    total_hidden.step()

    def leave(which, dtype):
        place = jnp.stack([chip, which * 2 + core, which, core]).astype(jnp.int32)
        return exit_norm(
            place, tokens_in, grad_one, leaving, leaving_got, memory_last, memory_theirs, gain_one,
            dtype,
        )

    def move_on(beside_it, *sums):
        sums = [item for item in sums if item.todo]
        beside_it, *arrived = together(beside_it, *[item.got for item in sums])
        for item, got in zip(sums, arrived):
            item.got = got
            item.step()
        return beside_it

    far_input = move_on(leave(1 - chip, BF), total_last, total_hidden, total_two)
    far_input = swap(far_input, "tensor", 2)
    near_input, early_totals, far_result_half = move_on(
        (leave(chip, F32), early_totals, far_result_half), total_last, total_hidden
    )
    far_input = move_on(far_input, total_last, total_hidden, total_two)
    while total_two.todo:
        far_input = move_on(far_input, total_two)
    totals_two = total_two.block
    grad_heads_in_two = turned(totals_two[:in_rows])
    grad_rows = unfold(totals_two[in_rows:])
    far_input = far_input.astype(F32)
    grad_input = jnp.where(
        chip == 0, jnp.stack([near_input, far_input]), jnp.stack([far_input, near_input])
    )
    result_pair = jnp.where(
        chip == 0,
        jnp.stack([result_half, far_result_half]),
        jnp.stack([far_result_half, result_half]),
    )
    other_pair = swap(result_pair, "tensor", 1)
    output = jnp.where(
        core == 0,
        jnp.concatenate([result_pair, other_pair], 1),
        jnp.concatenate([other_pair, result_pair], 1),
    ).astype(F32)
    early = [item.astype(F32) for item in early_totals]
    output, grad_input, grad_heads_in_two, grad_rows, early = move_on(
        (output, grad_input, grad_heads_in_two, grad_rows, early), total_last, total_hidden
    )
    while total_last.todo or total_hidden.todo:
        output = move_on(output, total_last, total_hidden)
    totals_last, totals_hidden_one = total_last.block, total_hidden.block
    gains = totals_last[4 * HD :].astype(F32)
    gains = gains + swap(gains, "tensor", 1)
    gains = (gains + swap(gains, "tensor", 2)).reshape(-1)
    return (
        output[:, None],
        grad_input[:, None],
        gains[:width],
        turned(totals_last[:heads_rows]),
        totals_last[heads_rows : 4 * HD].astype(F32),
        gains[width : 2 * width],
        totals_hidden_one[:width].astype(F32),
        totals_hidden_one[width:].astype(F32),
        gains[2 * width : 3 * width],
        grad_heads_in_two,
        grad_rows[-skip_rows:],
        grad_rows[:-skip_rows],
        gains[3 * width : 3 * width + wide],
        *early,
    )

def solution(mesh):
    return jax.shard_map(
        per_device,
        mesh=mesh,
        in_specs=(
            P(None, "clip", None, None),
            P(),
            P(None, None, "tensor"),
            P("tensor", None),
            P(),
            P(None, "tensor"),
            P("tensor", None),
            P(),
            P(None, None, "tensor"),
            P("tensor", None),
            P("tensor", None),
            P(),
            P(None, "tensor"),
            P("tensor", None),
            P(),
            P(),
            P(None, "clip", None, None),
        ),
        out_specs=(
            P(None, "clip", None, None),
            P(None, "clip", "tensor", None),
            P(),
            P(None, None, "tensor"),
            P("tensor", None),
            P(),
            P(None, "tensor"),
            P("tensor", None),
            P(),
            P(None, None, "tensor"),
            P("tensor", None),
            P("tensor", None),
            P(),
            P(None, "tensor"),
            P("tensor", None),
        ),
        check_vma=False,
    )
```

```python
import functools

import jax
import jax.numpy as jnp
from jax import lax
from jax.experimental import pallas as pl
from jax.experimental.pallas import tpu as pltpu
from jax.sharding import PartitionSpec as P

HD = 96
PAD = 128
TOK_LOW = 1052
EPSILON = 1e-06
MASKED_SCORE = -1e30
LOG2E = 1.4426950408889634
LN2 = 0.6931471805599453
SCALING = HD ** (-0.5)
BF = jnp.bfloat16
F32 = jnp.float32
MIB = 2**20
LARGE_MIB = 44
SMALL_MIB = 44
FFN_MIB = 20
EXIT_MIB = 60
COST = 1.0
GAIN_ROWS = 16
PIECE = 256
HIDDEN_SLABS = 2

NN = (((1,), (0,)), ((), ()))
NT = (((1,), (1,)), ((), ()))
TN = (((0,), (0,)), ((), ()))


def dot(left, right, form=NN):
    return lax.dot_general(left, right, form, preferred_element_type=F32)


def rms_factor(values):
    return lax.rsqrt(jnp.mean(values * values, -1, keepdims=True) + EPSILON)


def norm_grads(values, gain, grad):
    factor = rms_factor(values)
    scaled = values * factor
    term = grad * gain
    inner = jnp.mean(scaled * term, -1, keepdims=True)
    return factor * (term - scaled * inner), grad * scaled


def gelu_parts(values):
    root = 0.7978845608028654
    square = values * values
    tanh = jnp.tanh(values * (root + (root * 0.044715) * square))
    half = 0.5 + 0.5 * tanh
    slope = half + (0.5 * values) * (1.0 - tanh * tanh) * (root + (3 * root * 0.044715) * square)
    return values * half, slope


def gelu_only(values):
    root = 0.7978845608028654
    tanh = jnp.tanh(values * (root + (root * 0.044715) * (values * values)))
    return values * (0.5 + 0.5 * tanh)


def split_three(row):
    high = row.astype(BF).astype(F32)
    rest = row - high
    middle = rest.astype(BF).astype(F32)
    return high, middle, rest - middle


def call(body, name, grid, in_specs, out_specs, out_shape, scratch=(), prefetch=0, vmem=SMALL_MIB, us=1, aliases=()):
    return pl.pallas_call(
        body,
        name=name,
        grid_spec=pltpu.PrefetchScalarGridSpec(
            num_scalar_prefetch=prefetch,
            grid=grid,
            in_specs=in_specs,
            out_specs=out_specs,
            scratch_shapes=list(scratch),
        ),
        out_shape=out_shape,
        input_output_aliases=dict(aliases),
        compiler_params=pltpu.CompilerParams(vmem_limit_bytes=vmem * MIB),
        cost_estimate=pl.CostEstimate(
            flops=int(us * COST * 1.15e9), bytes_accessed=MIB // 4, transcendentals=0
        ),
    )


def whole(shape):
    return pl.BlockSpec(shape, lambda *_: (0,) * len(shape))


def shape_of(shape, dtype):
    return jax.ShapeDtypeStruct(shape, dtype)


def in_hbm(shape, dtype):
    return pltpu.HBM(shape, dtype)


def lane_scratch(rows, width):
    return pltpu.VMEM((width // PAD, rows, PAD), F32)


def slabs_of(block, lanes):
    parts = lanes.shape[0]
    rows = block.shape[0] // 4
    for part in range(parts):
        lanes[part] = block[:, part * PAD : (part + 1) * PAD]
    return [
        jnp.concatenate([lanes[part, pl.ds(s, rows, stride=4), :] for part in range(parts)], 1)
        for s in range(4)
    ]


def half_rows(core, half):
    return pl.ds(pl.multiple_of(core * half, half), half)


def half_block(rows, width, steps):
    per_half = steps // 2

    def place(step, _, core):
        return jnp.clip(step - per_half * core[0], 0, per_half - 1), 0

    return pl.BlockSpec((rows // steps, width), place)


def keep_half(core, step, steps, target, block):
    @pl.when(step // (steps // 2) == core[0])
    def _():
        target[...] = block


def entry_body(_, half, x_ref, gain_ref, *refs):
    normed_ref, factor_ref, pooled_ref, lanes = refs[-4:]
    total = None
    slabs = slabs_of(x_ref[0, 0], lanes)
    for slab in range(4):
        values = slabs[slab]
        factor = rms_factor(values)
        factor_ref[slab] = jnp.broadcast_to(factor, factor_ref.shape[1:])
        normed = (values * factor * gain_ref[...]).astype(BF)
        normed_ref[slab] = normed
        total = plus(total, normed.astype(F32))
    pooled_ref[...] = (total * 0.25).astype(BF)


def entry_norm(micro, half, tokens, gain, earlier=()):
    length, width = tokens.shape[2:]
    rows = length // 4
    block = rows // 4
    return call(
        entry_body,
        "entry_norm",
        (2,),
        [
            pl.BlockSpec((1, 1, 4 * block, width), lambda i, m, h: (m[0], 0, 2 * h[0] + i, 0)),
            whole((1, width)),
        ]
        + [pl.BlockSpec(memory_space=pl.ANY)] * len(earlier),
        [
            pl.BlockSpec((4, block, width), lambda i, m, h: (0, 2 * h[0] + i, 0)),
            pl.BlockSpec((4, block, PAD), lambda i, m, h: (0, 2 * h[0] + i, 0)),
            pl.BlockSpec((block, width), lambda i, *_: (i, 0)),
        ],
        [
            shape_of((4, rows, width), BF),
            in_hbm((4, rows, PAD), F32),
            shape_of((rows // 2, width), BF),
        ],
        scratch=[lane_scratch(4 * block, width)],
        prefetch=2,
        vmem=EXIT_MIB,
        us=3,
        aliases=[(4 + index, index) for index in range(len(earlier))],
    )(micro, half, tokens, gain.reshape(1, -1), *earlier)


def own_limit(place, resolution, length):
    return jnp.where(resolution[place[1], place[0]] == 1, length, TOK_LOW)


def memory_limit(place, resolution, carried, length):
    before = resolution[place[1], jnp.maximum(place[0] - 1, 0)]
    usable = (carried[place[1], place[0]] == 1) & (place[0] > 0)
    return jnp.where(usable, jnp.where(before == 1, length, TOK_LOW), 0)


def make_pair(limit, offset, source, weights):
    rows = source.shape[0]
    place = lax.broadcasted_iota(jnp.int32, (rows, 1), 0) * 4 + offset
    lane = lax.broadcasted_iota(jnp.int32, (rows, PAD), 1)
    bias = jnp.where(place < limit, 0.0, MASKED_SCORE)
    both = dot(source, weights[PAD:], NT)
    keys = jnp.where(lane < HD, both[:, :PAD], jnp.where(lane == HD, bias, 1.0))
    values = jnp.where(lane < HD, both[:, PAD:], 1.0)
    return keys.astype(BF), values.astype(BF)


def own_pairs_body(place, resolution, _, normed, weights, *results):
    limit = own_limit(place, resolution, 4 * normed.shape[1])
    for head in range(weights.shape[0]):
        parts = make_pair(limit, pl.program_id(0), normed[0], weights[head])
        for result, part in zip(results, parts):
            result[head, 0] = part


def pair_shapes(rows):
    return [(rows, PAD), (rows, PAD)]


def own_pairs(limits, normed, weights):
    _, rows, width = normed.shape
    heads = weights.shape[0]
    return call(
        own_pairs_body,
        "own_pairs",
        (4,),
        [pl.BlockSpec((1, rows, width), lambda i, *_: (i, 0, 0)), whole(weights.shape)],
        [
            pl.BlockSpec((heads, 1) + shape, lambda i, *_: (0, i, 0, 0))
            for shape in pair_shapes(rows)
        ],
        [shape_of((heads, 4) + shape, BF) for shape in pair_shapes(rows)],
        prefetch=3,
        us=6,
    )(*limits, normed, weights)


def query_tail(rows, parts):
    index = lax.broadcasted_iota(jnp.int32, (PAD - HD, rows), 0)
    tail = jnp.where(index == 0, 1.0, 0.0)
    for step, part in enumerate(parts):
        tail = jnp.where(index == step + 1, -part, tail)
    return tail.astype(BF)


def ask(source, weights):
    query = (dot(weights[:HD], source, NT) * (SCALING * LOG2E)).astype(BF)
    return query, jnp.concatenate([query, query_tail(query.shape[1], ())], 0)


def score_rows(asked, keys):
    parts = range(asked.shape[1] // PIECE)
    return [
        dot(keys(chunk)[part * PIECE : (part + 1) * PIECE], asked)
        for chunk in range(5)
        for part in parts
    ]


def attend_rows(query, scores, values):
    rows = query.shape[1]
    parts = rows // PIECE
    top = functools.reduce(jnp.maximum, [jnp.max(item, 0, keepdims=True) for item in scores])
    result = None
    for index, item in enumerate(scores):
        raised = jnp.exp2(item - top).astype(BF)
        part = index % parts
        term = dot(values(index // parts)[part * PIECE : (part + 1) * PIECE], raised, TN)
        result = term if result is None else result + term
    summed = result[HD : HD + 1]
    heads = (result[:HD] / summed).astype(BF)
    logsum = top + jnp.log2(summed)
    return heads, jnp.concatenate([query, query_tail(rows, split_three(logsum))], 0)


def chosen(own, memory, head):
    return lambda chunk: own[head, chunk] if chunk < 4 else memory[head]


def join_halves(core, mine, theirs, target):
    half = mine.shape[0]
    target[half_rows(core, half)] = mine[...]
    target[half_rows(1 - core, half)] = theirs[...]


def attend_one_body(
    place, resolution, carried, normed, mine, theirs, weights, out_weights, own_keys, own_values,
    memory, keys, values, queries_t, heads_t, partial,
):
    @pl.when(pl.program_id(0) == 0)
    def _():
        join_halves(place[2], mine, theirs, memory)
        limit = memory_limit(place, resolution, carried, 4 * memory.shape[0])
        for head in range(2):
            keys[head], values[head] = make_pair(limit, 0, memory[...], weights[head])

    total = None
    queries = [ask(normed[0], weights[head]) for head in range(2)]
    scores = [score_rows(queries[head][1], chosen(own_keys, keys, head)) for head in range(2)]
    for head in range(2):
        heads, asked = attend_rows(
            queries[head][0], scores[head], chosen(own_values, values, head)
        )
        heads_t[head] = heads
        queries_t[head] = asked
        term = dot(heads, out_weights[head], TN)
        total = term if total is None else total + term
    partial[0] = total.astype(BF)


def attend_one(limits, normed, mine, theirs, weights, out_weights, own_keys, own_values):
    _, rows, width = normed.shape
    heads = weights.shape[0]
    memory_shapes = [(heads,) + shape for shape in pair_shapes(rows)]
    return call(
        attend_one_body,
        "attend_one",
        (4,),
        [
            pl.BlockSpec((1, rows, width), lambda i, *_: (i, 0, 0)),
            whole(mine.shape),
            whole(theirs.shape),
            whole(weights.shape),
            whole(out_weights.shape),
            whole(own_keys.shape),
            whole(own_values.shape),
        ],
        [whole((rows, width))]
        + [whole(shape) for shape in memory_shapes]
        + [
            pl.BlockSpec((heads, PAD, rows), lambda i, *_: (0, 0, i)),
            pl.BlockSpec((heads, HD, rows), lambda i, *_: (0, 0, i)),
            pl.BlockSpec((1, rows, width), lambda i, *_: (i, 0, 0)),
        ],
        [shape_of((rows, width), BF)]
        + [shape_of(shape, BF) for shape in memory_shapes]
        + [
            shape_of((heads, PAD, 4 * rows), BF),
            shape_of((heads, HD, 4 * rows), BF),
            shape_of((4, rows, width), BF),
        ],
        prefetch=3,
        vmem=LARGE_MIB,
        us=22,
    )(*limits, normed, mine, theirs, weights, out_weights, own_keys, own_values)


def attend_two_body(
    place, resolution, carried, mine, theirs, pooled, weights, out_weights, skip, own_keys, own_values,
    memory, keys, values, queries_t, heads_t, partial, total,
):
    step = pl.program_id(0)

    @pl.when(step == 0)
    def _():
        join_halves(place[2], mine, theirs, memory)
        total[...] = dot(pooled[...], skip[...])

    limit = memory_limit(place, resolution, carried, 4 * memory.shape[0])
    here = range(weights.shape[0])
    queries = [ask(pooled[...], weights[head]) for head in here]
    for head in here:
        keys[head], values[head] = make_pair(limit, 0, memory[...], weights[head])
    scores = [score_rows(queries[head][1], chosen(own_keys, keys, head)) for head in here]
    for head in here:
        heads, asked = attend_rows(
            queries[head][0], scores[head], chosen(own_values, values, head)
        )
        heads_t[head] = heads
        queries_t[head] = asked
        total[...] += dot(heads, out_weights[head], TN)

    @pl.when(step == pl.num_programs(0) - 1)
    def _():
        partial[...] = total[...].astype(BF)


def attend_two(limits, mine, theirs, pooled, weights, out_weights, skip, own_keys, own_values):
    rows, width = pooled.shape
    heads = weights.shape[0]
    wide = out_weights.shape[2]

    def each(*shape):
        return pl.BlockSpec((2,) + shape, lambda h, *_: (h,) + (0,) * len(shape))

    results = pair_shapes(rows) + [(PAD, rows), (HD, rows)]
    return call(
        attend_two_body,
        "attend_two",
        (heads // 2,),
        [
            whole(mine.shape),
            whole(theirs.shape),
            whole((rows, width)),
            each(*weights.shape[1:]),
            each(HD, wide),
            whole(skip.shape),
            each(4, rows, PAD),
            each(4, rows, PAD),
        ],
        [whole((rows, width))] + [each(*shape) for shape in results] + [whole((rows, wide))],
        [shape_of((rows, width), BF)]
        + [shape_of((heads,) + shape, BF) for shape in results]
        + [shape_of((rows, wide), BF)],
        scratch=[pltpu.VMEM((rows, wide), F32)],
        prefetch=3,
        vmem=LARGE_MIB,
        us=16,
    )(*limits, mine, theirs, pooled, weights, out_weights, skip, own_keys, own_values)


def grad_chunk(keys, values, asked, given):
    chances = jnp.exp2(dot(keys, asked))
    spread = dot(values, given)
    grad_scores = (chances * spread).astype(BF)
    grad_values = dot(chances.astype(BF), given, NT)
    grad_keys = dot(grad_scores, asked, NT)
    return grad_keys, grad_values, dot(keys, grad_scores, TN)[:HD]


def given_rows(out_weights, grad, heads):
    back = dot(out_weights, grad, NT).astype(BF)
    inner = jnp.sum(back.astype(F32) * heads.astype(F32), 0, keepdims=True)
    high, middle, low = split_three(inner)
    index = lax.broadcasted_iota(jnp.int32, (PAD - HD, grad.shape[0]), 0)
    tail = jnp.where(index == 0, -high, jnp.where(index == 1, -middle, jnp.where(index == 2, -low, 0.0)))
    return jnp.concatenate([back, tail.astype(BF)], 0)


def pair_of(grad_keys, grad_values):
    return jnp.concatenate([(grad_keys * LN2).astype(BF), grad_values.astype(BF)], 1)


def plus(total, term):
    return term if total is None else total + term


class Kept:
    def __init__(self, refs, head):
        own_keys, own_values, keys, values, self.queries, self.heads = refs
        self.keys = chosen(own_keys, keys, head)
        self.values = chosen(own_values, values, head)
        self.head = head

    def grads(self, chunk, given):
        return grad_chunk(
            self.keys(chunk), self.values(chunk), self.queries[self.head], given
        )

    def given(self, out_weights, branch):
        return given_rows(out_weights[self.head], branch, self.heads[self.head])


def put_head(target, head, heads, grad_query, grad_pair, columns):
    width = target.shape[1]
    parts = [grad_query, grad_pair[:HD], grad_pair[PAD : PAD + HD]]
    sides = [columns[:, side : side + width] for side in range(0, columns.shape[1], width)]
    starts = [(index * heads + head) * HD for index in range(3)]
    starts += [(3 * heads + head * len(sides) + index) * HD for index in range(len(sides))]
    for start, part in zip(starts, parts + sides):
        target[pl.ds(pl.multiple_of(start, 32), HD)] = part.astype(BF)


def put_skip(target, start, columns, share):
    width = target.shape[1]
    for index, side in enumerate(range(0, columns.shape[1], width)):
        rows = columns[pl.ds(pl.multiple_of(share * HD, 32), HD), side : side + width]
        target[start + index * HD : start + (index + 1) * HD] = rows


def two_first_body(
    place, after, mine, theirs, cotangent, gain, normed, memory, pooled, weights, out_weights, skip,
    *refs
):
    kept, results, scratch = Kept(refs[:6], 0), refs[6:16], refs[16:]
    (branch, grad_gain, own_skip, grad_rows, grad_pool, memory_mine, memory_theirs, grad_weights,
     query_memory, pair_memory) = results
    total, columns = scratch
    step = pl.program_id(0)
    core, share = place[1], place[2]
    wide = after.shape[1]
    width = pooled.shape[1]
    sides = wide // width
    head_rows = (3 + sides) * HD

    @pl.when(step == 0)
    def _():
        first = jnp.where(core == 0, mine[...], theirs[...]).astype(F32)
        second = jnp.where(core == 0, theirs[...], mine[...]).astype(F32)
        arrived = jnp.concatenate([first, second], 0)
        back, terms = norm_grads(after[...], gain[...], arrived)
        grad_gain[...] = jnp.sum(terms, 0, keepdims=True)
        branch[...] = (cotangent[0, 0] + back).astype(BF)
        columns[...] = dot(pooled[...], branch[...], TN).astype(BF)
        put_skip(grad_weights, 2 * head_rows, columns, share ^ 2)
        put_skip(own_skip, 0, columns, share)
        grad_pool[...] = dot(branch[...], skip[...], NT)
        total[...] = jnp.zeros_like(total)

    given = kept.given(out_weights, branch[...])

    @pl.when(step < 2)
    def _():
        grad_query, grad_pair = None, None
        for chunk in range(5):
            grad_keys, grad_values, term = kept.grads(chunk, given)
            grad_query = plus(grad_query, term)
            pair = pair_of(grad_keys, grad_values)
            total[chunk] += dot(pair, weights[0, PAD:])
            source = normed[chunk] if chunk < 4 else memory[...]
            grad_pair = plus(grad_pair, dot(pair, source, TN))
        grad_query = (grad_query * SCALING).astype(BF)
        grad_pool[...] += dot(grad_query, weights[0, :HD], TN)
        put_head(
            grad_weights, step, 2, dot(grad_query, pooled[...]), grad_pair,
            dot(kept.heads[0], branch[...]),
        )

    @pl.when(step >= 2)
    def _():
        grad_keys, grad_values, term = kept.grads(4, given)
        query_memory[0] = term
        pair = pair_of(grad_keys, grad_values)
        total[4] += dot(pair, weights[0, PAD:])
        pair_memory[0] = dot(pair, memory[...], TN)

    @pl.when(step == 3)
    def _():
        half = memory_mine.shape[0]
        for chunk in range(4):
            grad_rows[chunk] = total[chunk].astype(BF)
        memory_mine[...] = total[4, half_rows(core, half)].astype(BF)
        memory_theirs[...] = total[4, half_rows(1 - core, half)].astype(BF)


def two_second_body(
    branch, normed, pooled, weights, out_weights, earlier_rows, earlier_pool, query_memory,
    pair_memory, own_skip, *refs
):
    kept, (grad_rows, grad_weights, total, total_pool) = Kept(refs[:6], 0), refs[6:]
    step = pl.program_id(0)
    head_rows = (grad_weights.shape[0] - own_skip.shape[0]) // 2

    @pl.when(step == 0)
    def _():
        grad_weights[2 * head_rows :] = own_skip[...]
        total_pool[...] = earlier_pool[...]
        for chunk in range(4):
            total[chunk] = earlier_rows[chunk].astype(F32)

    given = kept.given(out_weights, branch[...])
    grad_query, grad_pair = query_memory[0], pair_memory[0]
    for chunk in range(4):
        grad_keys, grad_values, term = kept.grads(chunk, given)
        grad_query = grad_query + term
        pair = pair_of(grad_keys, grad_values)
        total[chunk] += dot(pair, weights[0, PAD:])
        grad_pair = grad_pair + dot(pair, normed[chunk], TN)
    grad_query = (grad_query * SCALING).astype(BF)
    total_pool[...] += dot(grad_query, weights[0, :HD], TN)
    put_head(
        grad_weights, step, 2, dot(grad_query, pooled[...]), grad_pair,
        dot(kept.heads[0], branch[...]),
    )

    @pl.when(step == pl.num_programs(0) - 1)
    def _():
        for chunk in range(4):
            grad_rows[chunk] = (total[chunk] + 0.25 * total_pool[...]).astype(BF)


def kept_specs(each, rows, own=None):
    pair = pair_shapes(rows)
    return [(own or each)(4, *shape) for shape in pair] + [each(*shape) for shape in pair]


def two_first(
    place, after, mine, theirs, cotangent, gain, normed, memory, pooled, weights, out_weights, skip, kept
):
    _, rows, width = normed.shape
    wide = out_weights.shape[2]
    sides = wide // width
    all_rows = 2 * (3 + sides) * HD + sides * HD

    def each(*shape):
        return pl.BlockSpec((1,) + shape, lambda h, _: ((h + 2) % 4,) + (0,) * len(shape))

    def own(*shape):
        return pl.BlockSpec((1,) + shape, lambda h, _: (jnp.minimum(h, 1) + 2,) + (0,) * len(shape))

    def late(*shape):
        return pl.BlockSpec((1,) + shape, lambda h, _: (jnp.maximum(h, 2) - 2,) + (0,) * len(shape))

    return call(
        two_first_body,
        "back_two_first",
        (4,),
        [
            whole((rows, wide)),
            whole(mine.shape),
            whole(theirs.shape),
            pl.BlockSpec((1, 1, rows, wide), lambda h, m: (m[0], 0, 0, 0)),
            whole((1, wide)),
            whole((4, rows, width)),
            whole((rows, width)),
            whole((rows, width)),
            each(*weights.shape[1:]),
            each(HD, wide),
            whole(skip.shape),
        ]
        + kept_specs(each, rows, own)
        + [each(PAD, rows), each(HD, rows)],
        [
            whole((rows, wide)),
            whole((1, wide)),
            whole((sides * HD, width)),
            whole((4, rows, width)),
            whole((rows, width)),
            whole((rows // 2, width)),
            whole((rows // 2, width)),
            whole((all_rows, width)),
            late(HD, rows),
            late(2 * PAD, width),
        ],
        [
            shape_of((rows, wide), BF),
            shape_of((1, wide), F32),
            shape_of((sides * HD, width), BF),
            shape_of((4, rows, width), BF),
            shape_of((rows, width), F32),
            shape_of((rows // 2, width), BF),
            shape_of((rows // 2, width), BF),
            shape_of((all_rows, width), BF),
            shape_of((2, HD, rows), F32),
            shape_of((2, 2 * PAD, width), F32),
        ],
        scratch=[pltpu.VMEM((5, rows, width), F32), pltpu.VMEM((width, wide), BF)],
        prefetch=1,
        vmem=LARGE_MIB,
        us=23,
    )(
        place, after, mine, theirs, cotangent, gain.reshape(1, -1), normed, memory, pooled, weights,
        out_weights, skip, *kept,
    )


def two_second(
    branch, normed, pooled, weights, out_weights, earlier_rows, earlier_pool, query_memory,
    pair_memory, own_skip, kept
):
    _, rows, width = normed.shape
    wide = out_weights.shape[2]
    all_rows = 2 * (3 + wide // width) * HD + own_skip.shape[0]

    def each(*shape):
        return pl.BlockSpec((1,) + shape, lambda h: (h,) + (0,) * len(shape))

    return call(
        two_second_body,
        "back_two_second",
        (2,),
        [
            whole((rows, wide)),
            whole((4, rows, width)),
            whole((rows, width)),
            each(*weights.shape[1:]),
            each(HD, wide),
            whole((4, rows, width)),
            whole((rows, width)),
            each(HD, rows),
            each(2 * PAD, width),
            whole(own_skip.shape),
        ]
        + kept_specs(each, rows)
        + [each(PAD, rows), each(HD, rows)],
        [whole((4, rows, width)), whole((all_rows, width))],
        [shape_of((4, rows, width), BF), shape_of((all_rows, width), BF)],
        scratch=[pltpu.VMEM((4, rows, width), F32), pltpu.VMEM((rows, width), F32)],
        vmem=LARGE_MIB,
        us=14,
    )(
        branch, normed, pooled, weights, out_weights, earlier_rows, earlier_pool, query_memory,
        pair_memory, own_skip, *kept,
    )


def one_first_body(
    core, grad_two, after, own_part, other_part, gain, normed, memory, weights, out_weights, *refs
):
    kept, near_kept = Kept(refs[:6], 1), Kept(refs[:6], 0)
    (grad_one, branch_ref, grad_gain, grad_rows, memory_mine, memory_theirs, grad_weights,
     query_memory, pair_memory, memory_gain) = refs[6:16]
    total, total_keys, total_values, total_query, total_out, near_keys, near_values, rows_memory = (
        refs[16:]
    )
    slab = pl.program_id(0)

    @pl.when(slab == 0)
    def _():
        for item in (grad_gain, total_keys, total_values, total_query, total_out, near_keys, near_values):
            item[...] = jnp.zeros_like(item)

    arrived = own_part[0].astype(F32) + other_part[0].astype(F32)
    back, terms = norm_grads(after[0], gain[...], arrived)
    grad_gain[...] += jnp.sum(terms, 0, keepdims=True)
    state = grad_two[0] + back
    grad_one[0] = state
    branch = state.astype(BF)
    branch_ref[0] = branch
    given = kept.given(out_weights, branch)
    grad_query = None
    for chunk in range(5):
        grad_keys, grad_values, term = kept.grads(chunk, given)
        total_keys[chunk] += grad_keys
        total_values[chunk] += grad_values
        grad_query = plus(grad_query, term)
    grad_keys, grad_values, term = near_kept.grads(4, near_kept.given(out_weights, branch))
    near_keys[...] += grad_keys
    near_values[...] += grad_values
    query_memory[...] = term
    grad_query = (grad_query * SCALING).astype(BF)
    total_out[...] += dot(kept.heads[1], branch)
    total_query[...] += dot(grad_query, normed[slab])
    total[slab] = dot(grad_query, weights[1, :HD], TN)

    @pl.when(slab == pl.num_programs(0) - 1)
    def _():
        pair = pair_of(near_keys[...], near_values[...])
        pair_memory[...] = dot(pair, memory[...], TN)
        near_rows = dot(pair, weights[0, PAD:])
        grad_pair = None
        for chunk in range(5):
            pair = pair_of(total_keys[chunk], total_values[chunk])
            rows = dot(pair, weights[1, PAD:])
            source = normed[chunk] if chunk < 4 else memory[...]
            grad_pair = plus(grad_pair, dot(pair, source, TN))
            if chunk < 4:
                grad_rows[chunk] = (total[chunk] + rows).astype(BF)
            else:
                rows = near_rows + rows
                memory_gain[...] = jnp.sum(rows * memory[...].astype(F32), 0, keepdims=True)
                rows_memory[...] = rows
        half = memory_mine.shape[0]
        memory_mine[...] = rows_memory[half_rows(core[0], half)].astype(BF)
        memory_theirs[...] = rows_memory[half_rows(1 - core[0], half)].astype(BF)
        grad_weights[:HD] = total_query[...].astype(BF)
        grad_weights[HD : 2 * HD] = grad_pair[:HD].astype(BF)
        grad_weights[2 * HD : 3 * HD] = grad_pair[PAD : PAD + HD].astype(BF)
        grad_weights[3 * HD : 4 * HD] = total_out[...].astype(BF)
        grad_weights[4 * HD :] = jnp.zeros_like(grad_weights[4 * HD :])


def one_second_body(
    core, branch_ref, normed, weights, out_weights, earlier_rows, query_memory, pair_memory,
    memory_gain, gain, other_gains, *refs
):
    kept, (mine, theirs, grad_weights) = Kept(refs[:6], 0), refs[6:9]
    total, total_keys, total_values, total_query, total_out = refs[9:]
    slab = pl.program_id(0)

    @pl.when(slab == 0)
    def _():
        for item in (total_keys, total_values, total_query, total_out):
            item[...] = jnp.zeros_like(item)

    branch = branch_ref[0]
    given = kept.given(out_weights, branch)
    grad_query = query_memory[...]
    for chunk in range(4):
        grad_keys, grad_values, term = kept.grads(chunk, given)
        total_keys[chunk] += grad_keys
        total_values[chunk] += grad_values
        grad_query = grad_query + term
    grad_query = (grad_query * SCALING).astype(BF)
    total_out[...] += dot(kept.heads[0], branch)
    total_query[...] += dot(grad_query, normed[slab])
    total[slab] = dot(grad_query, weights[0, :HD], TN)

    @pl.when(slab == pl.num_programs(0) - 1)
    def _():
        grad_pair = pair_memory[...]
        gain_terms = memory_gain[...]
        share = mine.shape[2]
        for chunk in range(4):
            pair = pair_of(total_keys[chunk], total_values[chunk])
            rows = dot(pair, weights[0, PAD:]) + earlier_rows[chunk].astype(F32)
            rows = total[chunk] + rows
            gain_terms += jnp.sum(rows * normed[chunk].astype(F32), 0, keepdims=True)
            total[chunk] = rows
            for chip in range(mine.shape[1]):
                for target, which in ((mine, core[0]), (theirs, 1 - core[0])):
                    start = pl.multiple_of((2 * chip + which) * share, share)
                    target[chunk, chip] = total[chunk, pl.ds(start, share)].astype(BF)
            grad_pair = grad_pair + dot(pair, normed[chunk], TN)
        gains = jnp.concatenate([gain_terms / gain[...], other_gains[1:]], 0)
        grad_weights[4 * HD :] = gains.astype(BF)
        grad_weights[:HD] = total_query[...].astype(BF)
        grad_weights[HD : 2 * HD] = grad_pair[:HD].astype(BF)
        grad_weights[2 * HD : 3 * HD] = grad_pair[PAD : PAD + HD].astype(BF)
        grad_weights[3 * HD : 4 * HD] = total_out[...].astype(BF)


def one_specs(rows):
    def heads(*shape):
        return whole((2,) + shape)

    return kept_specs(heads, rows) + [
        pl.BlockSpec((2, PAD, rows), lambda i, *_: (0, 0, i)),
        pl.BlockSpec((2, HD, rows), lambda i, *_: (0, 0, i)),
    ]


def one_scratch(rows, width, chunks):
    return [
        pltpu.VMEM((4, rows, width), F32),
        pltpu.VMEM((chunks, rows, PAD), F32),
        pltpu.VMEM((chunks, rows, PAD), F32),
        pltpu.VMEM((HD, width), F32),
        pltpu.VMEM((HD, width), F32),
    ]


def one_first(
    core, grad_two, after, own_part, other_part, gain, normed, memory, weights, out_weights, kept
):
    _, rows, width = grad_two.shape
    slab = pl.BlockSpec((1, rows, width), lambda i, *_: (i, 0, 0))
    return call(
        one_first_body,
        "back_one_first",
        (4,),
        [slab, slab, slab, slab, whole((1, width)), whole((4, rows, width)), whole((rows, width))]
        + [whole(weights.shape), whole(out_weights.shape)]
        + one_specs(rows),
        [
            slab,
            slab,
            whole((1, width)),
            whole((4, rows, width)),
            whole((rows // 2, width)),
            whole((rows // 2, width)),
            whole((4 * HD + GAIN_ROWS, width)),
            pl.BlockSpec((HD, rows), lambda i, *_: (0, i)),
            whole((2 * PAD, width)),
            whole((1, width)),
        ],
        [
            shape_of((4, rows, width), F32),
            shape_of((4, rows, width), BF),
            shape_of((1, width), F32),
            shape_of((4, rows, width), BF),
            shape_of((rows // 2, width), BF),
            shape_of((rows // 2, width), BF),
            shape_of((4 * HD + GAIN_ROWS, width), BF),
            in_hbm((HD, 4 * rows), F32),
            shape_of((2 * PAD, width), F32),
            shape_of((1, width), F32),
        ],
        scratch=one_scratch(rows, width, 5)
        + [pltpu.VMEM((rows, PAD), F32), pltpu.VMEM((rows, PAD), F32), pltpu.VMEM((rows, width), F32)],
        prefetch=1,
        vmem=LARGE_MIB,
        us=27,
    )(
        core, grad_two, after, own_part, other_part, gain.reshape(1, -1), normed, memory, weights,
        out_weights, *kept,
    )


def one_second(
    core, branch, normed, weights, out_weights, earlier_rows, query_memory, pair_memory, memory_gain,
    gain, other_gains, kept
):
    _, rows, width = branch.shape
    slab = pl.BlockSpec((1, rows, width), lambda i, *_: (i, 0, 0))
    leaving = (4, 2, rows // 4, width)
    return call(
        one_second_body,
        "back_one_second",
        (4,),
        [
            slab,
            whole((4, rows, width)),
            whole(weights.shape),
            whole(out_weights.shape),
            whole((4, rows, width)),
            pl.BlockSpec((HD, rows), lambda i, *_: (0, i)),
            whole((2 * PAD, width)),
            whole((1, width)),
            whole((1, width)),
            whole(other_gains.shape),
        ]
        + one_specs(rows),
        [whole(leaving), whole(leaving), whole((4 * HD + other_gains.shape[0], width))],
        [
            shape_of(leaving, BF),
            shape_of(leaving, BF),
            shape_of((4 * HD + other_gains.shape[0], width), BF),
        ],
        scratch=one_scratch(rows, width, 4),
        prefetch=1,
        vmem=LARGE_MIB,
        us=18,
    )(
        core, branch, normed, weights, out_weights, earlier_rows, query_memory, pair_memory,
        memory_gain, gain.reshape(1, -1), other_gains, *kept,
    )


def flat(block):
    return block.reshape(block.shape[0] * block.shape[1], block.shape[2])


def hidden_one_body(_, x_ref, own_part, other_part, gain, w_in, w_out, after, partial, lanes):
    tokens = slabs_of(x_ref[0, 0], lanes)
    for pair in range(0, 4, HIDDEN_SLABS):
        slabs = slice(pair, pair + HIDDEN_SLABS)
        state = flat(own_part[slabs].astype(F32) + other_part[slabs].astype(F32))
        state = state + jnp.concatenate(tokens[slabs], 0)
        after[slabs] = state.reshape(HIDDEN_SLABS, -1, state.shape[1])
        normed = (state * rms_factor(state) * gain[...]).astype(BF)
        active = gelu_only(dot(normed, w_in[...], NT)).astype(BF)
        partial[slabs] = dot(active, w_out[...]).astype(BF).reshape(HIDDEN_SLABS, -1, state.shape[1])


def hidden_one(micro, tokens, own_part, other_part, gain, w_in, w_out):
    _, rows, width = own_part.shape
    block = rows // 4
    strip = pl.BlockSpec((4, block, width), lambda i, m: (0, i, 0))
    return call(
        hidden_one_body,
        "hidden_one",
        (4,),
        [
            pl.BlockSpec((1, 1, 4 * block, width), lambda i, m: (m[0], 0, i, 0)),
            strip,
            strip,
            whole((1, width)),
            whole(w_in.shape),
            whole(w_out.shape),
        ],
        [strip, strip],
        [shape_of((4, rows, width), F32), shape_of((4, rows, width), BF)],
        scratch=[lane_scratch(4 * block, width)],
        prefetch=1,
        vmem=LARGE_MIB,
        us=7,
    )(micro, tokens, own_part, other_part, gain.reshape(1, -1), w_in, w_out)


def norm_three_body(_, state, own_part, other_part, gain, *refs):
    after, normed, pooled = refs[-3:]
    total = None
    for slab in range(4):
        values = state[slab] + (own_part[slab].astype(F32) + other_part[slab].astype(F32))
        after[slab] = values
        rows = (values * rms_factor(values) * gain[...]).astype(BF)
        normed[slab] = rows
        total = plus(total, rows.astype(F32))
    pooled[...] = (total * 0.25).astype(BF)


def norm_three(half, state, own_part, other_part, gain, earlier=()):
    _, rows, width = state.shape
    block = rows // 4
    strip = pl.BlockSpec((4, block, width), lambda i, h: (0, 2 * h[0] + i, 0))
    pooled = pl.BlockSpec((block, width), lambda i, h: (2 * h[0] + i, 0))
    return call(
        norm_three_body,
        "norm_three",
        (2,),
        [strip, strip, strip, whole((1, width))]
        + [pl.BlockSpec(memory_space=pl.ANY)] * len(earlier),
        [strip, strip, pooled],
        [
            shape_of((4, rows, width), F32),
            shape_of((4, rows, width), BF),
            shape_of((rows, width), BF),
        ],
        prefetch=1,
        us=3,
        aliases=[(5 + index, index) for index in range(len(earlier))],
    )(half, state, own_part, other_part, gain.reshape(1, -1), *earlier)


def hidden_one_back_body(
    core, after_two, own_part, other_part, mine, theirs, gain_three, after_one, gain_two, w_in, w_out,
    grad_two, partial, grad_own, grad_sent, grad_gain, total_in, total_out,
):
    step = pl.program_id(0)

    @pl.when(step == 0)
    def _():
        total_in[...] = jnp.zeros_like(total_in)
        total_out[...] = jnp.zeros_like(total_out)
        grad_gain[...] = jnp.zeros_like(grad_gain)

    memory = jnp.where(step // 2 == core[0], mine[...], theirs[...]).astype(F32) * 0.25
    width = memory.shape[1]
    for pair in range(0, 4, HIDDEN_SLABS):
        slabs = slice(pair, pair + HIDDEN_SLABS)
        arrived = own_part[slabs].astype(F32) + other_part[slabs].astype(F32) + memory[None]
        back, terms = norm_grads(flat(after_two[slabs]), gain_three[...], flat(arrived))
        grad_gain[...] += jnp.sum(terms, 0, keepdims=True)
        grad_two[slabs] = back.reshape(HIDDEN_SLABS, -1, width)
        branch = back.astype(BF)
        state = flat(after_one[slabs])
        normed = (state * rms_factor(state) * gain_two[...]).astype(BF)
        active, slope = gelu_parts(dot(normed, w_in[...], NT))
        grad_pre = (slope * dot(branch, w_out[...], NT)).astype(BF)
        partial[slabs] = dot(grad_pre, w_in[...]).astype(BF).reshape(HIDDEN_SLABS, -1, width)
        total_out[...] += dot(active.astype(BF), branch, TN)
        total_in[...] += dot(grad_pre, normed, TN)

    @pl.when(step == pl.num_programs(0) - 1)
    def _():
        share = total_in.shape[0] // 2
        for target, start in ((grad_own, 0), (grad_sent, share)):
            target[:share] = jnp.transpose(total_in[start : start + share]).astype(BF)
            target[share:] = total_out[start : start + share].astype(BF)


def hidden_one_back(
    core, after_two, own_part, other_part, mine, theirs, gain_three, after_one, gain_two, w_in, w_out
):
    _, rows, width = after_two.shape
    block = rows // 4
    hidden = w_in.shape[0]
    strip = pl.BlockSpec((4, block, width), lambda i, *_: (0, i, 0))
    memory = pl.BlockSpec((block, width), lambda i, *_: (i % 2, 0))
    return call(
        hidden_one_back_body,
        "hidden_one_back",
        (4,),
        [
            strip,
            strip,
            strip,
            memory,
            memory,
            whole((1, width)),
            strip,
            whole((1, width)),
            whole(w_in.shape),
            whole(w_out.shape),
        ],
        [strip, strip, whole(w_in.shape), whole(w_out.shape), whole((1, width))],
        [
            in_hbm((4, rows, width), F32),
            shape_of((4, rows, width), BF),
            shape_of(w_in.shape, BF),
            shape_of(w_out.shape, BF),
            shape_of((1, width), F32),
        ],
        scratch=[pltpu.VMEM((hidden, width), F32), pltpu.VMEM((hidden, width), F32)],
        prefetch=1,
        us=15,
    )(
        core, after_two, own_part, other_part, mine, theirs, gain_three.reshape(1, -1), after_one,
        gain_two.reshape(1, -1), w_in, w_out,
    )


def norm_four_body(core, own_part, other_part, gain, after, normed_ref, half_ref):
    state = own_part[...].astype(F32) + other_part[...].astype(F32)
    after[...] = state
    normed = (state * rms_factor(state) * gain[...]).astype(BF)
    normed_ref[...] = normed

    @pl.when(pl.program_id(0) == core[0])
    def _():
        half_ref[...] = normed


def norm_four(core, own_part, other_part, gain):
    rows, wide = own_part.shape
    half = rows // 2
    strip = pl.BlockSpec((half, wide), lambda i, _: (i, 0))
    return call(
        norm_four_body,
        "norm_four",
        (2,),
        [strip, strip, whole((1, wide))],
        [strip, strip, whole((half, wide))],
        [shape_of((rows, wide), F32), shape_of((rows, wide), BF), shape_of((half, wide), BF)],
        prefetch=1,
        us=2,
        vmem=FFN_MIB,
    )(core, own_part, other_part, gain.reshape(1, -1))


def hidden_two_body(
    place, first, second, cotangent, w_in, w_out,
    normed_ref, active_ref, grad_pre_ref, grad_mine, grad_theirs, result_mine, result_theirs,
):
    mine = pl.program_id(0) == place[1]
    normed = jnp.where(mine, first[...], second[...])
    normed_ref[...] = normed
    active, slope = gelu_parts(dot(normed, w_in[...]))
    active = active.astype(BF)
    grad_pre = (slope * dot(cotangent[0, 0].astype(BF), w_out[...], NT)).astype(BF)
    grad_normed = dot(grad_pre, w_in[...], NT).astype(BF)
    active_ref[...] = active
    grad_pre_ref[...] = grad_pre
    result = dot(active, w_out[...]).astype(BF)

    @pl.when(mine)
    def _():
        grad_mine[...] = grad_normed
        result_mine[...] = result

    @pl.when(jnp.logical_not(mine))
    def _():
        grad_theirs[...] = grad_normed
        result_theirs[...] = result


def hidden_two(place, first, second, cotangent, w_in, w_out):
    wide, hidden = w_in.shape
    rows = cotangent.shape[2]
    half = rows // 2
    given = pl.BlockSpec((half, wide), lambda i, p: (i if first is second else 0, 0))
    strip = pl.BlockSpec((half, wide), lambda i, p: (i, 0))
    strip_hidden = pl.BlockSpec((half, hidden), lambda i, p: (i, 0))
    return call(
        hidden_two_body,
        "hidden_two",
        (2,),
        [
            given,
            given,
            pl.BlockSpec((1, 1, half, wide), lambda i, p: (p[0], 0, i, 0)),
            whole(w_in.shape),
            whole(w_out.shape),
        ],
        [strip, strip_hidden, strip_hidden] + [whole((half, wide))] * 4,
        [in_hbm((rows, wide), BF), in_hbm((rows, hidden), BF), in_hbm((rows, hidden), BF)]
        + [shape_of((half, wide), BF)] * 2
        + [in_hbm((half, wide), BF)] * 2,
        prefetch=1,
        us=5,
        vmem=FFN_MIB,
    )(place, first, second, cotangent, w_in, w_out)


def hidden_two_weights_body(
    _, own_normed, own_active, own_pre, other_normed, other_active, other_pre, own_cot, other_cot,
    grad_in, grad_out,
):
    grad_in[...] = (
        dot(own_normed[...], own_pre[...], TN) + dot(other_normed[...], other_pre[...], TN)
    ).astype(BF)
    grad_out[...] = (
        dot(own_active[...], own_cot[0, 0].astype(BF), TN)
        + dot(other_active[...], other_cot[0, 0].astype(BF), TN)
    ).astype(BF)


def hidden_two_weights(micros, own, other, cotangent):
    rows, wide = own[0].shape
    hidden = own[1].shape[1]
    parts = 3
    column = pl.BlockSpec((rows, wide // parts), lambda i, m: (0, i))
    column_hidden = pl.BlockSpec((rows, hidden // parts), lambda i, m: (0, i))
    return call(
        hidden_two_weights_body,
        "hidden_two_weights",
        (parts,),
        [
            column,
            column_hidden,
            whole((rows, hidden)),
            column,
            column_hidden,
            whole((rows, hidden)),
            pl.BlockSpec((1, 1, rows, wide), lambda i, m: (m[0], 0, 0, 0)),
            pl.BlockSpec((1, 1, rows, wide), lambda i, m: (m[1], 0, 0, 0)),
        ],
        [
            pl.BlockSpec((wide // parts, hidden), lambda i, m: (i, 0)),
            pl.BlockSpec((hidden // parts, wide), lambda i, m: (i, 0)),
        ],
        [shape_of((wide, hidden), BF), shape_of((hidden, wide), BF)],
        prefetch=1,
        us=5,
        vmem=FFN_MIB,
    )(micros, *own, *other, cotangent, cotangent)


def exit_body(place, normed, factor, grad_one, partial, got, mine, theirs, gain, grad_input, lanes):
    block = mine.shape[0]
    memory = jnp.where(place[1] == place[2], mine[...], theirs[...]).astype(F32) * 0.25
    for slab in range(4):
        term = partial[slab, 0].astype(F32) + got[slab, 0].astype(F32) + memory
        term = term * gain[...]
        scaled = normed[slab].astype(F32) / gain[...]
        inner = jnp.mean(scaled * term, -1, keepdims=True)
        result = grad_one[slab] + factor[slab, :, :1] * (term - scaled * inner)
        for part in range(lanes.shape[0]):
            lanes[part, pl.ds(slab, block, stride=4), :] = result[:, part * PAD : (part + 1) * PAD]
    for part in range(lanes.shape[0]):
        columns = lanes[part].astype(grad_input.dtype)
        grad_input[:, part * PAD : (part + 1) * PAD] = columns


def exit_norm(place, normed, factor, grad_one, partial, got, mine, theirs, gain, dtype):
    _, rows, width = normed.shape
    share = rows
    block = share // 4
    strip = pl.BlockSpec((4, block, width), lambda i, p: (0, p[0], 0))
    leaving = pl.BlockSpec((4, 1, block, width), lambda i, p: (0, p[1], 0, 0))
    memory = pl.BlockSpec((block, width), lambda i, p: (p[2], 0))
    return call(
        exit_body,
        "exit_norm",
        (1,),
        [
            strip,
            pl.BlockSpec((4, block, PAD), lambda i, p: (0, p[0], 0)),
            strip,
            leaving,
            leaving,
            memory,
            memory,
            whole((1, width)),
        ],
        whole((share, width)),
        shape_of((share, width), dtype),
        scratch=[lane_scratch(share, width)],
        prefetch=1,
        vmem=EXIT_MIB,
        us=4,
    )(place, normed, factor, grad_one, partial, got, mine, theirs, gain.reshape(1, -1))


def swap(block, axis, bit):
    return lax.ppermute(block, axis, [(i, i ^ bit) for i in range(lax.axis_size(axis))])


def shifted(block, distance):
    devices = lax.axis_size("clip")
    return lax.ppermute(block, "clip", [(i, (i + distance) % devices) for i in range(devices)])


def after(block, earlier):
    return lax.optimization_barrier((block, earlier))[0]


def in_order(core, mine, theirs):
    ordered = jnp.where(core == 0, jnp.stack([mine, theirs]), jnp.stack([theirs, mine]))
    return ordered.reshape((-1,) + mine.shape[1:])


def share_of(block, core):
    half = block.shape[0] // 2
    return lax.dynamic_slice_in_dim(block, core * half, half, 0)


def together(results, *others):
    return lax.optimization_barrier((results,) + others)


class ClipSum:
    def __init__(self, block, halvings=1):
        clips = lax.axis_size("clip")
        self.index = lax.axis_index("clip")
        steps = [2**k for k in range(clips.bit_length() - 1)]
        halved = steps[:halvings]
        self.todo = [("halve", step) for step in halved] + [("add", step) for step in steps[halvings:]]
        self.todo += [("join", step) for step in reversed(halved)]
        self.block = block
        self.send()

    @classmethod
    def resumed(cls, block, todo, got):
        self = cls.__new__(cls)
        self.index = lax.axis_index("clip")
        self.block, self.todo, self.got = block, list(todo), got
        return self

    def send(self):
        kind, step = self.todo[0]
        bit = self.index // step % 2
        sent = share_of(self.block, 1 - bit) if kind == "halve" else self.block
        self.got = swap(sent, "clip", step)

    def take(self):
        kind, step = self.todo.pop(0)
        bit = self.index // step % 2
        got, self.got = self.got, None
        if kind == "join":
            self.block = in_order(bit, self.block, got)
        else:
            kept = share_of(self.block, bit) if kind == "halve" else self.block
            self.block = plus_rounded(kept, got)

    def step(self):
        self.take()
        if self.todo:
            self.send()

def plus_rounded(own, got):
    return (own.astype(F32) + got.astype(F32)).astype(BF)


def pad_heads(turned):
    widths = [(0, 0)] * (turned.ndim - 2) + [(0, PAD - HD), (0, 0)]
    padded = jnp.pad(turned, widths)
    return padded.reshape(turned.shape[:-3] + (3 * PAD, turned.shape[-1]))


def per_device(
    tokens_in,
    gain_one,
    heads_in_one,
    heads_out_one,
    gain_two,
    hidden_in_one,
    hidden_out_one,
    gain_three,
    heads_in_two,
    skip_weight,
    heads_out_two,
    gain_four,
    hidden_in_two,
    hidden_out_two,
    resolution,
    continues,
    cotangent,
):
    clip_index = lax.axis_index("clip")
    part_index = lax.axis_index("tensor")
    chip, core = part_index // 2, part_index % 2
    micro = chip.astype(jnp.int32).reshape(1)
    core_index = core.astype(jnp.int32).reshape(1)
    length, width = tokens_in.shape[2:]
    rows = length // 4
    wide = heads_out_two.shape[1]

    limits = (jnp.stack([clip_index, chip, core]).astype(jnp.int32), resolution, continues)

    skip_rows = skip_weight.shape[0]
    heads_rows = 3 * HD
    own_one = jnp.concatenate(
        [jnp.transpose(heads_in_one, (1, 2, 0)).reshape(heads_rows, width), heads_out_one], 0
    )
    far_one = swap(own_one, "tensor", 2)

    *first_half, pooled_half = entry_norm(micro, core_index, tokens_in, gain_one)
    normed_one, factor_one, _ = entry_norm(micro, 1 - core_index, tokens_in, gain_one, first_half)
    hidden_in_one, hidden_out_one, heads_in_two = after(
        (hidden_in_one, hidden_out_one, heads_in_two), (normed_one, far_one)
    )
    own_hidden = jnp.stack([jnp.transpose(hidden_in_one), hidden_out_one])
    own_two = jnp.transpose(heads_in_two, (1, 2, 0)).reshape(3, -1, HD, width)
    own_two = jnp.swapaxes(own_two, 0, 1)
    memory_mine = shifted(pooled_half, 1)
    far_hidden = swap(own_hidden, "tensor", 2)
    both_one = jnp.stack([own_one, far_one])
    weights_one = pad_heads(both_one[:, :heads_rows].reshape(2, 3, HD, width))
    out_one = both_one[:, heads_rows:]
    own_kept_one = list(own_pairs(limits, normed_one, weights_one))
    memory_mine, own_kept_one = together(memory_mine, own_kept_one)
    memory_theirs = swap(memory_mine, "tensor", 1)
    memory_one, *kept_one, attn_part = attend_one(
        limits, normed_one, memory_mine, memory_theirs, weights_one, out_one, *own_kept_one,
    )
    kept_one = own_kept_one + kept_one
    attn_part, far_hidden = together(attn_part, far_hidden)
    far_two = swap(after(own_two, far_hidden), "tensor", 2)
    w_in_one = jnp.concatenate([own_hidden[0], far_hidden[0]], 0)
    w_out_one = jnp.concatenate([own_hidden[1], far_hidden[1]], 0)
    after_one, ffn_part = hidden_one(
        micro, tokens_in, attn_part, swap(attn_part, "tensor", 1), gain_two, w_in_one, w_out_one
    )
    ffn_part, far_two = together(ffn_part, far_two)
    weights_two = pad_heads(jnp.concatenate([own_two, far_two], 0))
    own_rows = jnp.concatenate([skip_weight, heads_out_two], 0)
    far_rows = swap(after(own_rows, far_two), "tensor", 2)
    ffn_got = swap(ffn_part, "tensor", 1)
    first_half = norm_three(core_index, after_one, ffn_part, ffn_got, gain_three)
    pooled_half = share_of(first_half[2], core)
    after_two, normed_three, pooled_three = norm_three(
        1 - core_index, after_one, ffn_part, ffn_got, gain_three, first_half
    )

    memory_mine = shifted(pooled_half, 1)
    own_kept_two = list(own_pairs(limits, normed_three, weights_two))
    memory_mine, own_kept_two, far_rows = together(memory_mine, own_kept_two, far_rows)
    out_two = jnp.concatenate([own_rows[skip_rows:], far_rows[skip_rows:]], 0).reshape(-1, HD, wide)
    skip = jnp.zeros((width, wide), BF)
    skip = lax.dynamic_update_slice(skip, own_rows[:skip_rows], (part_index * skip_rows, 0))
    skip = lax.dynamic_update_slice(skip, far_rows[:skip_rows], ((part_index ^ 2) * skip_rows, 0))
    memory_theirs = swap(memory_mine, "tensor", 1)
    memory_two, *kept_two, branch_part = attend_two(
        limits, memory_mine, memory_theirs, pooled_three, weights_two, out_two, skip,
        *own_kept_two,
    )
    kept_two = own_kept_two + kept_two
    after_three, normed_four, normed_half = norm_four(
        core_index, branch_part, swap(branch_part, "tensor", 1), gain_four
    )
    far_mine = swap(normed_half, "tensor", 2)
    near_place = jnp.stack([chip, core]).astype(jnp.int32)
    far_place = jnp.stack([1 - chip, core]).astype(jnp.int32)
    *own_ffn, own_mine, own_theirs, result_mine, result_theirs_ = hidden_two(
        near_place, normed_four, normed_four, cotangent, hidden_in_two, hidden_out_two
    )
    far_mine, own_theirs = together(far_mine, own_theirs)
    far_theirs = swap(far_mine, "tensor", 1)
    own_got = swap(own_theirs, "tensor", 1)
    *far_ffn, far_grad_mine, far_grad_theirs, far_result_mine_, far_result_theirs_ = hidden_two(
        far_place, far_mine, far_theirs, cotangent, hidden_in_two, hidden_out_two
    )
    far_sum = plus_rounded(far_grad_mine, swap(far_grad_theirs, "tensor", 1))
    far_sum = swap(far_sum, "tensor", 2)
    w_hidden_two = hidden_two_weights(
        jnp.concatenate([micro, 1 - micro]), own_ffn, far_ffn, cotangent
    )
    far_sum, own_got, w_hidden_two = together(far_sum, own_got, w_hidden_two)
    grad_mine = own_mine.astype(F32) + own_got.astype(F32) + far_sum.astype(F32)
    grad_mine = grad_mine.astype(BF)
    grad_theirs = swap(grad_mine, "tensor", 1)
    early_totals = lax.psum(tuple(w_hidden_two), "clip")
    sides = wide // width
    in_rows = heads_in_two.shape[2] * 3

    def turned(block):
        return jnp.transpose(block.reshape(3, -1, width), (2, 0, 1)).astype(F32)

    def unfold(block):
        block = block.reshape(-1, sides, HD, width).astype(F32)
        return jnp.concatenate([block[:, k] for k in range(sides)], 2).reshape(-1, wide)

    left = []

    def backward():
        place = jnp.stack([chip, core, part_index]).astype(jnp.int32)
        (branch_two, w_gain_four, w_skip, *early, memory_kept, memory_sent, w_two_sent, query_two,
         pair_two) = two_first(
            place, after_three, grad_mine, grad_theirs, cotangent, gain_four, normed_three,
            memory_two, pooled_three, weights_two, out_two, skip, kept_two,
        )
        memory_part = shifted(plus_rounded(memory_kept, swap(memory_sent, "tensor", 1)), -1)
        w_two_far = swap(w_two_sent, "tensor", 2)
        grad_rows_two, w_two = two_second(
            branch_two, normed_three, pooled_three, weights_two, out_two, *early, query_two,
            pair_two, w_skip, kept_two,
        )
        grad_rows_two, memory_part, w_two = together(grad_rows_two, memory_part, w_two)
        got_rows_two = swap(grad_rows_two, "tensor", 1)
        memory_theirs = swap(memory_part, "tensor", 1)
        grad_two, grad_part_two, w_hidden, w_hidden_sent, w_gain_three = hidden_one_back(
            core_index, after_two, grad_rows_two, got_rows_two, memory_part,
            memory_theirs, gain_three, after_one, gain_two, w_in_one, w_out_one,
        )
        grad_part_two, w_two_far, w_hidden, w_hidden_sent = together(
            grad_part_two, w_two_far, w_hidden, w_hidden_sent
        )
        far_result_mine, far_result_theirs, result_theirs = after(
            (far_result_mine_, far_result_theirs_, result_theirs_), w_two_far
        )
        result_far = plus_rounded(far_result_mine, swap(far_result_theirs, "tensor", 1))
        result_far = swap(result_far, "tensor", 2)
        result_got = swap(result_theirs, "tensor", 1)
        total_two = ClipSum(plus_rounded(w_two, w_two_far), 2)
        w_hidden_far = swap(w_hidden_sent, "tensor", 2)
        (grad_one, branch_one, w_gain_two, early_rows, memory_kept, memory_sent, w_last_sent,
         *memory_terms) = one_first(
            core_index, grad_two, after_one, grad_part_two, swap(grad_part_two, "tensor", 1),
            gain_two, normed_one, memory_one, weights_one, out_one, kept_one,
        )
        branch_one, total_two.got, w_hidden_far, w_last_sent, result_far, result_got = together(
            branch_one, total_two.got, w_hidden_far, w_last_sent, result_far, result_got
        )
        result_half = result_mine.astype(F32) + result_got.astype(F32) + result_far.astype(F32)
        result_half = (result_half + share_of(after_three, core)).astype(BF)
        total_two.step()
        total_hidden = ClipSum(plus_rounded(w_hidden, w_hidden_far), 2)
        memory_last = shifted(plus_rounded(memory_kept, swap(memory_sent, "tensor", 1)), -1)
        w_last_far = swap(w_last_sent, "tensor", 2)
        far_result_half = swap(result_half, "tensor", 2)
        gains = jnp.concatenate([w_gain_two, w_gain_three, w_gain_four], 1).reshape(-1, width) * 0.5
        gains = jnp.pad(gains, ((1, GAIN_ROWS - 1 - gains.shape[0]), (0, 0)))
        leaving, leaving_sent, w_last = one_second(
            core_index, branch_one, normed_one, weights_one, out_one, early_rows, *memory_terms,
            gain_one, gains, kept_one,
        )
        (leaving, leaving_sent, memory_last, total_two.got, total_hidden.got, w_last, w_last_far,
         far_result_half) = together(
            leaving, leaving_sent, memory_last, total_two.got, total_hidden.got, w_last, w_last_far,
            far_result_half,
        )
        left[:] = [total_two.todo, total_hidden.todo]
        return (
            leaving, leaving_sent, memory_last, total_two.got, total_hidden.got, w_last, w_last_far,
            far_result_half, grad_one, total_two.block, total_hidden.block, result_half,
        )

    shapes = jax.eval_shape(backward)

    def absent():
        return tuple(jnp.zeros(item.shape, item.dtype) for item in shapes)

    results = lax.cond(clip_index < tokens_in.shape[0] * lax.axis_size("clip"), backward, absent)
    results, early_totals = together(results, early_totals)
    (leaving, leaving_sent, memory_last, got_two, got_hidden, w_last, w_last_far, far_result_half,
     grad_one, block_two, block_hidden, result_half) = results
    total_two = ClipSum.resumed(block_two, left[0], got_two)
    total_hidden = ClipSum.resumed(block_hidden, left[1], got_hidden)
    leaving_got = swap(leaving_sent, "tensor", 1)
    memory_theirs = swap(memory_last, "tensor", 1)
    total_last = ClipSum(plus_rounded(w_last, w_last_far))
    total_hidden.step()
    total_two.step()

    def leave(which, dtype):
        place = jnp.stack([which * 2 + core, which, core]).astype(jnp.int32)
        return exit_norm(
            place, normed_one, factor_one, grad_one, leaving, leaving_got, memory_last, memory_theirs, gain_one,
            dtype,
        )

    def move_on(beside_it, *sums):
        sums = [item for item in sums if item.todo]
        beside_it, *arrived = together(beside_it, *[item.got for item in sums])
        for item, got in zip(sums, arrived):
            item.got = got
            item.step()
        return beside_it

    far_input = move_on(leave(1 - chip, BF), total_last, total_hidden, total_two)
    far_input = swap(far_input, "tensor", 2)
    near_input, early_totals, far_result_half = move_on(
        (leave(chip, F32), early_totals, far_result_half), total_last, total_hidden, total_two
    )
    far_input = move_on(far_input, total_last, total_hidden, total_two)
    far_input = far_input.astype(F32)
    grad_input = jnp.where(
        chip == 0, jnp.stack([near_input, far_input]), jnp.stack([far_input, near_input])
    )
    result_pair = jnp.where(
        chip == 0,
        jnp.stack([result_half, far_result_half]),
        jnp.stack([far_result_half, result_half]),
    )
    other_pair = swap(result_pair, "tensor", 1)
    output = jnp.where(
        core == 0,
        jnp.concatenate([result_pair, other_pair], 1),
        jnp.concatenate([other_pair, result_pair], 1),
    ).astype(F32)
    early = [item.astype(F32) for item in early_totals]
    output, grad_input, early = move_on(
        (output, grad_input, early), total_last, total_hidden, total_two
    )
    while total_last.todo or total_hidden.todo or total_two.todo:
        output = move_on(output, total_last, total_hidden, total_two)
    totals_two = total_two.block
    grad_heads_in_two = turned(totals_two[:in_rows])
    grad_rows = unfold(totals_two[in_rows:])
    totals_last, totals_hidden_one = total_last.block, total_hidden.block
    gains = totals_last[4 * HD :].astype(F32)
    gains = gains + swap(gains, "tensor", 1)
    gains = (gains + swap(gains, "tensor", 2)).reshape(-1)
    return (
        output[:, None],
        grad_input[:, None],
        gains[:width],
        turned(totals_last[:heads_rows]),
        totals_last[heads_rows : 4 * HD].astype(F32),
        gains[width : 2 * width],
        totals_hidden_one[:width].astype(F32),
        totals_hidden_one[width:].astype(F32),
        gains[2 * width : 3 * width],
        grad_heads_in_two,
        grad_rows[-skip_rows:],
        grad_rows[:-skip_rows],
        gains[3 * width : 3 * width + wide],
        *early,
    )

def solution(mesh):
    return jax.shard_map(
        per_device,
        mesh=mesh,
        in_specs=(
            P(None, "clip", None, None),
            P(),
            P(None, None, "tensor"),
            P("tensor", None),
            P(),
            P(None, "tensor"),
            P("tensor", None),
            P(),
            P(None, None, "tensor"),
            P("tensor", None),
            P("tensor", None),
            P(),
            P(None, "tensor"),
            P("tensor", None),
            P(),
            P(),
            P(None, "clip", None, None),
        ),
        out_specs=(
            P(None, "clip", None, None),
            P(None, "clip", "tensor", None),
            P(),
            P(None, None, "tensor"),
            P("tensor", None),
            P(),
            P(None, "tensor"),
            P("tensor", None),
            P(),
            P(None, None, "tensor"),
            P("tensor", None),
            P("tensor", None),
            P(),
            P(None, "tensor"),
            P("tensor", None),
        ),
        check_vma=False,
    )
```

```python
import functools

import jax
import jax.numpy as jnp
from jax import lax
from jax.experimental import pallas as pl
from jax.experimental.pallas import tpu as pltpu
from jax.sharding import PartitionSpec as P

HD = 96
PAD = 128
TOK_LOW = 1052
EPSILON = 1e-06
MASKED_SCORE = -1e30
LOG2E = 1.4426950408889634
LN2 = 0.6931471805599453
SCALING = HD ** (-0.5)
BF = jnp.bfloat16
F32 = jnp.float32
MIB = 2**20
LARGE_MIB = 44
SMALL_MIB = 44
FFN_MIB = 20
EXIT_MIB = 60
COST = 1.0
GAIN_ROWS = 16
PIECE = 256
HIDDEN_SLABS = 2

NN = (((1,), (0,)), ((), ()))
NT = (((1,), (1,)), ((), ()))
TN = (((0,), (0,)), ((), ()))


def dot(left, right, form=NN):
    return lax.dot_general(left, right, form, preferred_element_type=F32)


def rms_factor(values):
    return lax.rsqrt(jnp.mean(values * values, -1, keepdims=True) + EPSILON)


def norm_grads(values, gain, grad):
    factor = rms_factor(values)
    scaled = values * factor
    term = grad * gain
    inner = jnp.mean(scaled * term, -1, keepdims=True)
    return factor * (term - scaled * inner), grad * scaled


def gelu_parts(values):
    root = 0.7978845608028654
    square = values * values
    tanh = jnp.tanh(values * (root + (root * 0.044715) * square))
    half = 0.5 + 0.5 * tanh
    slope = half + (0.5 * values) * (1.0 - tanh * tanh) * (root + (3 * root * 0.044715) * square)
    return values * half, slope


def gelu_only(values):
    root = 0.7978845608028654
    tanh = jnp.tanh(values * (root + (root * 0.044715) * (values * values)))
    return values * (0.5 + 0.5 * tanh)


def split_three(row):
    high = row.astype(BF).astype(F32)
    rest = row - high
    middle = rest.astype(BF).astype(F32)
    return high, middle, rest - middle


def call(body, name, grid, in_specs, out_specs, out_shape, scratch=(), prefetch=0, vmem=SMALL_MIB, us=1, aliases=()):
    return pl.pallas_call(
        body,
        name=name,
        grid_spec=pltpu.PrefetchScalarGridSpec(
            num_scalar_prefetch=prefetch,
            grid=grid,
            in_specs=in_specs,
            out_specs=out_specs,
            scratch_shapes=list(scratch),
        ),
        out_shape=out_shape,
        input_output_aliases=dict(aliases),
        compiler_params=pltpu.CompilerParams(vmem_limit_bytes=vmem * MIB),
        cost_estimate=pl.CostEstimate(
            flops=int(us * COST * 1.15e9), bytes_accessed=MIB // 4, transcendentals=0
        ),
    )


def whole(shape):
    return pl.BlockSpec(shape, lambda *_: (0,) * len(shape))


def shape_of(shape, dtype):
    return jax.ShapeDtypeStruct(shape, dtype)


def in_hbm(shape, dtype):
    return pltpu.HBM(shape, dtype)


def lane_scratch(rows, width):
    return pltpu.VMEM((width // PAD, rows, PAD), F32)


def slabs_of(block, lanes):
    parts = lanes.shape[0]
    rows = block.shape[0] // 4
    for part in range(parts):
        lanes[part] = block[:, part * PAD : (part + 1) * PAD]
    return [
        jnp.concatenate([lanes[part, pl.ds(s, rows, stride=4), :] for part in range(parts)], 1)
        for s in range(4)
    ]


def half_rows(core, half):
    return pl.ds(pl.multiple_of(core * half, half), half)


def half_block(rows, width, steps):
    per_half = steps // 2

    def place(step, _, core):
        return jnp.clip(step - per_half * core[0], 0, per_half - 1), 0

    return pl.BlockSpec((rows // steps, width), place)


def keep_half(core, step, steps, target, block):
    @pl.when(step // (steps // 2) == core[0])
    def _():
        target[...] = block


def entry_body(_, half, x_ref, gain_ref, *refs):
    normed_ref, factor_ref, pooled_ref, lanes = refs[-4:]
    total = None
    slabs = slabs_of(x_ref[0, 0], lanes)
    for slab in range(4):
        values = slabs[slab]
        factor = rms_factor(values)
        factor_ref[slab] = jnp.broadcast_to(factor, factor_ref.shape[1:])
        normed = (values * factor * gain_ref[...]).astype(BF)
        normed_ref[slab] = normed
        total = plus(total, normed.astype(F32))
    pooled_ref[...] = (total * 0.25).astype(BF)


def entry_norm(micro, half, tokens, gain, earlier=()):
    length, width = tokens.shape[2:]
    rows = length // 4
    block = rows // 4
    return call(
        entry_body,
        "entry_norm",
        (2,),
        [
            pl.BlockSpec((1, 1, 4 * block, width), lambda i, m, h: (m[0], 0, 2 * h[0] + i, 0)),
            whole((1, width)),
        ]
        + [pl.BlockSpec(memory_space=pl.ANY)] * len(earlier),
        [
            pl.BlockSpec((4, block, width), lambda i, m, h: (0, 2 * h[0] + i, 0)),
            pl.BlockSpec((4, block, PAD), lambda i, m, h: (0, 2 * h[0] + i, 0)),
            pl.BlockSpec((block, width), lambda i, *_: (i, 0)),
        ],
        [
            shape_of((4, rows, width), BF),
            in_hbm((4, rows, PAD), F32),
            shape_of((rows // 2, width), BF),
        ],
        scratch=[lane_scratch(4 * block, width)],
        prefetch=2,
        vmem=EXIT_MIB,
        us=3,
        aliases=[(4 + index, index) for index in range(len(earlier))],
    )(micro, half, tokens, gain.reshape(1, -1), *earlier)


def own_limit(place, resolution, length):
    return jnp.where(resolution[place[1], place[0]] == 1, length, TOK_LOW)


def memory_limit(place, resolution, carried, length):
    before = resolution[place[1], jnp.maximum(place[0] - 1, 0)]
    usable = (carried[place[1], place[0]] == 1) & (place[0] > 0)
    return jnp.where(usable, jnp.where(before == 1, length, TOK_LOW), 0)


def make_pair(limit, offset, source, weights):
    rows = source.shape[0]
    place = lax.broadcasted_iota(jnp.int32, (rows, 1), 0) * 4 + offset
    lane = lax.broadcasted_iota(jnp.int32, (rows, PAD), 1)
    bias = jnp.where(place < limit, 0.0, MASKED_SCORE)
    both = dot(source, weights[PAD:], NT)
    keys = jnp.where(lane < HD, both[:, :PAD], jnp.where(lane == HD, bias, 1.0))
    values = jnp.where(lane < HD, both[:, PAD:], 1.0)
    return keys.astype(BF), values.astype(BF)


def own_pairs_body(place, resolution, _, normed, weights, *results):
    limit = own_limit(place, resolution, 4 * normed.shape[1])
    for head in range(weights.shape[0]):
        parts = make_pair(limit, pl.program_id(0), normed[0], weights[head])
        for result, part in zip(results, parts):
            result[head, 0] = part


def pair_shapes(rows):
    return [(rows, PAD), (rows, PAD)]


def own_pairs(limits, normed, weights):
    _, rows, width = normed.shape
    heads = weights.shape[0]
    return call(
        own_pairs_body,
        "own_pairs",
        (4,),
        [pl.BlockSpec((1, rows, width), lambda i, *_: (i, 0, 0)), whole(weights.shape)],
        [
            pl.BlockSpec((heads, 1) + shape, lambda i, *_: (0, i, 0, 0))
            for shape in pair_shapes(rows)
        ],
        [shape_of((heads, 4) + shape, BF) for shape in pair_shapes(rows)],
        prefetch=3,
        us=6,
    )(*limits, normed, weights)


def query_tail(rows, parts):
    index = lax.broadcasted_iota(jnp.int32, (PAD - HD, rows), 0)
    tail = jnp.where(index == 0, 1.0, 0.0)
    for step, part in enumerate(parts):
        tail = jnp.where(index == step + 1, -part, tail)
    return tail.astype(BF)


def ask(source, weights):
    query = (dot(weights[:HD], source, NT) * (SCALING * LOG2E)).astype(BF)
    return query, jnp.concatenate([query, query_tail(query.shape[1], ())], 0)


def score_rows(asked, keys):
    parts = range(asked.shape[1] // PIECE)
    return [
        dot(keys(chunk)[part * PIECE : (part + 1) * PIECE], asked)
        for chunk in range(5)
        for part in parts
    ]


def attend_rows(query, scores, values):
    rows = query.shape[1]
    parts = rows // PIECE
    top = functools.reduce(jnp.maximum, [jnp.max(item, 0, keepdims=True) for item in scores])
    result = None
    for index, item in enumerate(scores):
        raised = jnp.exp2(item - top).astype(BF)
        part = index % parts
        term = dot(values(index // parts)[part * PIECE : (part + 1) * PIECE], raised, TN)
        result = term if result is None else result + term
    summed = result[HD : HD + 1]
    heads = (result[:HD] / summed).astype(BF)
    logsum = top + jnp.log2(summed)
    return heads, jnp.concatenate([query, query_tail(rows, split_three(logsum))], 0)


def chosen(own, memory, head):
    return lambda chunk: own[head, chunk] if chunk < 4 else memory[head]


def join_halves(core, mine, theirs, target):
    half = mine.shape[0]
    target[half_rows(core, half)] = mine[...]
    target[half_rows(1 - core, half)] = theirs[...]


def attend_one_body(
    place, resolution, carried, normed, mine, theirs, weights, out_weights, own_keys, own_values,
    memory, keys, values, queries_t, heads_t, partial,
):
    @pl.when(pl.program_id(0) == 0)
    def _():
        join_halves(place[2], mine, theirs, memory)
        limit = memory_limit(place, resolution, carried, 4 * memory.shape[0])
        for head in range(2):
            keys[head], values[head] = make_pair(limit, 0, memory[...], weights[head])

    total = None
    queries = [ask(normed[0], weights[head]) for head in range(2)]
    scores = [score_rows(queries[head][1], chosen(own_keys, keys, head)) for head in range(2)]
    for head in range(2):
        heads, asked = attend_rows(
            queries[head][0], scores[head], chosen(own_values, values, head)
        )
        heads_t[head] = heads
        queries_t[head] = asked
        term = dot(heads, out_weights[head], TN)
        total = term if total is None else total + term
    partial[0] = total.astype(BF)


def attend_one(limits, normed, mine, theirs, weights, out_weights, own_keys, own_values):
    _, rows, width = normed.shape
    heads = weights.shape[0]
    memory_shapes = [(heads,) + shape for shape in pair_shapes(rows)]
    return call(
        attend_one_body,
        "attend_one",
        (4,),
        [
            pl.BlockSpec((1, rows, width), lambda i, *_: (i, 0, 0)),
            whole(mine.shape),
            whole(theirs.shape),
            whole(weights.shape),
            whole(out_weights.shape),
            whole(own_keys.shape),
            whole(own_values.shape),
        ],
        [whole((rows, width))]
        + [whole(shape) for shape in memory_shapes]
        + [
            pl.BlockSpec((heads, PAD, rows), lambda i, *_: (0, 0, i)),
            pl.BlockSpec((heads, HD, rows), lambda i, *_: (0, 0, i)),
            pl.BlockSpec((1, rows, width), lambda i, *_: (i, 0, 0)),
        ],
        [shape_of((rows, width), BF)]
        + [shape_of(shape, BF) for shape in memory_shapes]
        + [
            shape_of((heads, PAD, 4 * rows), BF),
            shape_of((heads, HD, 4 * rows), BF),
            shape_of((4, rows, width), BF),
        ],
        prefetch=3,
        vmem=LARGE_MIB,
        us=22,
    )(*limits, normed, mine, theirs, weights, out_weights, own_keys, own_values)


def attend_two_body(
    place, resolution, carried, mine, theirs, pooled, weights, out_weights, skip, own_keys, own_values,
    memory, keys, values, queries_t, heads_t, partial, total,
):
    step = pl.program_id(0)

    @pl.when(step == 0)
    def _():
        join_halves(place[2], mine, theirs, memory)
        total[...] = dot(pooled[...], skip[...])

    limit = memory_limit(place, resolution, carried, 4 * memory.shape[0])
    here = range(weights.shape[0])
    queries = [ask(pooled[...], weights[head]) for head in here]
    for head in here:
        keys[head], values[head] = make_pair(limit, 0, memory[...], weights[head])
    scores = [score_rows(queries[head][1], chosen(own_keys, keys, head)) for head in here]
    for head in here:
        heads, asked = attend_rows(
            queries[head][0], scores[head], chosen(own_values, values, head)
        )
        heads_t[head] = heads
        queries_t[head] = asked
        total[...] += dot(heads, out_weights[head], TN)

    @pl.when(step == pl.num_programs(0) - 1)
    def _():
        partial[...] = total[...].astype(BF)


def attend_two(limits, mine, theirs, pooled, weights, out_weights, skip, own_keys, own_values):
    rows, width = pooled.shape
    heads = weights.shape[0]
    wide = out_weights.shape[2]

    def each(*shape):
        return pl.BlockSpec((2,) + shape, lambda h, *_: (h,) + (0,) * len(shape))

    results = pair_shapes(rows) + [(PAD, rows), (HD, rows)]
    return call(
        attend_two_body,
        "attend_two",
        (heads // 2,),
        [
            whole(mine.shape),
            whole(theirs.shape),
            whole((rows, width)),
            each(*weights.shape[1:]),
            each(HD, wide),
            whole(skip.shape),
            each(4, rows, PAD),
            each(4, rows, PAD),
        ],
        [whole((rows, width))] + [each(*shape) for shape in results] + [whole((rows, wide))],
        [shape_of((rows, width), BF)]
        + [shape_of((heads,) + shape, BF) for shape in results]
        + [shape_of((rows, wide), BF)],
        scratch=[pltpu.VMEM((rows, wide), F32)],
        prefetch=3,
        vmem=LARGE_MIB,
        us=16,
    )(*limits, mine, theirs, pooled, weights, out_weights, skip, own_keys, own_values)


def grad_chunk(keys, values, asked, given):
    chances = jnp.exp2(dot(keys, asked))
    spread = dot(values, given)
    grad_scores = (chances * spread).astype(BF)
    grad_values = dot(chances.astype(BF), given, NT)
    grad_keys = dot(grad_scores, asked, NT)
    return grad_keys, grad_values, dot(keys, grad_scores, TN)[:HD]


def given_rows(out_weights, grad, heads):
    back = dot(out_weights, grad, NT).astype(BF)
    inner = jnp.sum(back.astype(F32) * heads.astype(F32), 0, keepdims=True)
    high, middle, low = split_three(inner)
    index = lax.broadcasted_iota(jnp.int32, (PAD - HD, grad.shape[0]), 0)
    tail = jnp.where(index == 0, -high, jnp.where(index == 1, -middle, jnp.where(index == 2, -low, 0.0)))
    return jnp.concatenate([back, tail.astype(BF)], 0)


def pair_of(grad_keys, grad_values):
    return jnp.concatenate([(grad_keys * LN2).astype(BF), grad_values.astype(BF)], 1)


def plus(total, term):
    return term if total is None else total + term


class Kept:
    def __init__(self, refs, head):
        own_keys, own_values, keys, values, self.queries, self.heads = refs
        self.keys = chosen(own_keys, keys, head)
        self.values = chosen(own_values, values, head)
        self.head = head

    def grads(self, chunk, given):
        return grad_chunk(
            self.keys(chunk), self.values(chunk), self.queries[self.head], given
        )

    def given(self, out_weights, branch):
        return given_rows(out_weights[self.head], branch, self.heads[self.head])


def put_head(target, head, heads, grad_query, grad_pair, columns):
    width = target.shape[1]
    parts = [grad_query, grad_pair[:HD], grad_pair[PAD : PAD + HD]]
    sides = [columns[:, side : side + width] for side in range(0, columns.shape[1], width)]
    starts = [(index * heads + head) * HD for index in range(3)]
    starts += [(3 * heads + head * len(sides) + index) * HD for index in range(len(sides))]
    for start, part in zip(starts, parts + sides):
        target[pl.ds(pl.multiple_of(start, 32), HD)] = part.astype(BF)


def put_skip(target, start, columns, share):
    width = target.shape[1]
    for index, side in enumerate(range(0, columns.shape[1], width)):
        rows = columns[pl.ds(pl.multiple_of(share * HD, 32), HD), side : side + width]
        target[start + index * HD : start + (index + 1) * HD] = rows


def two_first_body(
    place, after, mine, theirs, cotangent, gain, normed, memory, pooled, weights, out_weights, skip,
    *refs
):
    kept, results, scratch = Kept(refs[:6], 0), refs[6:16], refs[16:]
    (branch, grad_gain, own_skip, grad_rows, grad_pool, memory_mine, memory_theirs, grad_weights,
     query_memory, pair_memory) = results
    total, columns = scratch
    step = pl.program_id(0)
    core, share = place[1], place[2]
    wide = after.shape[1]
    width = pooled.shape[1]
    sides = wide // width
    head_rows = (3 + sides) * HD

    @pl.when(step == 0)
    def _():
        first = jnp.where(core == 0, mine[...], theirs[...]).astype(F32)
        second = jnp.where(core == 0, theirs[...], mine[...]).astype(F32)
        arrived = jnp.concatenate([first, second], 0)
        back, terms = norm_grads(after[...], gain[...], arrived)
        grad_gain[...] = jnp.sum(terms, 0, keepdims=True)
        branch[...] = (cotangent[0, 0] + back).astype(BF)
        columns[...] = dot(pooled[...], branch[...], TN).astype(BF)
        put_skip(grad_weights, 2 * head_rows, columns, share ^ 2)
        put_skip(own_skip, 0, columns, share)
        grad_pool[...] = dot(branch[...], skip[...], NT)
        total[...] = jnp.zeros_like(total)

    given = kept.given(out_weights, branch[...])

    @pl.when(step < 2)
    def _():
        grad_query, grad_pair = None, None
        for chunk in range(5):
            grad_keys, grad_values, term = kept.grads(chunk, given)
            grad_query = plus(grad_query, term)
            pair = pair_of(grad_keys, grad_values)
            total[chunk] += dot(pair, weights[0, PAD:])
            source = normed[chunk] if chunk < 4 else memory[...]
            grad_pair = plus(grad_pair, dot(pair, source, TN))
        grad_query = (grad_query * SCALING).astype(BF)
        grad_pool[...] += dot(grad_query, weights[0, :HD], TN)
        put_head(
            grad_weights, step, 2, dot(grad_query, pooled[...]), grad_pair,
            dot(kept.heads[0], branch[...]),
        )

    @pl.when(step >= 2)
    def _():
        grad_keys, grad_values, term = kept.grads(4, given)
        query_memory[0] = term
        pair = pair_of(grad_keys, grad_values)
        total[4] += dot(pair, weights[0, PAD:])
        pair_memory[0] = dot(pair, memory[...], TN)

    @pl.when(step == 3)
    def _():
        half = memory_mine.shape[0]
        for chunk in range(4):
            grad_rows[chunk] = total[chunk].astype(BF)
        memory_mine[...] = total[4, half_rows(core, half)].astype(BF)
        memory_theirs[...] = total[4, half_rows(1 - core, half)].astype(BF)


def two_second_body(
    branch, normed, pooled, weights, out_weights, earlier_rows, earlier_pool, query_memory,
    pair_memory, own_skip, *refs
):
    kept, (grad_rows, grad_weights, total, total_pool) = Kept(refs[:6], 0), refs[6:]
    step = pl.program_id(0)
    head_rows = (grad_weights.shape[0] - own_skip.shape[0]) // 2

    @pl.when(step == 0)
    def _():
        grad_weights[2 * head_rows :] = own_skip[...]
        total_pool[...] = earlier_pool[...]
        for chunk in range(4):
            total[chunk] = earlier_rows[chunk].astype(F32)

    given = kept.given(out_weights, branch[...])
    grad_query, grad_pair = query_memory[0], pair_memory[0]
    for chunk in range(4):
        grad_keys, grad_values, term = kept.grads(chunk, given)
        grad_query = grad_query + term
        pair = pair_of(grad_keys, grad_values)
        total[chunk] += dot(pair, weights[0, PAD:])
        grad_pair = grad_pair + dot(pair, normed[chunk], TN)
    grad_query = (grad_query * SCALING).astype(BF)
    total_pool[...] += dot(grad_query, weights[0, :HD], TN)
    put_head(
        grad_weights, step, 2, dot(grad_query, pooled[...]), grad_pair,
        dot(kept.heads[0], branch[...]),
    )

    @pl.when(step == pl.num_programs(0) - 1)
    def _():
        for chunk in range(4):
            grad_rows[chunk] = (total[chunk] + 0.25 * total_pool[...]).astype(BF)


def kept_specs(each, rows, own=None):
    pair = pair_shapes(rows)
    return [(own or each)(4, *shape) for shape in pair] + [each(*shape) for shape in pair]


def two_first(
    place, after, mine, theirs, cotangent, gain, normed, memory, pooled, weights, out_weights, skip, kept
):
    _, rows, width = normed.shape
    wide = out_weights.shape[2]
    sides = wide // width
    all_rows = 2 * (3 + sides) * HD + sides * HD

    def each(*shape):
        return pl.BlockSpec((1,) + shape, lambda h, _: ((h + 2) % 4,) + (0,) * len(shape))

    def own(*shape):
        return pl.BlockSpec((1,) + shape, lambda h, _: (jnp.minimum(h, 1) + 2,) + (0,) * len(shape))

    def late(*shape):
        return pl.BlockSpec((1,) + shape, lambda h, _: (jnp.maximum(h, 2) - 2,) + (0,) * len(shape))

    return call(
        two_first_body,
        "back_two_first",
        (4,),
        [
            whole((rows, wide)),
            whole(mine.shape),
            whole(theirs.shape),
            pl.BlockSpec((1, 1, rows, wide), lambda h, m: (m[0], 0, 0, 0)),
            whole((1, wide)),
            whole((4, rows, width)),
            whole((rows, width)),
            whole((rows, width)),
            each(*weights.shape[1:]),
            each(HD, wide),
            whole(skip.shape),
        ]
        + kept_specs(each, rows, own)
        + [each(PAD, rows), each(HD, rows)],
        [
            whole((rows, wide)),
            whole((1, wide)),
            whole((sides * HD, width)),
            whole((4, rows, width)),
            whole((rows, width)),
            whole((rows // 2, width)),
            whole((rows // 2, width)),
            whole((all_rows, width)),
            late(HD, rows),
            late(2 * PAD, width),
        ],
        [
            shape_of((rows, wide), BF),
            shape_of((1, wide), F32),
            shape_of((sides * HD, width), BF),
            shape_of((4, rows, width), BF),
            shape_of((rows, width), F32),
            shape_of((rows // 2, width), BF),
            shape_of((rows // 2, width), BF),
            shape_of((all_rows, width), BF),
            shape_of((2, HD, rows), F32),
            shape_of((2, 2 * PAD, width), F32),
        ],
        scratch=[pltpu.VMEM((5, rows, width), F32), pltpu.VMEM((width, wide), BF)],
        prefetch=1,
        vmem=LARGE_MIB,
        us=23,
    )(
        place, after, mine, theirs, cotangent, gain.reshape(1, -1), normed, memory, pooled, weights,
        out_weights, skip, *kept,
    )


def two_second(
    branch, normed, pooled, weights, out_weights, earlier_rows, earlier_pool, query_memory,
    pair_memory, own_skip, kept
):
    _, rows, width = normed.shape
    wide = out_weights.shape[2]
    all_rows = 2 * (3 + wide // width) * HD + own_skip.shape[0]

    def each(*shape):
        return pl.BlockSpec((1,) + shape, lambda h: (h,) + (0,) * len(shape))

    return call(
        two_second_body,
        "back_two_second",
        (2,),
        [
            whole((rows, wide)),
            whole((4, rows, width)),
            whole((rows, width)),
            each(*weights.shape[1:]),
            each(HD, wide),
            whole((4, rows, width)),
            whole((rows, width)),
            each(HD, rows),
            each(2 * PAD, width),
            whole(own_skip.shape),
        ]
        + kept_specs(each, rows)
        + [each(PAD, rows), each(HD, rows)],
        [whole((4, rows, width)), whole((all_rows, width))],
        [shape_of((4, rows, width), BF), shape_of((all_rows, width), BF)],
        scratch=[pltpu.VMEM((4, rows, width), F32), pltpu.VMEM((rows, width), F32)],
        vmem=LARGE_MIB,
        us=14,
    )(
        branch, normed, pooled, weights, out_weights, earlier_rows, earlier_pool, query_memory,
        pair_memory, own_skip, *kept,
    )


def put_last(target, grad_query, grad_pair, grad_out, gains):
    parts = [grad_query, grad_pair[:HD], gains, grad_pair[PAD : PAD + HD], grad_out, gains]
    start = 0
    for part in parts:
        target[start : start + part.shape[0]] = part.astype(BF)
        start += part.shape[0]


def one_first_body(
    core, grad_two, after, own_part, other_part, gain, normed, memory, weights, out_weights, *refs
):
    kept, near_kept = Kept(refs[:6], 1), Kept(refs[:6], 0)
    (grad_one, branch_ref, grad_gain, grad_rows, memory_mine, memory_theirs, grad_weights,
     query_memory, pair_memory, memory_gain) = refs[6:16]
    total, total_keys, total_values, total_query, total_out, near_keys, near_values, rows_memory = (
        refs[16:]
    )
    slab = pl.program_id(0)

    @pl.when(slab == 0)
    def _():
        for item in (grad_gain, total_keys, total_values, total_query, total_out, near_keys, near_values):
            item[...] = jnp.zeros_like(item)

    arrived = own_part[0].astype(F32) + other_part[0].astype(F32)
    back, terms = norm_grads(after[0], gain[...], arrived)
    grad_gain[...] += jnp.sum(terms, 0, keepdims=True)
    state = grad_two[0] + back
    grad_one[0] = state
    branch = state.astype(BF)
    branch_ref[0] = branch
    given = kept.given(out_weights, branch)
    grad_query = None
    for chunk in range(5):
        grad_keys, grad_values, term = kept.grads(chunk, given)
        total_keys[chunk] += grad_keys
        total_values[chunk] += grad_values
        grad_query = plus(grad_query, term)
    grad_keys, grad_values, term = near_kept.grads(4, near_kept.given(out_weights, branch))
    near_keys[...] += grad_keys
    near_values[...] += grad_values
    query_memory[...] = term
    grad_query = (grad_query * SCALING).astype(BF)
    total_out[...] += dot(kept.heads[1], branch)
    total_query[...] += dot(grad_query, normed[slab])
    total[slab] = dot(grad_query, weights[1, :HD], TN)

    @pl.when(slab == pl.num_programs(0) - 1)
    def _():
        pair = pair_of(near_keys[...], near_values[...])
        pair_memory[...] = dot(pair, memory[...], TN)
        near_rows = dot(pair, weights[0, PAD:])
        grad_pair = None
        for chunk in range(5):
            pair = pair_of(total_keys[chunk], total_values[chunk])
            rows = dot(pair, weights[1, PAD:])
            source = normed[chunk] if chunk < 4 else memory[...]
            grad_pair = plus(grad_pair, dot(pair, source, TN))
            if chunk < 4:
                grad_rows[chunk] = (total[chunk] + rows).astype(BF)
            else:
                rows = near_rows + rows
                memory_gain[...] = jnp.sum(rows * memory[...].astype(F32), 0, keepdims=True)
                rows_memory[...] = rows
        half = memory_mine.shape[0]
        memory_mine[...] = rows_memory[half_rows(core[0], half)].astype(BF)
        memory_theirs[...] = rows_memory[half_rows(1 - core[0], half)].astype(BF)
        put_last(
            grad_weights, total_query[...], grad_pair, total_out[...],
            jnp.zeros((GAIN_ROWS, grad_weights.shape[1]), F32),
        )


def one_second_body(
    core, branch_ref, normed, weights, out_weights, earlier_rows, query_memory, pair_memory,
    memory_gain, gain, other_gains, *refs
):
    kept, (mine, theirs, grad_weights) = Kept(refs[:6], 0), refs[6:9]
    total, total_keys, total_values, total_query, total_out = refs[9:]
    slab = pl.program_id(0)

    @pl.when(slab == 0)
    def _():
        for item in (total_keys, total_values, total_query, total_out):
            item[...] = jnp.zeros_like(item)

    branch = branch_ref[0]
    given = kept.given(out_weights, branch)
    grad_query = query_memory[...]
    for chunk in range(4):
        grad_keys, grad_values, term = kept.grads(chunk, given)
        total_keys[chunk] += grad_keys
        total_values[chunk] += grad_values
        grad_query = grad_query + term
    grad_query = (grad_query * SCALING).astype(BF)
    total_out[...] += dot(kept.heads[0], branch)
    total_query[...] += dot(grad_query, normed[slab])
    total[slab] = dot(grad_query, weights[0, :HD], TN)

    @pl.when(slab == pl.num_programs(0) - 1)
    def _():
        grad_pair = pair_memory[...]
        gain_terms = memory_gain[...]
        share = mine.shape[2]
        for chunk in range(4):
            pair = pair_of(total_keys[chunk], total_values[chunk])
            rows = dot(pair, weights[0, PAD:]) + earlier_rows[chunk].astype(F32)
            rows = total[chunk] + rows
            gain_terms += jnp.sum(rows * normed[chunk].astype(F32), 0, keepdims=True)
            total[chunk] = rows
            for chip in range(mine.shape[1]):
                for target, which in ((mine, core[0]), (theirs, 1 - core[0])):
                    start = pl.multiple_of((2 * chip + which) * share, share)
                    target[chunk, chip] = total[chunk, pl.ds(start, share)].astype(BF)
            grad_pair = grad_pair + dot(pair, normed[chunk], TN)
        gains = jnp.concatenate([gain_terms / gain[...], other_gains[1:]], 0)
        put_last(grad_weights, total_query[...], grad_pair, total_out[...], gains)


def one_specs(rows):
    def heads(*shape):
        return whole((2,) + shape)

    return kept_specs(heads, rows) + [
        pl.BlockSpec((2, PAD, rows), lambda i, *_: (0, 0, i)),
        pl.BlockSpec((2, HD, rows), lambda i, *_: (0, 0, i)),
    ]


def one_scratch(rows, width, chunks):
    return [
        pltpu.VMEM((4, rows, width), F32),
        pltpu.VMEM((chunks, rows, PAD), F32),
        pltpu.VMEM((chunks, rows, PAD), F32),
        pltpu.VMEM((HD, width), F32),
        pltpu.VMEM((HD, width), F32),
    ]


def one_first(
    core, grad_two, after, own_part, other_part, gain, normed, memory, weights, out_weights, kept
):
    _, rows, width = grad_two.shape
    slab = pl.BlockSpec((1, rows, width), lambda i, *_: (i, 0, 0))
    return call(
        one_first_body,
        "back_one_first",
        (4,),
        [slab, slab, slab, slab, whole((1, width)), whole((4, rows, width)), whole((rows, width))]
        + [whole(weights.shape), whole(out_weights.shape)]
        + one_specs(rows),
        [
            slab,
            slab,
            whole((1, width)),
            whole((4, rows, width)),
            whole((rows // 2, width)),
            whole((rows // 2, width)),
            whole((4 * HD + 2 * GAIN_ROWS, width)),
            pl.BlockSpec((HD, rows), lambda i, *_: (0, i)),
            whole((2 * PAD, width)),
            whole((1, width)),
        ],
        [
            shape_of((4, rows, width), F32),
            shape_of((4, rows, width), BF),
            shape_of((1, width), F32),
            shape_of((4, rows, width), BF),
            shape_of((rows // 2, width), BF),
            shape_of((rows // 2, width), BF),
            shape_of((4 * HD + 2 * GAIN_ROWS, width), BF),
            in_hbm((HD, 4 * rows), F32),
            shape_of((2 * PAD, width), F32),
            shape_of((1, width), F32),
        ],
        scratch=one_scratch(rows, width, 5)
        + [pltpu.VMEM((rows, PAD), F32), pltpu.VMEM((rows, PAD), F32), pltpu.VMEM((rows, width), F32)],
        prefetch=1,
        vmem=LARGE_MIB,
        us=27,
    )(
        core, grad_two, after, own_part, other_part, gain.reshape(1, -1), normed, memory, weights,
        out_weights, *kept,
    )


def one_second(
    core, branch, normed, weights, out_weights, earlier_rows, query_memory, pair_memory, memory_gain,
    gain, other_gains, kept
):
    _, rows, width = branch.shape
    slab = pl.BlockSpec((1, rows, width), lambda i, *_: (i, 0, 0))
    leaving = (4, 2, rows // 4, width)
    return call(
        one_second_body,
        "back_one_second",
        (4,),
        [
            slab,
            whole((4, rows, width)),
            whole(weights.shape),
            whole(out_weights.shape),
            whole((4, rows, width)),
            pl.BlockSpec((HD, rows), lambda i, *_: (0, i)),
            whole((2 * PAD, width)),
            whole((1, width)),
            whole((1, width)),
            whole(other_gains.shape),
        ]
        + one_specs(rows),
        [whole(leaving), whole(leaving), whole((4 * HD + 2 * other_gains.shape[0], width))],
        [
            shape_of(leaving, BF),
            shape_of(leaving, BF),
            shape_of((4 * HD + 2 * other_gains.shape[0], width), BF),
        ],
        scratch=one_scratch(rows, width, 4),
        prefetch=1,
        vmem=LARGE_MIB,
        us=18,
    )(
        core, branch, normed, weights, out_weights, earlier_rows, query_memory, pair_memory,
        memory_gain, gain.reshape(1, -1), other_gains, *kept,
    )


def flat(block):
    return block.reshape(block.shape[0] * block.shape[1], block.shape[2])


def hidden_one_body(_, x_ref, own_part, other_part, gain, w_in, w_out, after, partial, lanes):
    tokens = slabs_of(x_ref[0, 0], lanes)
    for pair in range(0, 4, HIDDEN_SLABS):
        slabs = slice(pair, pair + HIDDEN_SLABS)
        state = flat(own_part[slabs].astype(F32) + other_part[slabs].astype(F32))
        state = state + jnp.concatenate(tokens[slabs], 0)
        after[slabs] = state.reshape(HIDDEN_SLABS, -1, state.shape[1])
        normed = (state * rms_factor(state) * gain[...]).astype(BF)
        active = gelu_only(dot(normed, w_in[...], NT)).astype(BF)
        partial[slabs] = dot(active, w_out[...]).astype(BF).reshape(HIDDEN_SLABS, -1, state.shape[1])


def hidden_one(micro, tokens, own_part, other_part, gain, w_in, w_out):
    _, rows, width = own_part.shape
    block = rows // 4
    strip = pl.BlockSpec((4, block, width), lambda i, m: (0, i, 0))
    return call(
        hidden_one_body,
        "hidden_one",
        (4,),
        [
            pl.BlockSpec((1, 1, 4 * block, width), lambda i, m: (m[0], 0, i, 0)),
            strip,
            strip,
            whole((1, width)),
            whole(w_in.shape),
            whole(w_out.shape),
        ],
        [strip, strip],
        [shape_of((4, rows, width), F32), shape_of((4, rows, width), BF)],
        scratch=[lane_scratch(4 * block, width)],
        prefetch=1,
        vmem=LARGE_MIB,
        us=7,
    )(micro, tokens, own_part, other_part, gain.reshape(1, -1), w_in, w_out)


def norm_three_body(_, state, own_part, other_part, gain, *refs):
    after, normed, pooled = refs[-3:]
    total = None
    for slab in range(4):
        values = state[slab] + (own_part[slab].astype(F32) + other_part[slab].astype(F32))
        after[slab] = values
        rows = (values * rms_factor(values) * gain[...]).astype(BF)
        normed[slab] = rows
        total = plus(total, rows.astype(F32))
    pooled[...] = (total * 0.25).astype(BF)


def norm_three(half, state, own_part, other_part, gain, earlier=()):
    _, rows, width = state.shape
    block = rows // 4
    strip = pl.BlockSpec((4, block, width), lambda i, h: (0, 2 * h[0] + i, 0))
    pooled = pl.BlockSpec((block, width), lambda i, h: (2 * h[0] + i, 0))
    return call(
        norm_three_body,
        "norm_three",
        (2,),
        [strip, strip, strip, whole((1, width))]
        + [pl.BlockSpec(memory_space=pl.ANY)] * len(earlier),
        [strip, strip, pooled],
        [
            shape_of((4, rows, width), F32),
            shape_of((4, rows, width), BF),
            shape_of((rows, width), BF),
        ],
        prefetch=1,
        us=3,
        aliases=[(5 + index, index) for index in range(len(earlier))],
    )(half, state, own_part, other_part, gain.reshape(1, -1), *earlier)


def hidden_one_back_body(
    core, after_two, own_part, other_part, mine, theirs, gain_three, after_one, gain_two, w_in, w_out,
    grad_two, partial, grad_own, grad_sent, grad_gain, total_in, total_out,
):
    step = pl.program_id(0)

    @pl.when(step == 0)
    def _():
        total_in[...] = jnp.zeros_like(total_in)
        total_out[...] = jnp.zeros_like(total_out)
        grad_gain[...] = jnp.zeros_like(grad_gain)

    memory = jnp.where(step // 2 == core[0], mine[...], theirs[...]).astype(F32) * 0.25
    width = memory.shape[1]
    for pair in range(0, 4, HIDDEN_SLABS):
        slabs = slice(pair, pair + HIDDEN_SLABS)
        arrived = own_part[slabs].astype(F32) + other_part[slabs].astype(F32) + memory[None]
        back, terms = norm_grads(flat(after_two[slabs]), gain_three[...], flat(arrived))
        grad_gain[...] += jnp.sum(terms, 0, keepdims=True)
        grad_two[slabs] = back.reshape(HIDDEN_SLABS, -1, width)
        branch = back.astype(BF)
        state = flat(after_one[slabs])
        normed = (state * rms_factor(state) * gain_two[...]).astype(BF)
        active, slope = gelu_parts(dot(normed, w_in[...], NT))
        grad_pre = (slope * dot(branch, w_out[...], NT)).astype(BF)
        partial[slabs] = dot(grad_pre, w_in[...]).astype(BF).reshape(HIDDEN_SLABS, -1, width)
        total_out[...] += dot(active.astype(BF), branch, TN)
        total_in[...] += dot(grad_pre, normed, TN)

    @pl.when(step == pl.num_programs(0) - 1)
    def _():
        share = total_in.shape[0] // 2
        for target, start in ((grad_own, 0), (grad_sent, share)):
            target[:share] = jnp.transpose(total_in[start : start + share]).astype(BF)
            target[share:] = total_out[start : start + share].astype(BF)


def hidden_one_back(
    core, after_two, own_part, other_part, mine, theirs, gain_three, after_one, gain_two, w_in, w_out
):
    _, rows, width = after_two.shape
    block = rows // 4
    hidden = w_in.shape[0]
    strip = pl.BlockSpec((4, block, width), lambda i, *_: (0, i, 0))
    memory = pl.BlockSpec((block, width), lambda i, *_: (i % 2, 0))
    return call(
        hidden_one_back_body,
        "hidden_one_back",
        (4,),
        [
            strip,
            strip,
            strip,
            memory,
            memory,
            whole((1, width)),
            strip,
            whole((1, width)),
            whole(w_in.shape),
            whole(w_out.shape),
        ],
        [strip, strip, whole(w_in.shape), whole(w_out.shape), whole((1, width))],
        [
            in_hbm((4, rows, width), F32),
            shape_of((4, rows, width), BF),
            shape_of(w_in.shape, BF),
            shape_of(w_out.shape, BF),
            shape_of((1, width), F32),
        ],
        scratch=[pltpu.VMEM((hidden, width), F32), pltpu.VMEM((hidden, width), F32)],
        prefetch=1,
        us=15,
    )(
        core, after_two, own_part, other_part, mine, theirs, gain_three.reshape(1, -1), after_one,
        gain_two.reshape(1, -1), w_in, w_out,
    )


def norm_four_body(core, own_part, other_part, gain, after, normed_ref, half_ref):
    state = own_part[...].astype(F32) + other_part[...].astype(F32)
    after[...] = state
    normed = (state * rms_factor(state) * gain[...]).astype(BF)
    normed_ref[...] = normed

    @pl.when(pl.program_id(0) == core[0])
    def _():
        half_ref[...] = normed


def norm_four(core, own_part, other_part, gain):
    rows, wide = own_part.shape
    half = rows // 2
    strip = pl.BlockSpec((half, wide), lambda i, _: (i, 0))
    return call(
        norm_four_body,
        "norm_four",
        (2,),
        [strip, strip, whole((1, wide))],
        [strip, strip, whole((half, wide))],
        [shape_of((rows, wide), F32), shape_of((rows, wide), BF), shape_of((half, wide), BF)],
        prefetch=1,
        us=2,
        vmem=FFN_MIB,
    )(core, own_part, other_part, gain.reshape(1, -1))


def hidden_two_body(
    place, first, second, cotangent, w_in, w_out,
    normed_ref, active_ref, grad_pre_ref, grad_mine, grad_theirs, result_mine, result_theirs,
):
    mine = pl.program_id(0) == place[1]
    normed = jnp.where(mine, first[...], second[...])
    normed_ref[...] = normed
    active, slope = gelu_parts(dot(normed, w_in[...]))
    active = active.astype(BF)
    grad_pre = (slope * dot(cotangent[0, 0].astype(BF), w_out[...], NT)).astype(BF)
    grad_normed = dot(grad_pre, w_in[...], NT).astype(BF)
    active_ref[...] = active
    grad_pre_ref[...] = grad_pre
    result = dot(active, w_out[...]).astype(BF)

    @pl.when(mine)
    def _():
        grad_mine[...] = grad_normed
        result_mine[...] = result

    @pl.when(jnp.logical_not(mine))
    def _():
        grad_theirs[...] = grad_normed
        result_theirs[...] = result


def hidden_two(place, first, second, cotangent, w_in, w_out):
    wide, hidden = w_in.shape
    rows = cotangent.shape[2]
    half = rows // 2
    given = pl.BlockSpec((half, wide), lambda i, p: (i if first is second else 0, 0))
    strip = pl.BlockSpec((half, wide), lambda i, p: (i, 0))
    strip_hidden = pl.BlockSpec((half, hidden), lambda i, p: (i, 0))
    return call(
        hidden_two_body,
        "hidden_two",
        (2,),
        [
            given,
            given,
            pl.BlockSpec((1, 1, half, wide), lambda i, p: (p[0], 0, i, 0)),
            whole(w_in.shape),
            whole(w_out.shape),
        ],
        [strip, strip_hidden, strip_hidden] + [whole((half, wide))] * 4,
        [in_hbm((rows, wide), BF), in_hbm((rows, hidden), BF), in_hbm((rows, hidden), BF)]
        + [shape_of((half, wide), BF)] * 2
        + [in_hbm((half, wide), BF)] * 2,
        prefetch=1,
        us=5,
        vmem=FFN_MIB,
    )(place, first, second, cotangent, w_in, w_out)


def hidden_two_weights_body(
    _, own_normed, own_active, own_pre, other_normed, other_active, other_pre, own_cot, other_cot,
    grad_in, grad_out,
):
    grad_in[...] = (
        dot(own_normed[...], own_pre[...], TN) + dot(other_normed[...], other_pre[...], TN)
    ).astype(BF)
    grad_out[...] = (
        dot(own_active[...], own_cot[0, 0].astype(BF), TN)
        + dot(other_active[...], other_cot[0, 0].astype(BF), TN)
    ).astype(BF)


def hidden_two_weights(micros, own, other, cotangent):
    rows, wide = own[0].shape
    hidden = own[1].shape[1]
    parts = 3
    column = pl.BlockSpec((rows, wide // parts), lambda i, m: (0, i))
    column_hidden = pl.BlockSpec((rows, hidden // parts), lambda i, m: (0, i))
    return call(
        hidden_two_weights_body,
        "hidden_two_weights",
        (parts,),
        [
            column,
            column_hidden,
            whole((rows, hidden)),
            column,
            column_hidden,
            whole((rows, hidden)),
            pl.BlockSpec((1, 1, rows, wide), lambda i, m: (m[0], 0, 0, 0)),
            pl.BlockSpec((1, 1, rows, wide), lambda i, m: (m[1], 0, 0, 0)),
        ],
        [
            pl.BlockSpec((wide // parts, hidden), lambda i, m: (i, 0)),
            pl.BlockSpec((hidden // parts, wide), lambda i, m: (i, 0)),
        ],
        [shape_of((wide, hidden), BF), shape_of((hidden, wide), BF)],
        prefetch=1,
        us=5,
        vmem=FFN_MIB,
    )(micros, *own, *other, cotangent, cotangent)


def exit_body(place, normed, factor, grad_one, partial, got, mine, theirs, gain, grad_input, lanes):
    block = mine.shape[0]
    memory = jnp.where(place[1] == place[2], mine[...], theirs[...]).astype(F32) * 0.25
    for slab in range(4):
        term = partial[slab, 0].astype(F32) + got[slab, 0].astype(F32) + memory
        term = term * gain[...]
        scaled = normed[slab].astype(F32) / gain[...]
        inner = jnp.mean(scaled * term, -1, keepdims=True)
        result = grad_one[slab] + factor[slab, :, :1] * (term - scaled * inner)
        for part in range(lanes.shape[0]):
            lanes[part, pl.ds(slab, block, stride=4), :] = result[:, part * PAD : (part + 1) * PAD]
    for part in range(lanes.shape[0]):
        columns = lanes[part].astype(grad_input.dtype)
        grad_input[:, part * PAD : (part + 1) * PAD] = columns


def exit_norm(place, normed, factor, grad_one, partial, got, mine, theirs, gain, dtype):
    _, rows, width = normed.shape
    share = rows
    block = share // 4
    strip = pl.BlockSpec((4, block, width), lambda i, p: (0, p[0], 0))
    leaving = pl.BlockSpec((4, 1, block, width), lambda i, p: (0, p[1], 0, 0))
    memory = pl.BlockSpec((block, width), lambda i, p: (p[2], 0))
    return call(
        exit_body,
        "exit_norm",
        (1,),
        [
            strip,
            pl.BlockSpec((4, block, PAD), lambda i, p: (0, p[0], 0)),
            strip,
            leaving,
            leaving,
            memory,
            memory,
            whole((1, width)),
        ],
        whole((share, width)),
        shape_of((share, width), dtype),
        scratch=[lane_scratch(share, width)],
        prefetch=1,
        vmem=EXIT_MIB,
        us=4,
    )(place, normed, factor, grad_one, partial, got, mine, theirs, gain.reshape(1, -1))


def swap(block, axis, bit):
    return lax.ppermute(block, axis, [(i, i ^ bit) for i in range(lax.axis_size(axis))])


def shifted(block, distance):
    devices = lax.axis_size("clip")
    return lax.ppermute(block, "clip", [(i, (i + distance) % devices) for i in range(devices)])


def after(block, earlier):
    return lax.optimization_barrier((block, earlier))[0]


def in_order(core, mine, theirs):
    ordered = jnp.where(core == 0, jnp.stack([mine, theirs]), jnp.stack([theirs, mine]))
    return ordered.reshape((-1,) + mine.shape[1:])


def share_of(block, core):
    half = block.shape[0] // 2
    return lax.dynamic_slice_in_dim(block, core * half, half, 0)


def together(results, *others):
    return lax.optimization_barrier((results,) + others)


class ClipSum:
    def __init__(self, block, halvings=1):
        clips = lax.axis_size("clip")
        self.index = lax.axis_index("clip")
        steps = [2**k for k in range(clips.bit_length() - 1)]
        halved = steps[:halvings]
        self.todo = [("halve", step) for step in halved] + [("add", step) for step in steps[halvings:]]
        self.todo += [("join", step) for step in reversed(halved)]
        self.block = block
        self.half = None
        self.send()

    @classmethod
    def resumed(cls, block, todo, got):
        self = cls.__new__(cls)
        self.index = lax.axis_index("clip")
        self.block, self.todo, self.got, self.half = block, list(todo), got, None
        return self

    def send(self):
        kind, step = self.todo[0]
        bit = self.index // step % 2
        sent = share_of(self.block, 1 - bit) if kind == "halve" else self.block
        if kind == "join" and self.half is None:
            self.half = self.block
        self.got = swap(sent, "clip", step)

    def take(self):
        kind, step = self.todo.pop(0)
        bit = self.index // step % 2
        got, self.got = self.got, None
        if kind == "join":
            self.block = in_order(bit, self.block, got)
        else:
            kept = share_of(self.block, bit) if kind == "halve" else self.block
            self.block = plus_rounded(kept, got)

    def step(self):
        self.take()
        if self.todo:
            self.send()

def plus_rounded(own, got):
    return (own.astype(F32) + got.astype(F32)).astype(BF)


def pad_heads(turned):
    widths = [(0, 0)] * (turned.ndim - 2) + [(0, PAD - HD), (0, 0)]
    padded = jnp.pad(turned, widths)
    return padded.reshape(turned.shape[:-3] + (3 * PAD, turned.shape[-1]))


def per_device(
    tokens_in,
    gain_one,
    heads_in_one,
    heads_out_one,
    gain_two,
    hidden_in_one,
    hidden_out_one,
    gain_three,
    heads_in_two,
    skip_weight,
    heads_out_two,
    gain_four,
    hidden_in_two,
    hidden_out_two,
    resolution,
    continues,
    cotangent,
):
    clip_index = lax.axis_index("clip")
    part_index = lax.axis_index("tensor")
    chip, core = part_index // 2, part_index % 2
    micro = chip.astype(jnp.int32).reshape(1)
    core_index = core.astype(jnp.int32).reshape(1)
    length, width = tokens_in.shape[2:]
    rows = length // 4
    wide = heads_out_two.shape[1]

    limits = (jnp.stack([clip_index, chip, core]).astype(jnp.int32), resolution, continues)

    skip_rows = skip_weight.shape[0]
    heads_rows = 3 * HD
    own_one = jnp.concatenate(
        [jnp.transpose(heads_in_one, (1, 2, 0)).reshape(heads_rows, width), heads_out_one], 0
    )
    far_one = swap(own_one, "tensor", 2)

    *first_half, pooled_half = entry_norm(micro, core_index, tokens_in, gain_one)
    normed_one, factor_one, _ = entry_norm(micro, 1 - core_index, tokens_in, gain_one, first_half)
    hidden_in_one, hidden_out_one, heads_in_two = after(
        (hidden_in_one, hidden_out_one, heads_in_two), (normed_one, far_one)
    )
    own_hidden = jnp.stack([jnp.transpose(hidden_in_one), hidden_out_one])
    own_two = jnp.transpose(heads_in_two, (1, 2, 0)).reshape(3, -1, HD, width)
    own_two = jnp.swapaxes(own_two, 0, 1)
    memory_mine = shifted(pooled_half, 1)
    far_hidden = swap(own_hidden, "tensor", 2)
    both_one = jnp.stack([own_one, far_one])
    weights_one = pad_heads(both_one[:, :heads_rows].reshape(2, 3, HD, width))
    out_one = both_one[:, heads_rows:]
    own_kept_one = list(own_pairs(limits, normed_one, weights_one))
    memory_mine, own_kept_one = together(memory_mine, own_kept_one)
    memory_theirs = swap(memory_mine, "tensor", 1)
    memory_one, *kept_one, attn_part = attend_one(
        limits, normed_one, memory_mine, memory_theirs, weights_one, out_one, *own_kept_one,
    )
    kept_one = own_kept_one + kept_one
    attn_part, far_hidden = together(attn_part, far_hidden)
    far_two = swap(after(own_two, far_hidden), "tensor", 2)
    w_in_one = jnp.concatenate([own_hidden[0], far_hidden[0]], 0)
    w_out_one = jnp.concatenate([own_hidden[1], far_hidden[1]], 0)
    after_one, ffn_part = hidden_one(
        micro, tokens_in, attn_part, swap(attn_part, "tensor", 1), gain_two, w_in_one, w_out_one
    )
    ffn_part, far_two = together(ffn_part, far_two)
    weights_two = pad_heads(jnp.concatenate([own_two, far_two], 0))
    own_rows = jnp.concatenate([skip_weight, heads_out_two], 0)
    far_rows = swap(after(own_rows, far_two), "tensor", 2)
    ffn_got = swap(ffn_part, "tensor", 1)
    first_half = norm_three(core_index, after_one, ffn_part, ffn_got, gain_three)
    pooled_half = share_of(first_half[2], core)
    after_two, normed_three, pooled_three = norm_three(
        1 - core_index, after_one, ffn_part, ffn_got, gain_three, first_half
    )

    memory_mine = shifted(pooled_half, 1)
    own_kept_two = list(own_pairs(limits, normed_three, weights_two))
    memory_mine, own_kept_two, far_rows = together(memory_mine, own_kept_two, far_rows)
    out_two = jnp.concatenate([own_rows[skip_rows:], far_rows[skip_rows:]], 0).reshape(-1, HD, wide)
    skip = jnp.zeros((width, wide), BF)
    skip = lax.dynamic_update_slice(skip, own_rows[:skip_rows], (part_index * skip_rows, 0))
    skip = lax.dynamic_update_slice(skip, far_rows[:skip_rows], ((part_index ^ 2) * skip_rows, 0))
    memory_theirs = swap(memory_mine, "tensor", 1)
    memory_two, *kept_two, branch_part = attend_two(
        limits, memory_mine, memory_theirs, pooled_three, weights_two, out_two, skip,
        *own_kept_two,
    )
    kept_two = own_kept_two + kept_two
    after_three, normed_four, normed_half = norm_four(
        core_index, branch_part, swap(branch_part, "tensor", 1), gain_four
    )
    far_mine = swap(normed_half, "tensor", 2)
    near_place = jnp.stack([chip, core]).astype(jnp.int32)
    far_place = jnp.stack([1 - chip, core]).astype(jnp.int32)
    *own_ffn, own_mine, own_theirs, result_mine, result_theirs_ = hidden_two(
        near_place, normed_four, normed_four, cotangent, hidden_in_two, hidden_out_two
    )
    far_mine, own_theirs = together(far_mine, own_theirs)
    far_theirs = swap(far_mine, "tensor", 1)
    own_got = swap(own_theirs, "tensor", 1)
    *far_ffn, far_grad_mine, far_grad_theirs, far_result_mine_, far_result_theirs_ = hidden_two(
        far_place, far_mine, far_theirs, cotangent, hidden_in_two, hidden_out_two
    )
    far_sum = plus_rounded(far_grad_mine, swap(far_grad_theirs, "tensor", 1))
    far_sum = swap(far_sum, "tensor", 2)
    w_hidden_two = hidden_two_weights(
        jnp.concatenate([micro, 1 - micro]), own_ffn, far_ffn, cotangent
    )
    far_sum, own_got, w_hidden_two = together(far_sum, own_got, w_hidden_two)
    grad_mine = own_mine.astype(F32) + own_got.astype(F32) + far_sum.astype(F32)
    grad_mine = grad_mine.astype(BF)
    grad_theirs = swap(grad_mine, "tensor", 1)
    early_totals = lax.psum(tuple(w_hidden_two), "clip")
    sides = wide // width
    in_rows = heads_in_two.shape[2] * 3

    def turned(block):
        return jnp.transpose(block.reshape(3, -1, width), (2, 0, 1)).astype(F32)

    def unfold(block):
        block = block.reshape(-1, sides, HD, width).astype(F32)
        return jnp.concatenate([block[:, k] for k in range(sides)], 2).reshape(-1, wide)

    left = []

    def backward():
        place = jnp.stack([chip, core, part_index]).astype(jnp.int32)
        (branch_two, w_gain_four, w_skip, *early, memory_kept, memory_sent, w_two_sent, query_two,
         pair_two) = two_first(
            place, after_three, grad_mine, grad_theirs, cotangent, gain_four, normed_three,
            memory_two, pooled_three, weights_two, out_two, skip, kept_two,
        )
        memory_part = shifted(plus_rounded(memory_kept, swap(memory_sent, "tensor", 1)), -1)
        w_two_far = swap(w_two_sent, "tensor", 2)
        grad_rows_two, w_two = two_second(
            branch_two, normed_three, pooled_three, weights_two, out_two, *early, query_two,
            pair_two, w_skip, kept_two,
        )
        grad_rows_two, memory_part, w_two = together(grad_rows_two, memory_part, w_two)
        got_rows_two = swap(grad_rows_two, "tensor", 1)
        memory_theirs = swap(memory_part, "tensor", 1)
        grad_two, grad_part_two, w_hidden, w_hidden_sent, w_gain_three = hidden_one_back(
            core_index, after_two, grad_rows_two, got_rows_two, memory_part,
            memory_theirs, gain_three, after_one, gain_two, w_in_one, w_out_one,
        )
        grad_part_two, w_two_far, w_hidden, w_hidden_sent = together(
            grad_part_two, w_two_far, w_hidden, w_hidden_sent
        )
        far_result_mine, far_result_theirs, result_theirs = after(
            (far_result_mine_, far_result_theirs_, result_theirs_), w_two_far
        )
        result_far = plus_rounded(far_result_mine, swap(far_result_theirs, "tensor", 1))
        result_far = swap(result_far, "tensor", 2)
        result_got = swap(result_theirs, "tensor", 1)
        total_two = ClipSum(plus_rounded(w_two, w_two_far), 2)
        w_hidden_far = swap(w_hidden_sent, "tensor", 2)
        (grad_one, branch_one, w_gain_two, early_rows, memory_kept, memory_sent, w_last_sent,
         *memory_terms) = one_first(
            core_index, grad_two, after_one, grad_part_two, swap(grad_part_two, "tensor", 1),
            gain_two, normed_one, memory_one, weights_one, out_one, kept_one,
        )
        branch_one, total_two.got, w_hidden_far, w_last_sent, result_far, result_got = together(
            branch_one, total_two.got, w_hidden_far, w_last_sent, result_far, result_got
        )
        result_half = result_mine.astype(F32) + result_got.astype(F32) + result_far.astype(F32)
        result_half = (result_half + share_of(after_three, core)).astype(BF)
        total_two.step()
        total_hidden = ClipSum(plus_rounded(w_hidden, w_hidden_far), 2)
        memory_last = shifted(plus_rounded(memory_kept, swap(memory_sent, "tensor", 1)), -1)
        w_last_far = swap(w_last_sent, "tensor", 2)
        far_result_half = swap(result_half, "tensor", 2)
        gains = jnp.concatenate([w_gain_two, w_gain_three, w_gain_four], 1).reshape(-1, width) * 0.5
        gains = jnp.pad(gains, ((1, GAIN_ROWS - 1 - gains.shape[0]), (0, 0)))
        leaving, leaving_sent, w_last = one_second(
            core_index, branch_one, normed_one, weights_one, out_one, early_rows, *memory_terms,
            gain_one, gains, kept_one,
        )
        (leaving, leaving_sent, memory_last, total_two.got, total_hidden.got, w_last, w_last_far,
         far_result_half) = together(
            leaving, leaving_sent, memory_last, total_two.got, total_hidden.got, w_last, w_last_far,
            far_result_half,
        )
        left[:] = [total_two.todo, total_hidden.todo]
        return (
            leaving, leaving_sent, memory_last, total_two.got, total_hidden.got, w_last, w_last_far,
            far_result_half, grad_one, total_two.block, total_hidden.block, result_half,
        )

    shapes = jax.eval_shape(backward)

    def absent():
        return tuple(jnp.zeros(item.shape, item.dtype) for item in shapes)

    results = lax.cond(clip_index < tokens_in.shape[0] * lax.axis_size("clip"), backward, absent)
    results, early_totals = together(results, early_totals)
    (leaving, leaving_sent, memory_last, got_two, got_hidden, w_last, w_last_far, far_result_half,
     grad_one, block_two, block_hidden, result_half) = results
    total_two = ClipSum.resumed(block_two, left[0], got_two)
    total_hidden = ClipSum.resumed(block_hidden, left[1], got_hidden)
    leaving_got = swap(leaving_sent, "tensor", 1)
    memory_theirs = swap(memory_last, "tensor", 1)
    total_last = ClipSum(plus_rounded(w_last, w_last_far))
    total_hidden.step()
    total_two.step()

    def leave(which, dtype):
        place = jnp.stack([which * 2 + core, which, core]).astype(jnp.int32)
        return exit_norm(
            place, normed_one, factor_one, grad_one, leaving, leaving_got, memory_last, memory_theirs, gain_one,
            dtype,
        )

    def move_on(beside_it, *sums):
        sums = [item for item in sums if item.todo]
        beside_it, *arrived = together(beside_it, *[item.got for item in sums])
        for item, got in zip(sums, arrived):
            item.got = got
            item.step()
        return beside_it

    far_input = move_on(leave(1 - chip, BF), total_last, total_hidden, total_two)
    far_input = swap(far_input, "tensor", 2)
    near_input, early_totals, far_result_half = move_on(
        (leave(chip, F32), early_totals, far_result_half), total_last, total_hidden, total_two
    )
    far_input = move_on(far_input, total_last, total_hidden, total_two)
    far_input = far_input.astype(F32)
    grad_input = jnp.where(
        chip == 0, jnp.stack([near_input, far_input]), jnp.stack([far_input, near_input])
    )
    result_pair = jnp.where(
        chip == 0,
        jnp.stack([result_half, far_result_half]),
        jnp.stack([far_result_half, result_half]),
    )
    other_pair = swap(result_pair, "tensor", 1)
    output = jnp.where(
        core == 0,
        jnp.concatenate([result_pair, other_pair], 1),
        jnp.concatenate([other_pair, result_pair], 1),
    ).astype(F32)
    early = [item.astype(F32) for item in early_totals]
    def all_gains():
        gains = total_last.half[-GAIN_ROWS:].astype(F32)
        gains = gains + swap(gains, "tensor", 1)
        return gains, swap(gains, "tensor", 2)

    early_gains = all_gains() if total_last.half is not None else None
    output, grad_input, early, early_gains = move_on(
        (output, grad_input, early, early_gains), total_last, total_hidden, total_two
    )
    while total_last.todo or total_hidden.todo or total_two.todo:
        output = move_on(output, total_last, total_hidden, total_two)
    near_gains, far_gains = all_gains() if early_gains is None else early_gains
    gains = (near_gains + far_gains).reshape(-1)
    totals_two = total_two.block
    grad_heads_in_two = turned(totals_two[:in_rows])
    grad_rows = unfold(totals_two[in_rows:])
    totals_hidden_one = total_hidden.block
    totals_last = total_last.block.reshape(2, -1, width)[:, : 2 * HD].reshape(-1, width)
    return (
        output[:, None],
        grad_input[:, None],
        gains[:width],
        turned(totals_last[:heads_rows]),
        totals_last[heads_rows:].astype(F32),
        gains[width : 2 * width],
        totals_hidden_one[:width].astype(F32),
        totals_hidden_one[width:].astype(F32),
        gains[2 * width : 3 * width],
        grad_heads_in_two,
        grad_rows[-skip_rows:],
        grad_rows[:-skip_rows],
        gains[3 * width : 3 * width + wide],
        *early,
    )

def solution(mesh):
    return jax.shard_map(
        per_device,
        mesh=mesh,
        in_specs=(
            P(None, "clip", None, None),
            P(),
            P(None, None, "tensor"),
            P("tensor", None),
            P(),
            P(None, "tensor"),
            P("tensor", None),
            P(),
            P(None, None, "tensor"),
            P("tensor", None),
            P("tensor", None),
            P(),
            P(None, "tensor"),
            P("tensor", None),
            P(),
            P(),
            P(None, "clip", None, None),
        ),
        out_specs=(
            P(None, "clip", None, None),
            P(None, "clip", "tensor", None),
            P(),
            P(None, None, "tensor"),
            P("tensor", None),
            P(),
            P(None, "tensor"),
            P("tensor", None),
            P(),
            P(None, None, "tensor"),
            P("tensor", None),
            P("tensor", None),
            P(),
            P(None, "tensor"),
            P("tensor", None),
        ),
        check_vma=False,
    )
```
